32 devices in a mesh: group: 2 (over y), dev: 16 (over z, x, core).
Axes of the slice: x: 2, y: 2, z: 4, core: 2. Of those that a mesh axis runs over, the one named last changes fastest.
Arguments:
- forces: float32 [3, 65536], P(None, ('group', 'dev')), may hold values from -4 to 4
- stencil_start: int32 [3, 65536], P(None, ('group', 'dev')), may hold values from 0 to 1023, as said below
- fraction: float32 [3, 65536], P(None, ('group', 'dev')), may hold values from 0 to 1
- tile_pairs: int32 [1536, 2], P(('group', 'dev')), may hold values from 0 to 15, as said below
- pair_count: int32 [32], P(('group', 'dev')), may hold values from 1 to 48, as said below
Outputs:
- velocity: float32 [3, 65536], P(None, ('group', 'dev'))
The draws below stay inside these ranges and needn't reach their ends.
Inputs may be any that keep to these rules, and one draw needn't show every extreme that they name: `stencil_start`: along the first dimension, a point of block b = p // 2048 starts in planes b * 32 to (b + 1) * 32 - 1; along the others it lies in 0 to 127 and 0 to 127. `tile_pairs`: tile numbers are local to the device's block of 2048 points. `pair_count`: the live slots are the first ones of each device's list; some device has all 48 live.
All inputs are finite; a program needn't handle non-finite values.
Results may differ from the reference program's by a relative error of at most 0.0003.
Values sent between devices are 32-bit elements; how exact they have to be, the bound alone decides.
No kernel may reach another device: no remote copies, remote signals or barrier semaphores. Data moves between devices by JAX's collectives and lax.ppermute only.
A program may use at most 128 MiB of HBM per device.

```python
import jax
import jax.numpy as jnp
from jax import lax

NX = 1024
NY = 128
NZ = 128
PD = 2048
TL = 48
PX = 32
NPTS = 65536
NTILES = 512


def draw_forces(key, part):
    subkeys = jax.random.split(jax.random.fold_in(key, 5), 1)
    base = jax.random.normal(subkeys[0], (3, NTILES, 128), jnp.float32)
    centred = base - jnp.mean(base, axis=2, keepdims=True)
    largest = jnp.max(jnp.abs(centred), axis=2, keepdims=True)
    return (4.0 * centred / largest).reshape(3, NPTS).astype(jnp.float32)


def draw_stencil_start(key, part):
    subkeys = jax.random.split(jax.random.fold_in(key, 11), 7)
    blocks = NPTS // PD
    position = jnp.arange(NPTS, dtype=jnp.int32)
    owner_block = position // PD
    tile_of = position // 128
    along_x = owner_block * PX + jax.random.randint(subkeys[0], (NPTS,), 0, PX)
    base_y = jax.random.randint(subkeys[1], (blocks,), 0, NY)[owner_block]
    tile_y = jax.random.randint(subkeys[2], (NTILES,), 0, 12)[tile_of]
    point_y = jax.random.randint(subkeys[3], (NPTS,), 0, 8)
    base_z = jax.random.randint(subkeys[4], (blocks,), 0, NZ)[owner_block]
    tile_z = jax.random.randint(subkeys[5], (NTILES,), 0, 12)[tile_of]
    point_z = jax.random.randint(subkeys[6], (NPTS,), 0, 8)
    across_y = (base_y + tile_y + point_y) % NY
    across_z = (base_z + tile_z + point_z) % NZ
    return jnp.stack([along_x, across_y, across_z]).astype(jnp.int32)


def draw_tile_pairs(key, part):
    blocks = NPTS // PD
    return jax.random.randint(jax.random.fold_in(key, 17), (blocks * TL, 2), 0, PD // 128).astype(jnp.int32)


def draw_pair_count(key, part):
    subkeys = jax.random.split(jax.random.fold_in(key, 23), 3)
    blocks = NPTS // PD
    first_draw = jax.random.randint(subkeys[0], (blocks,), 1, TL + 1)
    second_draw = jax.random.randint(subkeys[1], (blocks,), 1, TL + 1)
    counts = jnp.minimum(first_draw, second_draw)
    fullest = jax.random.randint(subkeys[2], (), 0, blocks)
    return jnp.where(jnp.arange(blocks, dtype=jnp.int32) == fullest, TL, counts).astype(jnp.int32)


def block_scale(stream_key, dims, cuts, low, high):
    loudness = 1.0
    for dim, shards_of in cuts:
        draws = jax.random.uniform(jax.random.fold_in(jax.random.fold_in(stream_key, 6), dim), (shards_of,), jnp.float32, low / len(cuts), high / len(cuts))
        loudness = loudness * jnp.repeat(jnp.exp(draws), dims[dim] // shards_of).reshape((-1,) + (1,) * (len(dims) - 1 - dim))
    return loudness


def setup_inputs(seed: int = 0) -> dict:
    keys = jax.random.split(jax.random.key(seed), 6)
    forces = draw_forces(jax.random.fold_in(keys[5], 71), 0)
    stencil_start = draw_stencil_start(jax.random.fold_in(keys[5], 71), 0)
    fraction = jnp.clip(1.0 * jax.random.uniform(keys[2], (3, NPTS), jnp.float32) ** block_scale(keys[2], (3, NPTS), ((1, 32),), -0.2, 0.2), 0.0, 1.0)
    tile_pairs = draw_tile_pairs(jax.random.fold_in(keys[5], 71), 0)
    pair_count = draw_pair_count(jax.random.fold_in(keys[5], 71), 0)
    return dict(forces=forces, stencil_start=stencil_start, fraction=fraction, tile_pairs=tile_pairs, pair_count=pair_count)


TWO_PI = 6.283185307179586
EPS_SQ = 1.0
RANGE_SQ = 16.0
NEAR_SCALE = 0.25

def spline_weights(fraction):
    square = fraction * fraction
    cube = square * fraction
    return [(1.0 - fraction) ** 3 / 6.0, (3.0 * cube - 6.0 * square + 4.0) / 6.0, (-3.0 * cube + 3.0 * square + 3.0 * fraction + 1.0) / 6.0, cube / 6.0]

def wave_numbers(index, length):
    signed_index = jnp.where(index > length // 2, index - length, index)
    return (signed_index.astype(jnp.float32) * (TWO_PI / length), index != length // 2)

def wrap_gap(gap, length):
    gap = jnp.where(gap > length // 2, gap - length, gap)
    return jnp.where(gap < -(length // 2), gap + length, gap)

def pair_terms(stencil_start, fraction, forces, pairs, count):
    tiles = stencil_start.shape[1] // 128
    slots = pairs.shape[0]
    start_tiles = stencil_start.reshape(3, tiles, 128)
    frac_tiles = fraction.reshape(3, tiles, 128)
    force_tiles = forces.reshape(3, tiles, 128)
    target = pairs[:, 0]
    source = pairs[:, 1]
    lengths = (NX, NY, NZ)
    deltas = []
    for component in range(3):
        gap = start_tiles[component][target][:, :, None] - start_tiles[component][source][:, None, :]
        if component > 0:
            gap = wrap_gap(gap, lengths[component])
        offset = frac_tiles[component][target][:, :, None] - frac_tiles[component][source][:, None, :]
        deltas.append(gap.astype(jnp.float32) + offset)
    distance = deltas[0] * deltas[0] + deltas[1] * deltas[1] + deltas[2] * deltas[2]
    softened = distance + EPS_SQ
    falloff = NEAR_SCALE * jnp.exp(-distance / RANGE_SQ) / (softened * jnp.sqrt(softened))
    diagonal = (distance + 2.0 * EPS_SQ) * falloff
    pulled = [force_tiles[component][source][:, None, :] for component in range(3)]
    along = deltas[0] * pulled[0] + deltas[1] * pulled[1] + deltas[2] * pulled[2]
    live = (jnp.arange(slots, dtype=jnp.int32) < count).astype(jnp.float32)[:, None]
    return jnp.stack([lax.optimization_barrier(jnp.sum(diagonal * pulled[component] + falloff * deltas[component] * along, axis=2)) * live for component in range(3)])

def near_block(items):
    stencil_start, fraction, forces, pairs, count = items
    tiles = stencil_start.shape[1] // 128
    terms = pair_terms(stencil_start, fraction, forces, pairs, count)
    near = jnp.zeros((3, tiles, 128), jnp.float32).at[:, pairs[:, 0]].add(terms)
    return near.reshape(3, tiles * 128)

def reference(forces, stencil_start, fraction, tile_pairs, pair_count):
    weights = spline_weights(fraction)
    grid = jnp.zeros((3, NX, NY, NZ), jnp.float32)
    cells = []
    for step_x in range(4):
        for step_y in range(4):
            for step_z in range(4):
                index_x = (stencil_start[0] + step_x) % NX
                index_y = (stencil_start[1] + step_y) % NY
                index_z = (stencil_start[2] + step_z) % NZ
                weight = weights[step_x][0] * weights[step_y][1] * weights[step_z][2]
                cells.append((index_x, index_y, index_z, weight))
                grid = grid.at[:, index_x, index_y, index_z].add(forces * weight)
    spectrum = jnp.fft.fftn(grid, axes=(1, 2, 3))
    wave_x, keep_x = wave_numbers(jnp.arange(NX, dtype=jnp.int32), NX)
    wave_y, keep_y = wave_numbers(jnp.arange(NY, dtype=jnp.int32), NY)
    wave_z, keep_z = wave_numbers(jnp.arange(NZ, dtype=jnp.int32), NZ)
    wave_x = wave_x[:, None, None]
    wave_y = wave_y[None, :, None]
    wave_z = wave_z[None, None, :]
    squared = wave_x * wave_x + wave_y * wave_y + wave_z * wave_z
    anchor = squared == 0
    keep = keep_x[:, None, None] & keep_y[None, :, None] & keep_z[None, None, :] & jnp.logical_not(anchor)
    inverse = jnp.where(keep, 1.0 / jnp.where(anchor, 1.0, squared), 0.0)
    project = (wave_x * spectrum[0] + wave_y * spectrum[1] + wave_z * spectrum[2]) * inverse
    flow = jnp.stack([(spectrum[0] - wave_x * project) * inverse, (spectrum[1] - wave_y * project) * inverse, (spectrum[2] - wave_z * project) * inverse])
    field = jnp.real(jnp.fft.ifftn(flow, axes=(1, 2, 3))).astype(jnp.float32)
    far = jnp.zeros_like(forces)
    for index_x, index_y, index_z, weight in cells:
        far = far + field[:, index_x, index_y, index_z] * weight
    blocks = NPTS // PD
    near = lax.map(near_block, (stencil_start.reshape(3, blocks, PD).transpose(1, 0, 2), fraction.reshape(3, blocks, PD).transpose(1, 0, 2), forces.reshape(3, blocks, PD).transpose(1, 0, 2), tile_pairs.reshape(blocks, TL, 2), pair_count))
    near = near.transpose(1, 0, 2).reshape(3, NPTS)
    return far + near
```

```python
import functools

import jax
import jax.numpy as jnp
import ml_dtypes
import numpy as np
from jax import lax
from jax.experimental import pallas as pl
from jax.experimental.pallas import tpu as pltpu
from jax.sharding import PartitionSpec as P

NX = 1024
NY = 128
NZ = 128

TWO_PI = 6.283185307179586
EPS_SQ = 1.0
RANGE_SQ = 16.0
NEAR_SCALE = 0.25

LANES = 128
KZ = 16
KY = 8
COLS = 4 * KY * KZ
CHUNK = 512
BF16 = jnp.bfloat16
F32 = jnp.float32


def wrap_gap(gap, length):
    gap = jnp.where(gap > length // 2, gap - length, gap)
    return jnp.where(gap < -(length // 2), gap + length, gap)


def pair_terms(stencil_start, fraction, forces, pairs, count):
    tiles = stencil_start.shape[1] // 128
    slots = pairs.shape[0]
    start_tiles = stencil_start.reshape(3, tiles, 128)
    frac_tiles = fraction.reshape(3, tiles, 128)
    force_tiles = forces.reshape(3, tiles, 128)
    target = pairs[:, 0]
    source = pairs[:, 1]
    lengths = (NX, NY, NZ)
    deltas = []
    for component in range(3):
        gap = (
            start_tiles[component][target][:, :, None] - start_tiles[component][source][:, None, :]
        )
        if component > 0:
            gap = wrap_gap(gap, lengths[component])
        offset = (
            frac_tiles[component][target][:, :, None] - frac_tiles[component][source][:, None, :]
        )
        deltas.append(gap.astype(jnp.float32) + offset)
    distance = deltas[0] * deltas[0] + deltas[1] * deltas[1] + deltas[2] * deltas[2]
    softened = distance + EPS_SQ
    falloff = NEAR_SCALE * jnp.exp(-distance / RANGE_SQ) / (softened * jnp.sqrt(softened))
    diagonal = (distance + 2.0 * EPS_SQ) * falloff
    pulled = [force_tiles[component][source][:, None, :] for component in range(3)]
    along = deltas[0] * pulled[0] + deltas[1] * pulled[1] + deltas[2] * pulled[2]
    live = (jnp.arange(slots, dtype=jnp.int32) < count).astype(jnp.float32)[:, None]
    return jnp.stack(
        [
            jnp.sum(diagonal * pulled[component] + falloff * deltas[component] * along, axis=2)
            * live
            for component in range(3)
        ]
    )


def split(value):
    high = value.astype(BF16)
    low = (value - high.astype(F32)).astype(BF16)
    return high, low


def spline_weights(fraction):
    square = fraction * fraction
    cube = square * fraction
    rest = 1.0 - fraction
    return [
        rest * rest * rest * (1.0 / 6.0),
        (3.0 * cube - 6.0 * square + 4.0) * (1.0 / 6.0),
        (-3.0 * cube + 3.0 * square + 3.0 * fraction + 1.0) * (1.0 / 6.0),
        cube * (1.0 / 6.0),
    ]


def cos_sin_turns(turns):
    part = turns - jnp.floor(turns + 0.5)
    half = part * (0.5 * TWO_PI)
    square = half * half
    sine = half * (
        1.0
        + square
        * (
            -1.0 / 6.0
            + square
            * (1.0 / 120.0 + square * (-1.0 / 5040.0 + square * (1.0 / 362880.0 + square * (-1.0 / 39916800.0))))
        )
    )
    cosine = 1.0 + square * (
        -0.5
        + square
        * (
            1.0 / 24.0
            + square
            * (-1.0 / 720.0 + square * (1.0 / 40320.0 + square * (-1.0 / 3628800.0 + square * (1.0 / 479001600.0))))
        )
    )
    return 1.0 - 2.0 * sine * sine, 2.0 * sine * cosine


def widen(table, width):
    return jnp.concatenate([table] * (width // LANES), axis=1)


def mode_rows(start, weights, modes, length):
    width = start.shape[1]
    cosine, sine = cos_sin_turns(widen(modes[0], width) * start * (1.0 / length))
    sum_cos = weights[0] + weights[1] * widen(modes[1], width)
    sum_sin = weights[1] * widen(modes[2], width)
    sum_cos = sum_cos + weights[2] * widen(modes[3], width) + weights[3] * widen(modes[5], width)
    sum_sin = sum_sin + weights[2] * widen(modes[4], width) + weights[3] * widen(modes[6], width)
    return cosine * sum_cos - sine * sum_sin, sine * sum_cos + cosine * sum_sin


def column_values(points, modes_y, modes_z):
    weights = spline_weights(points[6:9])
    rows_y = mode_rows(points[4:5], [w[1:2] for w in weights], modes_y, NY)
    rows_z = mode_rows(points[5:6], [w[2:3] for w in weights], modes_z, NZ)
    values = []
    for ty in range(2):
        for tz in range(2):
            for iy in range(KY):
                values.append(rows_y[ty][iy : iy + 1] * rows_z[tz])
    return values, [w[0:1] for w in weights]


def plane_rows(start, weights, rows):
    iota = lax.broadcasted_iota(jnp.int32, (rows, start.shape[1]), 0).astype(F32)
    away = iota - start
    result = jnp.where(away == 0.0, weights[0], 0.0)
    for stencil in range(1, 4):
        result = jnp.where(away == float(stencil), weights[stencil], result)
    return result


def chunk_of(points_ref, index):
    per_block = points_ref.shape[2] // CHUNK
    at = pl.ds(pl.multiple_of(lax.rem(index, per_block) * CHUNK, CHUNK), CHUNK)
    return points_ref[lax.div(index, per_block), :, at]


def spread_kernel(planes, rows, points_ref, modes_y_ref, modes_z_ref, out_ref, acc):
    step = pl.program_id(0)
    chunk = CHUNK
    count = points_ref.shape[0] * points_ref.shape[2] // chunk

    @pl.when(step == 0)
    def _():
        out_ref[...] = jnp.zeros_like(out_ref)

    modes_y = [modes_y_ref[i] for i in range(7)]
    modes_z = [modes_z_ref[i] for i in range(7)]

    def one(index):
        points = chunk_of(points_ref, index)
        values, weights_x = column_values(points, modes_y, modes_z)
        weight = plane_rows(points[3:4], weights_x, rows)
        stack = jnp.concatenate([weight * points[c : c + 1] for c in range(3)], axis=0)
        if 3 * rows < LANES:
            stack = jnp.concatenate([stack, jnp.zeros((LANES - 3 * rows, chunk), F32)], axis=0)
        high, low = split(stack)
        both = jnp.concatenate([high, low], axis=0)
        highs, lows = [], []
        for value in values:
            h, l = split(value)
            highs.append(h)
            lows.append(l)
        left = jnp.concatenate([jnp.concatenate(highs, axis=0), jnp.concatenate(lows, axis=0)], axis=1)
        right = jnp.concatenate([both, both], axis=1)
        return lax.dot_general(
            left, right, (((1,), (1,)), ((), ())), preferred_element_type=F32
        )

    acc[...] = jnp.zeros_like(acc)

    @pl.loop(0, count)
    def _(index):
        acc[...] += one(index)

    total = (acc[:, :LANES] + acc[:, LANES:]).T
    first = pl.multiple_of(step * planes, 8)
    for c in range(3):
        out_ref[c, pl.ds(first, rows)] += total[c * rows : (c + 1) * rows]

    @pl.when(step == pl.num_programs(0) - 1)
    def _():
        extra = out_ref.shape[1] - NX
        for c in range(3):
            out_ref[c, 0:extra] += out_ref[c, NX : NX + extra]


def spread(points, modes_y, modes_z, planes, rows, joined):
    blocks, _, count = points.shape
    extra = rows - planes
    return pl.pallas_call(
        functools.partial(spread_kernel, planes, rows),
        grid=(blocks // joined,),
        in_specs=[
            pl.BlockSpec((joined, 9, count), lambda i: (i, 0, 0)),
            pl.BlockSpec(modes_y.shape, lambda i: (0, 0, 0)),
            pl.BlockSpec(modes_z.shape, lambda i: (0, 0, 0)),
        ],
        out_specs=pl.BlockSpec((3, NX + extra, COLS), lambda i: (0, 0, 0)),
        out_shape=jax.ShapeDtypeStruct((3, NX + extra, COLS), F32),
        scratch_shapes=[
            pltpu.VMEM((COLS, 2 * LANES), F32),
        ],
        compiler_params=pltpu.CompilerParams(vmem_limit_bytes=56 * 2**20),
        name="spread",
    )(points, modes_y, modes_z)


def solve_kernel(extra, spread_ref, forward_ref, back_ref, waves_ref, scale_ref, out_ref, modes, stacked):
    half = NX // 2
    quarter = NX // 4
    lanes = COLS // 4

    def fill(value):
        high, low = split(value)
        stacked[0:half] = high
        stacked[half : 2 * half] = high
        stacked[2 * half : 3 * half] = low

    for parity in range(2):

        @pl.loop(0, 3)
        def _(c):
            first = spread_ref[c, 0:half]
            second = spread_ref[c, half:NX]
            fill(first + second if parity == 0 else first - second)
            modes[parity, c] = jnp.dot(forward_ref[parity], stacked[...], preferred_element_type=F32)

    wave_y = waves_ref[0:1]
    wave_z = waves_ref[1:2]
    mult = waves_ref[2:3]
    flat = wave_y * wave_y + wave_z * wave_z
    group = 8

    for parity in range(2):

        @pl.loop(0, quarter // group)
        def _(index):
            row = pl.multiple_of(index * group, group)
            number = lax.broadcasted_iota(jnp.int32, (group, lanes), 0) + row
            number = (2 * number + parity).astype(F32)
            wave_x = number * (TWO_PI / NX)
            squared = wave_x * wave_x + flat
            anchor = squared == 0.0
            inverse = jnp.where(anchor, 0.0, 1.0 / jnp.where(anchor, 1.0, squared))
            factor = inverse * mult * jnp.where(number == 0.0, 1.0, 2.0)
            waves = (wave_x, wave_y, wave_z)
            values = {}
            for c in range(3):
                for tx in range(2):
                    for tyz in range(4):
                        values[c, tx, tyz // 2, tyz % 2] = modes[
                            parity,
                            c,
                            pl.ds(pl.multiple_of(tx * quarter + row, group), group),
                            tyz * lanes : (tyz + 1) * lanes,
                        ]

            def flip(state, axis):
                return tuple(1 - t if i == axis else t for i, t in enumerate(state))

            states = [(a, b, d) for a in range(2) for b in range(2) for d in range(2)]
            divergence = {}
            for state in states:
                total = None
                for axis in range(3):
                    term = waves[axis] * values[(axis,) + flip(state, axis)]
                    if state[axis]:
                        term = -term
                    total = term if total is None else total + term
                divergence[state] = total * inverse
            for state in states:
                for axis in range(3):
                    term = waves[axis] * divergence[flip(state, axis)]
                    value = values[(axis,) + state]
                    value = value - term if state[axis] else value + term
                    tyz = 2 * state[1] + state[2]
                    modes[
                        parity,
                        axis,
                        pl.ds(pl.multiple_of(state[0] * quarter + row, group), group),
                        tyz * lanes : (tyz + 1) * lanes,
                    ] = value * factor

    @pl.loop(0, 3)
    def _(c):
        fill(modes[0, c])
        even = jnp.dot(back_ref[0], stacked[...], preferred_element_type=F32)
        out_ref[c, 0:half] = even
        fill(modes[1, c])
        odd = jnp.dot(back_ref[1], stacked[...], preferred_element_type=F32)
        even = out_ref[c, 0:half]
        out_ref[c, 0:half] = even + odd
        out_ref[c, half:NX] = even - odd
        out_ref[c, NX : NX + extra] = out_ref[c, 0:extra]


def solve(spectrum, waves, forward, back):
    extra = spectrum.shape[1] - NX
    full = pl.BlockSpec(memory_space=pltpu.VMEM)
    return pl.pallas_call(
        functools.partial(solve_kernel, extra),
        in_specs=[full] * 5,
        out_specs=full,
        out_shape=jax.ShapeDtypeStruct(spectrum.shape, F32),
        scratch_shapes=[
            pltpu.VMEM((2, 3, NX // 2, COLS), F32),
            pltpu.VMEM((3 * NX // 2, COLS), BF16),
        ],
        compiler_params=pltpu.CompilerParams(vmem_limit_bytes=56 * 2**20),
        name="solve",
    )(spectrum, forward, back, waves, waves)


def gather_kernel(planes, rows, points_ref, modes_y_ref, modes_z_ref, lines_ref, out_ref, plane):
    step = pl.program_id(0)
    chunk = CHUNK
    count = points_ref.shape[0] * points_ref.shape[2] // chunk
    first = pl.multiple_of(step * planes, 8)
    stack = jnp.concatenate([lines_ref[c, pl.ds(first, rows)] for c in range(3)], axis=0)
    if 3 * rows < LANES:
        stack = jnp.concatenate([stack, jnp.zeros((LANES - 3 * rows, COLS), F32)], axis=0)
    high, low = split(stack)
    plane[0:LANES] = high
    plane[LANES:] = low
    modes_y = [modes_y_ref[i] for i in range(7)]
    modes_z = [modes_z_ref[i] for i in range(7)]

    @pl.loop(0, count)
    def _(index):
        at = pl.ds(pl.multiple_of(index * chunk, chunk), chunk)
        points = chunk_of(points_ref, index)
        values, weights_x = column_values(points, modes_y, modes_z)
        highs, lows = [], []
        for value in values:
            h, l = split(value)
            highs.append(h)
            lows.append(l)
        result = jnp.dot(plane[...], jnp.concatenate(highs, axis=0), preferred_element_type=F32)
        small = jnp.dot(plane[0:LANES], jnp.concatenate(lows, axis=0), preferred_element_type=F32)
        result = result[:LANES] + result[LANES:] + small
        weight = plane_rows(points[3:4], weights_x, rows)
        out_ref[:, at] = jnp.concatenate(
            [
                jnp.sum(weight * result[c * rows : (c + 1) * rows], axis=0, keepdims=True)
                for c in range(3)
            ],
            axis=0,
        )


def gather(points, modes_y, modes_z, lines, planes, rows, joined):
    blocks, _, count = points.shape
    return pl.pallas_call(
        functools.partial(gather_kernel, planes, rows),
        grid=(blocks // joined,),
        in_specs=[
            pl.BlockSpec((joined, 9, count), lambda i: (i, 0, 0)),
            pl.BlockSpec(modes_y.shape, lambda i: (0, 0, 0)),
            pl.BlockSpec(modes_z.shape, lambda i: (0, 0, 0)),
            pl.BlockSpec(lines.shape, lambda i: (0, 0, 0)),
        ],
        out_specs=pl.BlockSpec((3, joined * count), lambda i: (0, i)),
        out_shape=jax.ShapeDtypeStruct((3, blocks * count), F32),
        scratch_shapes=[pltpu.VMEM((2 * LANES, COLS), BF16)],
        compiler_params=pltpu.CompilerParams(vmem_limit_bytes=56 * 2**20),
        name="interpolate",
    )(points, modes_y, modes_z, lines)


def line_tables():
    half = NX // 2
    place = np.arange(half)
    forward, back = [], []
    for parity in range(2):
        number = 2 * np.arange(NX // 4) + parity
        angle = (number[:, None] * place[None, :] % NX) * (2.0 * np.pi / NX)
        table = np.concatenate([np.cos(angle), np.sin(angle)], axis=0)
        for tables, value in ((forward, table), (back, table.T)):
            high = value.astype(ml_dtypes.bfloat16)
            low = (value - high.astype(np.float64)).astype(ml_dtypes.bfloat16)
            tables.append(np.concatenate([high, low, high], axis=1))
    return np.stack(forward), np.stack(back)


def mode_table(numbers, length):
    angle = numbers * (TWO_PI / length)
    rows = [numbers]
    for stencil in range(1, 4):
        rows += [jnp.cos(stencil * angle), jnp.sin(stencil * angle)]
    return jnp.broadcast_to(jnp.stack(rows)[:, :, None], (7, numbers.shape[0], LANES))


def far_tables(device, devices):
    quads = (NY // 2) * (NZ // 2) // devices
    own_y = quads // KZ
    parts_z = NZ // 2 // KZ
    first_y = (device // parts_z) * own_y
    first_z = (device % parts_z) * KZ
    local_y = jnp.arange(KY, dtype=jnp.int32)
    number_y = (first_y + local_y).astype(F32)
    number_z = (first_z + jnp.arange(KZ, dtype=jnp.int32)).astype(F32)
    modes_y = mode_table(number_y, NY)
    modes_z = mode_table(number_z, NZ)
    mult_y = jnp.where(local_y < own_y, jnp.where(number_y == 0, 1.0, 2.0), 0.0)
    mult_z = jnp.where(number_z == 0, 1.0, 2.0) / float(NX * NY * NZ)
    waves = jnp.stack(
        [
            jnp.repeat(number_y * (TWO_PI / NY), KZ),
            jnp.tile(number_z * (TWO_PI / NZ), KY),
            (mult_y[:, None] * mult_z[None, :]).reshape(-1),
        ]
    )
    waves = jnp.concatenate([waves, jnp.zeros((5, KY * KZ), F32)])
    return modes_y, modes_z, waves


def per_device(forces, stencil_start, fraction, tile_pairs, pair_count):
    groups = lax.axis_size("group")
    members = lax.axis_size("dev")
    devices = groups * members
    planes = NX // devices
    points = forces.shape[1]
    tiles = points // 128
    device = lax.axis_index("group") * members + lax.axis_index("dev")
    joined = max(1, 8 // planes)
    first_plane = (device // joined) * (joined * planes)
    start_x = (stencil_start[0:1] - first_plane).astype(F32)
    packed = jnp.concatenate(
        [forces, start_x, stencil_start[1:].astype(F32), fraction], axis=0
    )
    gathered = lax.all_gather(packed, ("group", "dev"))
    planes = planes * joined
    rows = (planes + 3 + 7) // 8 * 8
    modes_y, modes_z, waves = far_tables(device, devices)
    forward, back = line_tables()
    spectrum = spread(gathered, modes_y, modes_z, planes, rows, joined)
    lines = solve(spectrum, waves, jnp.asarray(forward), jnp.asarray(back))
    partial = gather(gathered, modes_y, modes_z, lines, planes, rows, joined)
    far = lax.psum_scatter(partial, ("group", "dev"), scatter_dimension=1, tiled=True)
    terms = pair_terms(stencil_start, fraction, forces, tile_pairs, pair_count[0])
    onehot = (tile_pairs[:, 0][:, None] == jnp.arange(tiles, dtype=jnp.int32)[None, :]).astype(
        jnp.float32
    )
    near = jnp.einsum("st,csp->ctp", onehot, terms, precision=lax.Precision.HIGHEST).reshape(
        3, points
    )
    return far + near


def solution(mesh):
    in_specs = (
        P(None, ("group", "dev")),
        P(None, ("group", "dev")),
        P(None, ("group", "dev")),
        P(("group", "dev"), None),
        P(("group", "dev")),
    )
    out_specs = P(None, ("group", "dev"))
    return jax.shard_map(
        per_device, mesh=mesh, in_specs=in_specs, out_specs=out_specs, check_vma=False
    )
```

```python
import functools

import jax
import jax.numpy as jnp
import ml_dtypes
import numpy as np
from jax import lax
from jax.experimental import pallas as pl
from jax.experimental.pallas import tpu as pltpu
from jax.sharding import PartitionSpec as P

NX = 1024
NY = 128
NZ = 128

TWO_PI = 6.283185307179586
EPS_SQ = 1.0
RANGE_SQ = 16.0
NEAR_SCALE = 0.25

LANES = 128
KZ = 16
BF16 = jnp.bfloat16
F32 = jnp.float32


def wrap_gap(gap, length):
    gap = jnp.where(gap > length // 2, gap - length, gap)
    return jnp.where(gap < -(length // 2), gap + length, gap)


def pair_terms(stencil_start, fraction, forces, pairs, count):
    tiles = stencil_start.shape[1] // 128
    slots = pairs.shape[0]
    start_tiles = stencil_start.reshape(3, tiles, 128)
    frac_tiles = fraction.reshape(3, tiles, 128)
    force_tiles = forces.reshape(3, tiles, 128)
    target = pairs[:, 0]
    source = pairs[:, 1]
    lengths = (NX, NY, NZ)
    deltas = []
    for component in range(3):
        gap = (
            start_tiles[component][target][:, :, None] - start_tiles[component][source][:, None, :]
        )
        if component > 0:
            gap = wrap_gap(gap, lengths[component])
        offset = (
            frac_tiles[component][target][:, :, None] - frac_tiles[component][source][:, None, :]
        )
        deltas.append(gap.astype(jnp.float32) + offset)
    distance = deltas[0] * deltas[0] + deltas[1] * deltas[1] + deltas[2] * deltas[2]
    softened = distance + EPS_SQ
    falloff = NEAR_SCALE * jnp.exp(-distance / RANGE_SQ) / (softened * jnp.sqrt(softened))
    diagonal = (distance + 2.0 * EPS_SQ) * falloff
    pulled = [force_tiles[component][source][:, None, :] for component in range(3)]
    along = deltas[0] * pulled[0] + deltas[1] * pulled[1] + deltas[2] * pulled[2]
    live = (jnp.arange(slots, dtype=jnp.int32) < count).astype(jnp.float32)[:, None]
    return jnp.stack(
        [
            jnp.sum(diagonal * pulled[component] + falloff * deltas[component] * along, axis=2)
            * live
            for component in range(3)
        ]
    )


def split(value):
    high = value.astype(BF16)
    low = (value - high.astype(F32)).astype(BF16)
    return high, low


def spline_weights(fraction):
    square = fraction * fraction
    cube = square * fraction
    rest = 1.0 - fraction
    return [
        rest * rest * rest * (1.0 / 6.0),
        (3.0 * cube - 6.0 * square + 4.0) * (1.0 / 6.0),
        (-3.0 * cube + 3.0 * square + 3.0 * fraction + 1.0) * (1.0 / 6.0),
        cube * (1.0 / 6.0),
    ]


def cos_sin_turns(turns):
    part = turns - jnp.floor(turns + 0.5)
    half = part * (0.5 * TWO_PI)
    square = half * half
    sine = half * (
        1.0
        + square
        * (
            -1.0 / 6.0
            + square
            * (1.0 / 120.0 + square * (-1.0 / 5040.0 + square * (1.0 / 362880.0 + square * (-1.0 / 39916800.0))))
        )
    )
    cosine = 1.0 + square * (
        -0.5
        + square
        * (
            1.0 / 24.0
            + square
            * (-1.0 / 720.0 + square * (1.0 / 40320.0 + square * (-1.0 / 3628800.0 + square * (1.0 / 479001600.0))))
        )
    )
    return 1.0 - 2.0 * sine * sine, 2.0 * sine * cosine


def widen(table, width):
    return jnp.concatenate([table] * (width // LANES), axis=1)


def mode_rows(start, weights, modes, length):
    width = start.shape[1]
    cosine, sine = cos_sin_turns(widen(modes[0], width) * start * (1.0 / length))
    sum_cos = weights[0] + weights[1] * widen(modes[1], width)
    sum_sin = weights[1] * widen(modes[2], width)
    sum_cos = sum_cos + weights[2] * widen(modes[3], width) + weights[3] * widen(modes[5], width)
    sum_sin = sum_sin + weights[2] * widen(modes[4], width) + weights[3] * widen(modes[6], width)
    return cosine * sum_cos - sine * sum_sin, sine * sum_cos + cosine * sum_sin


def column_values(main, last, modes_y, modes_z):
    weights = spline_weights(main[6:8])
    weights_z = spline_weights(last)
    rows_y = mode_rows(main[4:5], [w[1:2] for w in weights], modes_y, NY)
    rows_z = mode_rows(main[5:6], weights_z, modes_z, NZ)
    values = []
    for ty in range(2):
        for tz in range(2):
            for iy in range(rows_y[0].shape[0]):
                values.append(rows_y[ty][iy : iy + 1] * rows_z[tz])
    return values, [w[0:1] for w in weights]


def plane_rows(start, weights, rows):
    iota = lax.broadcasted_iota(jnp.int32, (rows, start.shape[1]), 0).astype(F32)
    away = iota - start
    result = jnp.where(away == 0.0, weights[0], 0.0)
    for stencil in range(1, 4):
        result = jnp.where(away == float(stencil), weights[stencil], result)
    return result


def first_plane(block, planes):
    joined = max(1, 8 // planes)
    return lax.div(block, joined) * (joined * planes)


def spread_kernel(rows, main_ref, last_ref, modes_y_ref, modes_z_ref, out_ref):
    main, last = main_ref[0], last_ref[0]
    count = main.shape[1]
    modes_y = [modes_y_ref[i] for i in range(7)]
    modes_z = [modes_z_ref[i] for i in range(7)]
    values, weights_x = column_values(main, last, modes_y, modes_z)
    weight = plane_rows(main[3:4], weights_x, rows)
    stack = jnp.concatenate([weight * main[c : c + 1] for c in range(3)], axis=0)
    if 3 * rows < LANES:
        stack = jnp.concatenate([stack, jnp.zeros((LANES - 3 * rows, count), F32)], axis=0)
    both = jnp.concatenate(split(stack), axis=0)
    parts = [split(value) for value in values]
    left = jnp.concatenate(
        [jnp.concatenate([p[i] for p in parts], axis=0) for i in range(2)], axis=1
    )
    right = jnp.concatenate([both, both], axis=1)
    acc = lax.dot_general(left, right, (((1,), (1,)), ((), ())), preferred_element_type=F32)
    total = (acc[:, :LANES] + acc[:, LANES:]).T
    out_ref[0] = total[: 3 * rows]


def spread(points, modes_y, modes_z, rows):
    main, last = points
    blocks, _, count = main.shape
    cols = 4 * modes_y.shape[1] * KZ
    return pl.pallas_call(
        functools.partial(spread_kernel, rows),
        grid=(blocks,),
        in_specs=[
            pl.BlockSpec((1, 8, count), lambda i: (i, 0, 0)),
            pl.BlockSpec((1, 1, count), lambda i: (i, 0, 0)),
            pl.BlockSpec(modes_y.shape, lambda i: (0, 0, 0)),
            pl.BlockSpec(modes_z.shape, lambda i: (0, 0, 0)),
        ],
        out_specs=pl.BlockSpec((1, 3 * rows, cols), lambda i: (i, 0, 0)),
        out_shape=jax.ShapeDtypeStruct((blocks, 3 * rows, cols), F32),
        compiler_params=pltpu.CompilerParams(vmem_limit_bytes=40 * 2**20),
        cost_estimate=pl.CostEstimate(
            flops=blocks * count * cols * LANES * 14,
            bytes_accessed=blocks * (9 * count + 3 * rows * cols) * 4,
            transcendentals=0,
        ),
        name="spread",
    )(main, last, modes_y, modes_z)


def solve_kernel(planes, rows, parts, ids_ref, *refs):
    piece_refs = refs[:parts]
    forward_ref, back_ref, waves_ref, out_ref, modes, stacked = refs[parts:]
    extra = 8
    out_ref[...] = jnp.zeros_like(out_ref)
    before = 0
    for piece_ref in piece_refs:

        @pl.loop(0, piece_ref.shape[0])
        def _(index):
            first = pl.multiple_of(first_plane(ids_ref[before + index], planes), 8)
            for c in range(3):
                out_ref[c, pl.ds(first, rows)] += piece_ref[index, c * rows : (c + 1) * rows]

        before += piece_ref.shape[0]
    for c in range(3):
        out_ref[c, 0:extra] += out_ref[c, NX : NX + extra]
    half = NX // 2
    quarter = NX // 4
    lanes = waves_ref.shape[1]

    def fill(value):
        high, low = split(value)
        stacked[0:half] = high
        stacked[half : 2 * half] = high
        stacked[2 * half : 3 * half] = low

    for parity in range(2):

        @pl.loop(0, 3)
        def _(c):
            first = out_ref[c, 0:half]
            second = out_ref[c, half:NX]
            fill(first + second if parity == 0 else first - second)
            modes[parity, c] = jnp.dot(forward_ref[parity], stacked[...], preferred_element_type=F32)

    wave_y = waves_ref[0:1]
    wave_z = waves_ref[1:2]
    mult = waves_ref[2:3]
    flat = wave_y * wave_y + wave_z * wave_z
    group = 8

    for parity in range(2):

        @pl.loop(0, quarter // group)
        def _(index):
            row = pl.multiple_of(index * group, group)
            number = lax.broadcasted_iota(jnp.int32, (group, lanes), 0) + row
            number = (2 * number + parity).astype(F32)
            wave_x = number * (TWO_PI / NX)
            squared = wave_x * wave_x + flat
            anchor = squared == 0.0
            inverse = jnp.where(anchor, 0.0, 1.0 / jnp.where(anchor, 1.0, squared))
            factor = inverse * mult * jnp.where(number == 0.0, 1.0, 2.0)
            waves = (wave_x, wave_y, wave_z)
            values = {}
            for c in range(3):
                for tx in range(2):
                    for tyz in range(4):
                        values[c, tx, tyz // 2, tyz % 2] = modes[
                            parity,
                            c,
                            pl.ds(pl.multiple_of(tx * quarter + row, group), group),
                            tyz * lanes : (tyz + 1) * lanes,
                        ]

            def flip(state, axis):
                return tuple(1 - t if i == axis else t for i, t in enumerate(state))

            states = [(a, b, d) for a in range(2) for b in range(2) for d in range(2)]
            divergence = {}
            for state in states:
                total = None
                for axis in range(3):
                    term = waves[axis] * values[(axis,) + flip(state, axis)]
                    if state[axis]:
                        term = -term
                    total = term if total is None else total + term
                divergence[state] = total * inverse
            for state in states:
                for axis in range(3):
                    term = waves[axis] * divergence[flip(state, axis)]
                    value = values[(axis,) + state]
                    value = value - term if state[axis] else value + term
                    tyz = 2 * state[1] + state[2]
                    modes[
                        parity,
                        axis,
                        pl.ds(pl.multiple_of(state[0] * quarter + row, group), group),
                        tyz * lanes : (tyz + 1) * lanes,
                    ] = value * factor

    @pl.loop(0, 3)
    def _(c):
        fill(modes[0, c])
        even = jnp.dot(back_ref[0], stacked[...], preferred_element_type=F32)
        out_ref[c, 0:half] = even
        fill(modes[1, c])
        odd = jnp.dot(back_ref[1], stacked[...], preferred_element_type=F32)
        even = out_ref[c, 0:half]
        out_ref[c, 0:half] = even + odd
        out_ref[c, half:NX] = even - odd
        out_ref[c, NX : NX + extra] = out_ref[c, 0:extra]


def solve(pieces, ids, waves, forward, back, planes, rows):
    full = pl.BlockSpec(memory_space=pltpu.VMEM)
    cols = pieces[0].shape[2]
    return pl.pallas_call(
        functools.partial(solve_kernel, planes, rows, len(pieces)),
        in_specs=[pl.BlockSpec(memory_space=pltpu.SMEM)] + [full] * (len(pieces) + 3),
        out_specs=full,
        out_shape=jax.ShapeDtypeStruct((3, NX + 8, cols), F32),
        scratch_shapes=[
            pltpu.VMEM((2, 3, NX // 2, cols), F32),
            pltpu.VMEM((3 * NX // 2, cols), BF16),
        ],
        compiler_params=pltpu.CompilerParams(vmem_limit_bytes=56 * 2**20),
        cost_estimate=pl.CostEstimate(
            flops=36 * NX // 2 * NX // 2 * cols,
            bytes_accessed=6 * NX * cols * 4,
            transcendentals=0,
        ),
        name="solve",
    )(ids, *pieces, forward, back, waves)


def gather_kernel(planes, rows, parts, ids_ref, *refs):
    mains, lasts = refs[:parts], refs[parts : 2 * parts]
    modes_y_ref, modes_z_ref, lines_ref, out_ref, plane = refs[2 * parts :]
    step = pl.program_id(0)
    each = pl.num_programs(0) // parts
    first = pl.multiple_of(first_plane(ids_ref[step], planes), 8)
    stack = jnp.concatenate([lines_ref[c, pl.ds(first, rows)] for c in range(3)], axis=0)
    if 3 * rows < LANES:
        stack = jnp.concatenate([stack, jnp.zeros((LANES - 3 * rows, lines_ref.shape[2]), F32)], axis=0)
    high, low = split(stack)
    plane[0:LANES] = high
    plane[LANES:] = low
    modes_y = [modes_y_ref[i] for i in range(7)]
    modes_z = [modes_z_ref[i] for i in range(7)]
    main, last = mains[0][0], lasts[0][0]
    for part in range(1, parts):
        here = step >= part * each
        main = jnp.where(here, mains[part][0], main)
        last = jnp.where(here, lasts[part][0], last)
    count = main.shape[1]
    chunk = count // 4
    for index in range(4):
        at = slice(index * chunk, (index + 1) * chunk)
        values, weights_x = column_values(main[:, at], last[:, at], modes_y, modes_z)
        pairs = [split(value) for value in values]
        highs = jnp.concatenate([p[0] for p in pairs], axis=0)
        lows = jnp.concatenate([p[1] for p in pairs], axis=0)
        result = jnp.dot(plane[...], highs, preferred_element_type=F32)
        small = jnp.dot(plane[0:LANES], lows, preferred_element_type=F32)
        result = result[:LANES] + result[LANES:] + small
        weight = plane_rows(main[3:4, at], weights_x, rows)
        out_ref[0, :, at] = jnp.concatenate(
            [
                jnp.sum(weight * result[c * rows : (c + 1) * rows], axis=0, keepdims=True)
                for c in range(3)
            ],
            axis=0,
        )


def gather(points, ids, modes_y, modes_z, lines, planes, rows):
    parts = len(points)
    mains = [p[0] for p in points]
    lasts = [p[1] for p in points]
    each, _, count = mains[0].shape
    blocks = parts * each
    cols = lines.shape[2]

    def at(part):
        return lambda i, ids: (jnp.clip(i - part * each, 0, each - 1), 0, 0)

    return pl.pallas_call(
        functools.partial(gather_kernel, planes, rows, parts),
        grid_spec=pltpu.PrefetchScalarGridSpec(
            num_scalar_prefetch=1,
            grid=(blocks,),
            in_specs=[pl.BlockSpec((1, 8, count), at(part)) for part in range(parts)]
            + [pl.BlockSpec((1, 1, count), at(part)) for part in range(parts)]
            + [
                pl.BlockSpec(modes_y.shape, lambda i, ids: (0, 0, 0)),
                pl.BlockSpec(modes_z.shape, lambda i, ids: (0, 0, 0)),
                pl.BlockSpec(lines.shape, lambda i, ids: (0, 0, 0)),
            ],
            out_specs=pl.BlockSpec((1, 3, count), lambda i, ids: (ids[i], 0, 0)),
            scratch_shapes=[pltpu.VMEM((2 * LANES, cols), BF16)],
        ),
        out_shape=jax.ShapeDtypeStruct((blocks, 3, count), F32),
        compiler_params=pltpu.CompilerParams(vmem_limit_bytes=48 * 2**20),
        cost_estimate=pl.CostEstimate(
            flops=blocks * count * cols * LANES * 14,
            bytes_accessed=blocks * 12 * count * 4,
            transcendentals=0,
        ),
        name="interpolate",
    )(ids, *mains, *lasts, modes_y, modes_z, lines)


def line_tables():
    half = NX // 2
    place = np.arange(half)
    forward, back = [], []
    for parity in range(2):
        number = 2 * np.arange(NX // 4) + parity
        angle = (number[:, None] * place[None, :] % NX) * (2.0 * np.pi / NX)
        table = np.concatenate([np.cos(angle), np.sin(angle)], axis=0)
        for tables, value in ((forward, table), (back, table.T)):
            high = value.astype(ml_dtypes.bfloat16)
            low = (value - high.astype(np.float64)).astype(ml_dtypes.bfloat16)
            tables.append(np.concatenate([high, low, high], axis=1))
    return np.stack(forward), np.stack(back)


def mode_table(numbers, length):
    angle = numbers * (TWO_PI / length)
    rows = [numbers]
    for stencil in range(1, 4):
        rows += [jnp.cos(stencil * angle), jnp.sin(stencil * angle)]
    return jnp.broadcast_to(jnp.stack(rows)[:, :, None], (7, numbers.shape[0], LANES))


def far_tables(device, devices):
    quads = (NY // 2) * (NZ // 2) // devices
    own_y = quads // KZ
    parts_z = NZ // 2 // KZ
    first_y = (device // parts_z) * own_y
    first_z = (device % parts_z) * KZ
    local_y = jnp.arange(own_y, dtype=jnp.int32)
    number_y = (first_y + local_y).astype(F32)
    number_z = (first_z + jnp.arange(KZ, dtype=jnp.int32)).astype(F32)
    modes_y = mode_table(number_y, NY)
    modes_z = mode_table(number_z, NZ)
    mult_y = jnp.where(number_y == 0, 1.0, 2.0)
    mult_z = jnp.where(number_z == 0, 1.0, 2.0) / float(NX * NY * NZ)
    waves = jnp.stack(
        [
            jnp.repeat(number_y * (TWO_PI / NY), KZ),
            jnp.tile(number_z * (TWO_PI / NZ), own_y),
            (mult_y[:, None] * mult_z[None, :]).reshape(-1),
        ]
    )
    waves = jnp.concatenate([waves, jnp.zeros((5, own_y * KZ), F32)])
    return modes_y, modes_z, waves


def per_device(forces, stencil_start, fraction, tile_pairs, pair_count):
    groups = lax.axis_size("group")
    members = lax.axis_size("dev")
    devices = groups * members
    planes = NX // devices
    points = forces.shape[1]
    tiles = points // 128
    device = lax.axis_index("group") * members + lax.axis_index("dev")
    rows = max(8, planes) + 8
    start_x = (stencil_start[0:1] - first_plane(device, planes)).astype(F32)
    main = jnp.concatenate(
        [forces, start_x, stencil_start[1:].astype(F32), fraction[0:2]], axis=0
    )
    own = (main[None], fraction[2:3][None])

    def from_flipped(values, mask):
        pairs = [(i, i ^ mask) for i in range(devices)]
        return jax.tree.map(lambda v: lax.ppermute(v, ("group", "dev"), pairs), values)

    def join(*values):
        return jax.tree.map(lambda *v: jnp.concatenate(v, axis=0), *values)

    near_blocks = join(own, *[from_flipped(own, mask) for mask in (4, 8, 12)])
    masks = [0, 4, 8, 12]
    last_bit = devices.bit_length() - 2
    for bit in [1] + list(range(4, last_bit)):
        near_blocks = join(near_blocks, from_flipped(near_blocks, 1 << bit))
        masks = masks + [m ^ 1 << bit for m in masks]
    core = from_flipped(near_blocks, 1)
    other = from_flipped(near_blocks, 1 << last_bit)
    blocks = [near_blocks, core, other, from_flipped(other, 1)]
    masks = np.array(
        [m ^ flip for flip in (0, 1, 1 << last_bit, 1 << last_bit ^ 1) for m in masks], np.int32
    )
    ids = device ^ jnp.asarray(masks)
    modes_y, modes_z, waves = far_tables(device, devices)
    forward, back = line_tables()
    pieces = [spread(points_of, modes_y, modes_z, rows) for points_of in blocks]
    lines = solve(pieces, ids, waves, jnp.asarray(forward), jnp.asarray(back), planes, rows)
    partial = gather(blocks, ids, modes_y, modes_z, lines, planes, rows)
    shares = lax.all_to_all(partial, ("group", "dev"), 0, 0, tiled=True)
    far = jnp.sum(shares, axis=0)
    terms = pair_terms(stencil_start, fraction, forces, tile_pairs, pair_count[0])
    onehot = (tile_pairs[:, 0][:, None] == jnp.arange(tiles, dtype=jnp.int32)[None, :]).astype(
        jnp.float32
    )
    near = jnp.einsum("st,csp->ctp", onehot, terms, precision=lax.Precision.HIGHEST).reshape(
        3, points
    )
    return far + near


def solution(mesh):
    in_specs = (
        P(None, ("group", "dev")),
        P(None, ("group", "dev")),
        P(None, ("group", "dev")),
        P(("group", "dev"), None),
        P(("group", "dev")),
    )
    out_specs = P(None, ("group", "dev"))
    return jax.shard_map(
        per_device, mesh=mesh, in_specs=in_specs, out_specs=out_specs, check_vma=False
    )
```

```python
import functools

import jax
import jax.numpy as jnp
import ml_dtypes
import numpy as np
from jax import lax
from jax.experimental import pallas as pl
from jax.experimental.pallas import tpu as pltpu
from jax.sharding import PartitionSpec as P

NX = 1024
NY = 128
NZ = 128

TWO_PI = 6.283185307179586
EPS_SQ = 1.0
RANGE_SQ = 16.0
NEAR_SCALE = 0.25

LANES = 128
SPREAD_LIMIT = 24 * 2**20
SOLVE_LIMIT = 36 * 2**20
GATHER_LIMIT = 20 * 2**20
KZ = 16
BF16 = jnp.bfloat16
F32 = jnp.float32


def wrapped(gap, length):
    gap = jnp.where(gap > length / 2, gap - length, gap)
    return jnp.where(gap < -length / 2, gap + length, gap)


def near_kernel(pairs_ref, count_ref, forces_ref, start_ref, fraction_ref, out_ref, columns):
    tiles = out_ref.shape[1] // LANES
    out_ref[...] = jnp.zeros_like(out_ref)
    for tile in range(tiles):
        at = slice(tile * LANES, (tile + 1) * LANES)
        nine = jnp.concatenate(
            [
                start_ref[:, at].astype(F32),
                fraction_ref[:, at],
                forces_ref[:, at],
                jnp.zeros((7, LANES), F32),
            ],
            axis=0,
        )
        columns[at] = nine.T

    @pl.loop(0, count_ref[0])
    def _(slot):
        target = pl.ds(pl.multiple_of(pairs_ref[2 * slot] * LANES, LANES), LANES)
        base = pl.multiple_of(pairs_ref[2 * slot + 1] * LANES, LANES)
        start = start_ref[:, target].astype(F32)
        fraction = fraction_ref[:, target]
        sums = [jnp.zeros((8, LANES), F32) for _ in range(3)]
        for row in range(0, LANES, 8):
            source = columns[pl.ds(base + row, 8)]
            gaps = []
            for axis, length in enumerate((None, NY, NZ)):
                gap = start[axis : axis + 1] - source[:, axis : axis + 1]
                if length is not None:
                    gap = wrapped(gap, float(length))
                gaps.append(gap + (fraction[axis : axis + 1] - source[:, 3 + axis : 4 + axis]))
            pulled = [source[:, 6 + axis : 7 + axis] for axis in range(3)]
            distance = gaps[0] * gaps[0] + gaps[1] * gaps[1] + gaps[2] * gaps[2]
            inverse = lax.rsqrt(distance + EPS_SQ)
            fall = NEAR_SCALE * jnp.exp(distance * (-1.0 / RANGE_SQ)) * (inverse * inverse * inverse)
            diagonal = (distance + 2.0 * EPS_SQ) * fall
            along = fall * (gaps[0] * pulled[0] + gaps[1] * pulled[1] + gaps[2] * pulled[2])
            sums = [sums[i] + (diagonal * pulled[i] + gaps[i] * along) for i in range(3)]
        out_ref[:, target] += jnp.concatenate(
            [jnp.sum(value, axis=0, keepdims=True) for value in sums], axis=0
        )


def near_field(forces, stencil_start, fraction, tile_pairs, pair_count):
    smem = pl.BlockSpec(memory_space=pltpu.SMEM)
    vmem = pl.BlockSpec(memory_space=pltpu.VMEM)
    points = forces.shape[1]
    slots = tile_pairs.shape[0]
    return pl.pallas_call(
        near_kernel,
        in_specs=[smem, smem, vmem, vmem, vmem],
        out_specs=vmem,
        out_shape=jax.ShapeDtypeStruct((3, points), F32),
        scratch_shapes=[pltpu.VMEM((points, 16), F32)],
        compiler_params=pltpu.CompilerParams(vmem_limit_bytes=8 * 2**20),
        cost_estimate=pl.CostEstimate(
            flops=slots * LANES * LANES * 6000, bytes_accessed=points * 48, transcendentals=0
        ),
        name="near",
    )(tile_pairs.reshape(-1), pair_count, forces, stencil_start, fraction)


def pack_kernel(first_ref, forces_ref, start_ref, fraction_ref, out_ref):
    points = forces_ref.shape[1]
    piece = points // 8
    start = start_ref[...]
    out_ref[0, 0:3, 0:points] = forces_ref[...]
    out_ref[0, 3:4, 0:points] = (start[0:1] - first_ref[0]).astype(F32)
    out_ref[0, 4:6, 0:points] = start[1:3].astype(F32)
    out_ref[0, 6:8, 0:points] = fraction_ref[0:2]
    for row in range(8):
        out_ref[0, row : row + 1, points:] = fraction_ref[2:3, row * piece : (row + 1) * piece]


def pack(first, forces, stencil_start, fraction):
    vmem = pl.BlockSpec(memory_space=pltpu.VMEM)
    points = forces.shape[1]
    return pl.pallas_call(
        pack_kernel,
        in_specs=[pl.BlockSpec(memory_space=pltpu.SMEM), vmem, vmem, vmem],
        out_specs=vmem,
        out_shape=jax.ShapeDtypeStruct((1, 8, points + points // 8), F32),
        name="pack",
    )(first, forces, stencil_start, fraction)


def unpack(values):
    points = values.shape[1] // 9 * 8
    pieces = [values[row : row + 1, points:] for row in range(8)]
    return values[:, :points], jnp.concatenate(pieces, axis=1)


def split(value):
    high = value.astype(BF16)
    low = (value - high.astype(F32)).astype(BF16)
    return high, low


def spline_weights(fraction):
    square = fraction * fraction
    cube = square * fraction
    rest = 1.0 - fraction
    return [
        rest * rest * rest * (1.0 / 6.0),
        (3.0 * cube - 6.0 * square + 4.0) * (1.0 / 6.0),
        (-3.0 * cube + 3.0 * square + 3.0 * fraction + 1.0) * (1.0 / 6.0),
        cube * (1.0 / 6.0),
    ]


def cos_sin_turns(turns):
    part = turns - jnp.floor(turns + 0.5)
    half = part * (0.5 * TWO_PI)
    square = half * half
    sine = half * (
        1.0
        + square
        * (
            -1.0 / 6.0
            + square
            * (1.0 / 120.0 + square * (-1.0 / 5040.0 + square * (1.0 / 362880.0 + square * (-1.0 / 39916800.0))))
        )
    )
    cosine = 1.0 + square * (
        -0.5
        + square
        * (
            1.0 / 24.0
            + square
            * (-1.0 / 720.0 + square * (1.0 / 40320.0 + square * (-1.0 / 3628800.0 + square * (1.0 / 479001600.0))))
        )
    )
    return 1.0 - 2.0 * sine * sine, 2.0 * sine * cosine


def widen(table, width):
    return jnp.concatenate([table] * (width // LANES), axis=1)


def mode_rows(start, weights, modes, length):
    width = start.shape[1]
    cosine, sine = cos_sin_turns(widen(modes[0], width) * start * (1.0 / length))
    sum_cos = weights[0] + weights[1] * widen(modes[1], width)
    sum_sin = weights[1] * widen(modes[2], width)
    sum_cos = sum_cos + weights[2] * widen(modes[3], width) + weights[3] * widen(modes[5], width)
    sum_sin = sum_sin + weights[2] * widen(modes[4], width) + weights[3] * widen(modes[6], width)
    return cosine * sum_cos - sine * sum_sin, sine * sum_cos + cosine * sum_sin


def column_values(main, last, modes_y, modes_z):
    weights = spline_weights(main[6:8])
    weights_z = spline_weights(last)
    rows_y = mode_rows(main[4:5], [w[1:2] for w in weights], modes_y, NY)
    rows_z = mode_rows(main[5:6], weights_z, modes_z, NZ)
    values = []
    for ty in range(2):
        for tz in range(2):
            for iy in range(rows_y[0].shape[0]):
                values.append(rows_y[ty][iy : iy + 1] * rows_z[tz])
    return values, [w[0:1] for w in weights]


def plane_rows(start, weights, rows):
    iota = lax.broadcasted_iota(jnp.int32, (rows, start.shape[1]), 0).astype(F32)
    away = iota - start
    result = jnp.where(away == 0.0, weights[0], 0.0)
    for stencil in range(1, 4):
        result = jnp.where(away == float(stencil), weights[stencil], result)
    return result


def first_plane(block, planes):
    joined = max(1, 8 // planes)
    return lax.div(block, joined) * (joined * planes)


def spread_kernel(rows, points_ref, modes_y_ref, modes_z_ref, out_ref):
    main, last = unpack(points_ref[0])
    count = main.shape[1]
    modes_y = [modes_y_ref[i] for i in range(7)]
    modes_z = [modes_z_ref[i] for i in range(7)]
    values, weights_x = column_values(main, last, modes_y, modes_z)
    weight = plane_rows(main[3:4], weights_x, rows)
    stack = jnp.concatenate([weight * main[c : c + 1] for c in range(3)], axis=0)
    if 3 * rows < LANES:
        stack = jnp.concatenate([stack, jnp.zeros((LANES - 3 * rows, count), F32)], axis=0)
    both = jnp.concatenate(split(stack), axis=0)
    parts = [split(value) for value in values]
    left = jnp.concatenate(
        [jnp.concatenate([p[i] for p in parts], axis=0) for i in range(2)], axis=1
    )
    right = jnp.concatenate([both, both], axis=1)
    acc = lax.dot_general(left, right, (((1,), (1,)), ((), ())), preferred_element_type=F32)
    total = (acc[:, :LANES] + acc[:, LANES:]).T
    out_ref[0] = total[: 3 * rows]


def spread(points, modes_y, modes_z, rows):
    blocks, _, width = points.shape
    count = width // 9 * 8
    cols = 4 * modes_y.shape[1] * KZ
    return pl.pallas_call(
        functools.partial(spread_kernel, rows),
        grid=(blocks,),
        in_specs=[
            pl.BlockSpec((1, 8, width), lambda i: (i, 0, 0)),
            pl.BlockSpec(modes_y.shape, lambda i: (0, 0, 0)),
            pl.BlockSpec(modes_z.shape, lambda i: (0, 0, 0)),
        ],
        out_specs=pl.BlockSpec((1, 3 * rows, cols), lambda i: (i, 0, 0)),
        out_shape=jax.ShapeDtypeStruct((blocks, 3 * rows, cols), F32),
        compiler_params=pltpu.CompilerParams(vmem_limit_bytes=SPREAD_LIMIT),
        cost_estimate=pl.CostEstimate(
            flops=blocks * count * cols * LANES * 14,
            bytes_accessed=blocks * (9 * count + 3 * rows * cols) * 4,
            transcendentals=0,
        ),
        name="spread",
    )(points, modes_y, modes_z)


def solve_kernel(planes, rows, parts, ids_ref, *refs):
    piece_refs = refs[:parts]
    forward_ref, back_ref, waves_ref, out_ref, modes, stacked = refs[parts:]
    extra = 8
    out_ref[...] = jnp.zeros_like(out_ref)
    before = 0
    for piece_ref in piece_refs:

        @pl.loop(0, piece_ref.shape[0])
        def _(index):
            first = pl.multiple_of(first_plane(ids_ref[before + index], planes), 8)
            for c in range(3):
                out_ref[c, pl.ds(first, rows)] += piece_ref[index, c * rows : (c + 1) * rows]

        before += piece_ref.shape[0]
    for c in range(3):
        out_ref[c, 0:extra] += out_ref[c, NX : NX + extra]
    half = NX // 2
    quarter = NX // 4
    lanes = waves_ref.shape[1]

    def fill(value):
        high, low = split(value)
        stacked[0:half] = high
        stacked[half : 2 * half] = high
        stacked[2 * half : 3 * half] = low

    for parity in range(2):

        @pl.loop(0, 3)
        def _(c):
            first = out_ref[c, 0:half]
            second = out_ref[c, half:NX]
            fill(first + second if parity == 0 else first - second)
            modes[parity, c] = jnp.dot(forward_ref[parity], stacked[...], preferred_element_type=F32)

    wave_y = waves_ref[0:1]
    wave_z = waves_ref[1:2]
    mult = waves_ref[2:3]
    flat = wave_y * wave_y + wave_z * wave_z
    group = 8

    for parity in range(2):

        @pl.loop(0, quarter // group)
        def _(index):
            row = pl.multiple_of(index * group, group)
            number = lax.broadcasted_iota(jnp.int32, (group, lanes), 0) + row
            number = (2 * number + parity).astype(F32)
            wave_x = number * (TWO_PI / NX)
            squared = wave_x * wave_x + flat
            anchor = squared == 0.0
            inverse = jnp.where(anchor, 0.0, 1.0 / jnp.where(anchor, 1.0, squared))
            factor = inverse * mult * jnp.where(number == 0.0, 1.0, 2.0)
            waves = (wave_x, wave_y, wave_z)
            values = {}
            for c in range(3):
                for tx in range(2):
                    for tyz in range(4):
                        values[c, tx, tyz // 2, tyz % 2] = modes[
                            parity,
                            c,
                            pl.ds(pl.multiple_of(tx * quarter + row, group), group),
                            tyz * lanes : (tyz + 1) * lanes,
                        ]

            def flip(state, axis):
                return tuple(1 - t if i == axis else t for i, t in enumerate(state))

            states = [(a, b, d) for a in range(2) for b in range(2) for d in range(2)]
            divergence = {}
            for state in states:
                total = None
                for axis in range(3):
                    term = waves[axis] * values[(axis,) + flip(state, axis)]
                    if state[axis]:
                        term = -term
                    total = term if total is None else total + term
                divergence[state] = total * inverse
            for state in states:
                for axis in range(3):
                    term = waves[axis] * divergence[flip(state, axis)]
                    value = values[(axis,) + state]
                    value = value - term if state[axis] else value + term
                    tyz = 2 * state[1] + state[2]
                    modes[
                        parity,
                        axis,
                        pl.ds(pl.multiple_of(state[0] * quarter + row, group), group),
                        tyz * lanes : (tyz + 1) * lanes,
                    ] = value * factor

    @pl.loop(0, 3)
    def _(c):
        fill(modes[0, c])
        even = jnp.dot(back_ref[0], stacked[...], preferred_element_type=F32)
        out_ref[c, 0:half] = even
        fill(modes[1, c])
        odd = jnp.dot(back_ref[1], stacked[...], preferred_element_type=F32)
        even = out_ref[c, 0:half]
        out_ref[c, 0:half] = even + odd
        out_ref[c, half:NX] = even - odd
        out_ref[c, NX : NX + extra] = out_ref[c, 0:extra]


def solve(pieces, ids, waves, forward, back, planes, rows):
    full = pl.BlockSpec(memory_space=pltpu.VMEM)
    cols = pieces[0].shape[2]
    return pl.pallas_call(
        functools.partial(solve_kernel, planes, rows, len(pieces)),
        in_specs=[pl.BlockSpec(memory_space=pltpu.SMEM)] + [full] * (len(pieces) + 3),
        out_specs=full,
        out_shape=jax.ShapeDtypeStruct((3, NX + 8, cols), F32),
        scratch_shapes=[
            pltpu.VMEM((2, 3, NX // 2, cols), F32),
            pltpu.VMEM((3 * NX // 2, cols), BF16),
        ],
        compiler_params=pltpu.CompilerParams(vmem_limit_bytes=SOLVE_LIMIT),
        cost_estimate=pl.CostEstimate(
            flops=36 * NX // 2 * NX // 2 * cols,
            bytes_accessed=6 * NX * cols * 4,
            transcendentals=0,
        ),
        name="solve",
    )(ids, *pieces, forward, back, waves)


def gather_kernel(planes, rows, parts, before, ids_ref, *refs):
    modes_y_ref, modes_z_ref, lines_ref, out_ref, plane = refs[parts:]
    step = pl.program_id(0)
    each = pl.num_programs(0) // parts
    first = pl.multiple_of(first_plane(ids_ref[before + step], planes), 8)
    stack = jnp.concatenate([lines_ref[c, pl.ds(first, rows)] for c in range(3)], axis=0)
    if 3 * rows < LANES:
        stack = jnp.concatenate([stack, jnp.zeros((LANES - 3 * rows, lines_ref.shape[2]), F32)], axis=0)
    high, low = split(stack)
    plane[0:LANES] = high
    plane[LANES:] = low
    modes_y = [modes_y_ref[i] for i in range(7)]
    modes_z = [modes_z_ref[i] for i in range(7)]
    values = refs[0][0]
    for part in range(1, parts):
        values = jnp.where(step >= part * each, refs[part][0], values)
    main, last = unpack(values)
    count = main.shape[1]
    chunk = count // 4
    for index in range(4):
        at = slice(index * chunk, (index + 1) * chunk)
        values, weights_x = column_values(main[:, at], last[:, at], modes_y, modes_z)
        pairs = [split(value) for value in values]
        highs = jnp.concatenate([p[0] for p in pairs], axis=0)
        lows = jnp.concatenate([p[1] for p in pairs], axis=0)
        result = jnp.dot(plane[...], highs, preferred_element_type=F32)
        small = jnp.dot(plane[0:LANES], lows, preferred_element_type=F32)
        result = result[:LANES] + result[LANES:] + small
        weight = plane_rows(main[3:4, at], weights_x, rows)
        out_ref[0, :, at] = jnp.concatenate(
            [
                jnp.sum(weight * result[c * rows : (c + 1) * rows], axis=0, keepdims=True)
                for c in range(3)
            ],
            axis=0,
        )


def gather(points, before, ids, modes_y, modes_z, lines, planes, rows):
    parts = len(points)
    each, _, width = points[0].shape
    count = width // 9 * 8
    blocks = parts * each
    cols = lines.shape[2]

    def at(part):
        return lambda i: (jnp.clip(i - part * each, 0, each - 1), 0, 0)

    return pl.pallas_call(
        functools.partial(gather_kernel, planes, rows, parts, before),
        grid=(blocks,),
        in_specs=[pl.BlockSpec(memory_space=pltpu.SMEM)]
        + [pl.BlockSpec((1, 8, width), at(part)) for part in range(parts)]
        + [
            pl.BlockSpec(modes_y.shape, lambda i: (0, 0, 0)),
            pl.BlockSpec(modes_z.shape, lambda i: (0, 0, 0)),
            pl.BlockSpec(memory_space=pltpu.VMEM),
        ],
        out_specs=pl.BlockSpec((1, 3, count), lambda i: (i, 0, 0)),
        out_shape=jax.ShapeDtypeStruct((blocks, 3, count), F32),
        scratch_shapes=[pltpu.VMEM((2 * LANES, cols), BF16)],
        compiler_params=pltpu.CompilerParams(vmem_limit_bytes=GATHER_LIMIT),
        cost_estimate=pl.CostEstimate(
            flops=blocks * count * cols * LANES * 14,
            bytes_accessed=blocks * 12 * count * 4,
            transcendentals=0,
        ),
        name="interpolate",
    )(ids, *points, modes_y, modes_z, lines)


def line_tables():
    half = NX // 2
    place = np.arange(half)
    forward, back = [], []
    for parity in range(2):
        number = 2 * np.arange(NX // 4) + parity
        angle = (number[:, None] * place[None, :] % NX) * (2.0 * np.pi / NX)
        table = np.concatenate([np.cos(angle), np.sin(angle)], axis=0)
        for tables, value in ((forward, table), (back, table.T)):
            high = value.astype(ml_dtypes.bfloat16)
            low = (value - high.astype(np.float64)).astype(ml_dtypes.bfloat16)
            tables.append(np.concatenate([high, low, high], axis=1))
    return np.stack(forward), np.stack(back)


def mode_table(numbers, length):
    angle = numbers * (2.0 * np.pi / length)
    rows = [numbers]
    for stencil in range(1, 4):
        rows += [np.cos(stencil * angle), np.sin(stencil * angle)]
    table = np.stack(rows, axis=1)[..., None].astype(np.float32)
    return np.broadcast_to(table, table.shape[:3] + (LANES,))


def far_tables(device, devices):
    own_y = (NY // 2) * (NZ // 2) // devices // KZ
    parts_z = NZ // 2 // KZ
    number_y = np.arange(NY // 2).reshape(-1, own_y).astype(np.float64)
    number_z = np.arange(NZ // 2).reshape(-1, KZ).astype(np.float64)
    mult_y = np.where(number_y == 0, 1.0, 2.0)
    mult_z = np.where(number_z == 0, 1.0, 2.0) / float(NX * NY * NZ)
    shape = (number_y.shape[0], parts_z, own_y, KZ)
    waves = [
        np.broadcast_to(number_y[:, None, :, None] * (TWO_PI / NY), shape),
        np.broadcast_to(number_z[None, :, None, :] * (TWO_PI / NZ), shape),
        mult_y[:, None, :, None] * mult_z[None, :, None, :],
    ]
    waves = np.stack([w.reshape(devices, own_y * KZ) for w in waves], axis=1)
    waves = np.concatenate([waves, np.zeros((devices, 5, own_y * KZ))], axis=1)

    def own(table, index):
        return lax.dynamic_index_in_dim(jnp.asarray(table, F32), index, 0, keepdims=False)

    return (
        own(mode_table(number_y, NY), device // parts_z),
        own(mode_table(number_z, NZ), device % parts_z),
        own(waves, device),
    )


def per_device(forces, stencil_start, fraction, tile_pairs, pair_count):
    groups = lax.axis_size("group")
    members = lax.axis_size("dev")
    devices = groups * members
    planes = NX // devices
    device = lax.axis_index("group") * members + lax.axis_index("dev")
    rows = max(8, planes) + 8
    first = first_plane(device, planes).reshape(1)
    own = pack(first, forces, stencil_start, fraction)

    def from_flipped(values, mask):
        pairs = [(i, i ^ mask) for i in range(devices)]
        return lax.ppermute(values, ("group", "dev"), pairs)

    start_masks = (4, 8, 12)
    own_half = jnp.concatenate([own] + [from_flipped(own, mask) for mask in start_masks], axis=0)
    masks = [0, *start_masks]
    last_bit = devices.bit_length() - 2
    bits = [1] + list(range(4, last_bit))
    for bit in bits:
        own_half = jnp.concatenate([own_half, from_flipped(own_half, 1 << bit)], axis=0)
        masks = masks + [m ^ 1 << bit for m in masks]
    top = 1 << last_bit
    core = from_flipped(own_half, 1)
    other = from_flipped(own_half, top)
    blocks = [own_half, core, other, from_flipped(other, 1)]
    each = len(masks)
    masks = np.array([m ^ flip for flip in (0, 1, top, top ^ 1) for m in masks], np.int32)
    ids = device ^ jnp.asarray(masks)
    modes_y, modes_z, waves = far_tables(device, devices)
    forward, back = line_tables()
    pieces = [spread(points, modes_y, modes_z, rows) for points in blocks]
    lines = solve(pieces, ids, waves, jnp.asarray(forward), jnp.asarray(back), planes, rows)

    def sums(first, count):
        return gather(
            blocks[first : first + count], first * each, ids, modes_y, modes_z, lines, planes, rows
        )

    across = sums(2, 2)
    across = across[:each] + from_flipped(across[each:], 1)
    across = from_flipped(across, top)
    beside = from_flipped(sums(1, 1), 1)
    total = sums(0, 1) + beside + across
    for bit in reversed(bits):
        half = total.shape[0] // 2
        total = total[:half] + from_flipped(total[half:], 1 << bit)
    far = total[0]
    for index, mask in enumerate(start_masks):
        far = far + from_flipped(total[index + 1], mask)
    return far + near_field(forces, stencil_start, fraction, tile_pairs, pair_count)


def solution(mesh):
    in_specs = (
        P(None, ("group", "dev")),
        P(None, ("group", "dev")),
        P(None, ("group", "dev")),
        P(("group", "dev"), None),
        P(("group", "dev")),
    )
    out_specs = P(None, ("group", "dev"))
    return jax.shard_map(
        per_device, mesh=mesh, in_specs=in_specs, out_specs=out_specs, check_vma=False
    )
```

```python
import functools

import jax
import jax.numpy as jnp
import ml_dtypes
import numpy as np
from jax import lax
from jax.experimental import pallas as pl
from jax.experimental.pallas import tpu as pltpu
from jax.sharding import PartitionSpec as P

NX = 1024
NY = 128
NZ = 128

TWO_PI = 6.283185307179586
EPS_SQ = 1.0
RANGE_SQ = 16.0
NEAR_SCALE = 0.25

LANES = 128
SPREAD_LIMIT = 24 * 2**20
SOLVE_LIMIT = 20 * 2**20
GATHER_LIMIT = 20 * 2**20
KEEP_BYTES = 32 * 2**20
KZ = 16
BF16 = jnp.bfloat16
F32 = jnp.float32


def wrapped(gap, length):
    gap = jnp.where(gap > length / 2, gap - length, gap)
    return jnp.where(gap < -length / 2, gap + length, gap)


def near_kernel(pairs_ref, count_ref, forces_ref, start_ref, fraction_ref, out_ref, columns):
    tiles = out_ref.shape[1] // LANES
    out_ref[...] = jnp.zeros_like(out_ref)
    for tile in range(tiles):
        at = slice(tile * LANES, (tile + 1) * LANES)
        nine = jnp.concatenate(
            [
                start_ref[:, at].astype(F32),
                fraction_ref[:, at],
                forces_ref[:, at],
                jnp.zeros((7, LANES), F32),
            ],
            axis=0,
        )
        columns[at] = nine.T

    @pl.loop(0, count_ref[0])
    def _(slot):
        target = pl.ds(pl.multiple_of(pairs_ref[2 * slot] * LANES, LANES), LANES)
        base = pl.multiple_of(pairs_ref[2 * slot + 1] * LANES, LANES)
        start = start_ref[:, target].astype(F32)
        fraction = fraction_ref[:, target]
        sums = [jnp.zeros((8, LANES), F32) for _ in range(3)]
        for row in range(0, LANES, 8):
            source = columns[pl.ds(base + row, 8)]
            gaps = []
            for axis, length in enumerate((None, NY, NZ)):
                gap = start[axis : axis + 1] - source[:, axis : axis + 1]
                if length is not None:
                    gap = wrapped(gap, float(length))
                gaps.append(gap + (fraction[axis : axis + 1] - source[:, 3 + axis : 4 + axis]))
            pulled = [source[:, 6 + axis : 7 + axis] for axis in range(3)]
            distance = gaps[0] * gaps[0] + gaps[1] * gaps[1] + gaps[2] * gaps[2]
            inverse = lax.rsqrt(distance + EPS_SQ)
            fall = NEAR_SCALE * jnp.exp(distance * (-1.0 / RANGE_SQ)) * (inverse * inverse * inverse)
            diagonal = (distance + 2.0 * EPS_SQ) * fall
            along = fall * (gaps[0] * pulled[0] + gaps[1] * pulled[1] + gaps[2] * pulled[2])
            sums = [sums[i] + (diagonal * pulled[i] + gaps[i] * along) for i in range(3)]
        out_ref[:, target] += jnp.concatenate(
            [jnp.sum(value, axis=0, keepdims=True) for value in sums], axis=0
        )


def near_field(forces, stencil_start, fraction, tile_pairs, pair_count):
    smem = pl.BlockSpec(memory_space=pltpu.SMEM)
    vmem = pl.BlockSpec(memory_space=pltpu.VMEM)
    points = forces.shape[1]
    slots = tile_pairs.shape[0]
    return pl.pallas_call(
        near_kernel,
        in_specs=[smem, smem, vmem, vmem, vmem],
        out_specs=vmem,
        out_shape=jax.ShapeDtypeStruct((3, points), F32),
        scratch_shapes=[pltpu.VMEM((points, 16), F32)],
        compiler_params=pltpu.CompilerParams(vmem_limit_bytes=8 * 2**20),
        cost_estimate=pl.CostEstimate(
            flops=slots * LANES * LANES * 6000, bytes_accessed=points * 48, transcendentals=0
        ),
        name="near",
    )(tile_pairs.reshape(-1), pair_count, forces, stencil_start, fraction)


def pack_kernel(first_ref, forces_ref, start_ref, fraction_ref, out_ref):
    points = forces_ref.shape[1]
    piece = points // 8
    start = start_ref[...]
    out_ref[0, 0:3, 0:points] = forces_ref[...]
    out_ref[0, 3:4, 0:points] = (start[0:1] - first_ref[0]).astype(F32)
    out_ref[0, 4:6, 0:points] = start[1:3].astype(F32)
    out_ref[0, 6:8, 0:points] = fraction_ref[0:2]
    for row in range(8):
        out_ref[0, row : row + 1, points:] = fraction_ref[2:3, row * piece : (row + 1) * piece]


def pack(first, forces, stencil_start, fraction):
    vmem = pl.BlockSpec(memory_space=pltpu.VMEM)
    points = forces.shape[1]
    return pl.pallas_call(
        pack_kernel,
        in_specs=[pl.BlockSpec(memory_space=pltpu.SMEM), vmem, vmem, vmem],
        out_specs=vmem,
        out_shape=jax.ShapeDtypeStruct((1, 8, points + points // 8), F32),
        name="pack",
    )(first, forces, stencil_start, fraction)


def unpack(values):
    points = values.shape[1] // 9 * 8
    pieces = [values[row : row + 1, points:] for row in range(8)]
    return values[:, :points], jnp.concatenate(pieces, axis=1)


def split(value):
    high = value.astype(BF16)
    low = (value - high.astype(F32)).astype(BF16)
    return high, low


def spline_weights(fraction):
    square = fraction * fraction
    cube = square * fraction
    rest = 1.0 - fraction
    return [
        rest * rest * rest * (1.0 / 6.0),
        (3.0 * cube - 6.0 * square + 4.0) * (1.0 / 6.0),
        (-3.0 * cube + 3.0 * square + 3.0 * fraction + 1.0) * (1.0 / 6.0),
        cube * (1.0 / 6.0),
    ]


def cos_sin_turns(turns):
    part = turns - jnp.floor(turns + 0.5)
    half = part * (0.5 * TWO_PI)
    square = half * half
    sine = half * (
        1.0
        + square
        * (
            -1.0 / 6.0
            + square
            * (1.0 / 120.0 + square * (-1.0 / 5040.0 + square * (1.0 / 362880.0 + square * (-1.0 / 39916800.0))))
        )
    )
    cosine = 1.0 + square * (
        -0.5
        + square
        * (
            1.0 / 24.0
            + square
            * (-1.0 / 720.0 + square * (1.0 / 40320.0 + square * (-1.0 / 3628800.0 + square * (1.0 / 479001600.0))))
        )
    )
    return 1.0 - 2.0 * sine * sine, 2.0 * sine * cosine


def widen(table, width):
    return jnp.concatenate([table] * (width // LANES), axis=1)


def mode_rows(start, weights, modes, length):
    width = start.shape[1]
    cosine, sine = cos_sin_turns(widen(modes[0], width) * start * (1.0 / length))
    sum_cos = weights[0] + weights[1] * widen(modes[1], width)
    sum_sin = weights[1] * widen(modes[2], width)
    sum_cos = sum_cos + weights[2] * widen(modes[3], width) + weights[3] * widen(modes[5], width)
    sum_sin = sum_sin + weights[2] * widen(modes[4], width) + weights[3] * widen(modes[6], width)
    return cosine * sum_cos - sine * sum_sin, sine * sum_cos + cosine * sum_sin


def basis_rows(main, last, modes_y, modes_z):
    weights_y = [w[1:2] for w in spline_weights(main[6:8])]
    rows_y = mode_rows(main[4:5], weights_y, modes_y, NY)
    rows_z = mode_rows(main[5:6], spline_weights(last), modes_z, NZ)
    return rows_y, rows_z


def column_values(rows_y, rows_z):
    values = []
    for ty in range(2):
        for tz in range(2):
            for iy in range(rows_y[0].shape[0]):
                values.append(rows_y[ty][iy : iy + 1] * rows_z[tz])
    return values


def plane_rows(start, weights, rows):
    iota = lax.broadcasted_iota(jnp.int32, (rows, start.shape[1]), 0).astype(F32)
    away = iota - start
    result = jnp.where(away == 0.0, weights[0], 0.0)
    for stencil in range(1, 4):
        result = jnp.where(away == float(stencil), weights[stencil], result)
    return result


def first_plane(block, planes):
    joined = max(1, 8 // planes)
    return lax.div(block, joined) * (joined * planes)


def spread_kernel(rows, points_ref, modes_y_ref, modes_z_ref, out_ref, *kept_refs):
    main, last = unpack(points_ref[0])
    count = main.shape[1]
    modes_y = [modes_y_ref[i] for i in range(7)]
    modes_z = [modes_z_ref[i] for i in range(7)]
    rows_y, rows_z = basis_rows(main, last, modes_y, modes_z)
    for kept_ref in kept_refs:
        kept_ref[0] = jnp.concatenate([*rows_y, *rows_z], axis=0)
    values = column_values(rows_y, rows_z)
    weights_x = spline_weights(main[6:7])
    weight = plane_rows(main[3:4], weights_x, rows)
    stack = jnp.concatenate([weight * main[c : c + 1] for c in range(3)], axis=0)
    if 3 * rows < LANES:
        stack = jnp.concatenate([stack, jnp.zeros((LANES - 3 * rows, count), F32)], axis=0)
    both = jnp.concatenate(split(stack), axis=0)
    parts = [split(value) for value in values]
    left = jnp.concatenate(
        [jnp.concatenate([p[i] for p in parts], axis=0) for i in range(2)], axis=1
    )
    right = jnp.concatenate([both, both], axis=1)
    acc = lax.dot_general(left, right, (((1,), (1,)), ((), ())), preferred_element_type=F32)
    total = (acc[:, :LANES] + acc[:, LANES:]).T
    out_ref[0] = total[: 3 * rows]


def keeps(points, modes_y):
    blocks_rows = 2 * (modes_y.shape[1] + KZ)
    return modes_y.shape[1] % 8 == 0 and lax.axis_size(("group", "dev")) * blocks_rows * (
        points.shape[2] // 9 * 8
    ) * 4 <= KEEP_BYTES


def spread(points, modes_y, modes_z, rows, keep):
    blocks, _, width = points.shape
    count = width // 9 * 8
    own_y = modes_y.shape[1]
    cols = 4 * own_y * KZ
    kept = 2 * (own_y + KZ)
    out_specs = [pl.BlockSpec((1, 3 * rows, cols), lambda i: (i, 0, 0))]
    out_shape = [jax.ShapeDtypeStruct((blocks, 3 * rows, cols), F32)]
    if keep:
        out_specs.append(pl.BlockSpec((1, kept, count), lambda i: (i, 0, 0)))
        out_shape.append(jax.ShapeDtypeStruct((blocks, kept, count), F32))
    return pl.pallas_call(
        functools.partial(spread_kernel, rows),
        grid=(blocks,),
        in_specs=[
            pl.BlockSpec((1, 8, width), lambda i: (i, 0, 0)),
            pl.BlockSpec(modes_y.shape, lambda i: (0, 0, 0)),
            pl.BlockSpec(modes_z.shape, lambda i: (0, 0, 0)),
        ],
        out_specs=out_specs,
        out_shape=out_shape,
        compiler_params=pltpu.CompilerParams(vmem_limit_bytes=SPREAD_LIMIT),
        cost_estimate=pl.CostEstimate(
            flops=blocks * count * cols * LANES * 14,
            bytes_accessed=blocks * (9 * count + 3 * rows * cols) * 4,
            transcendentals=0,
        ),
        name="spread",
    )(points, modes_y, modes_z)


def solve_kernel(planes, rows, parts, ids_ref, *refs):
    piece_refs = refs[:parts]
    forward_ref, back_ref, waves_ref, out_ref, modes, stacked = refs[parts:]
    extra = 8
    out_ref[...] = jnp.zeros_like(out_ref)
    before = 0
    for piece_ref in piece_refs:

        @pl.loop(0, piece_ref.shape[0])
        def _(index):
            first = pl.multiple_of(first_plane(ids_ref[before + index], planes), 8)
            for c in range(3):
                out_ref[c, pl.ds(first, rows)] += piece_ref[index, c * rows : (c + 1) * rows]

        before += piece_ref.shape[0]
    for c in range(3):
        out_ref[c, 0:extra] += out_ref[c, NX : NX + extra]
    half = NX // 2
    quarter = NX // 4
    lanes = waves_ref.shape[1]

    def fill(value):
        high, low = split(value)
        stacked[0:half] = high
        stacked[half : 2 * half] = high
        stacked[2 * half : 3 * half] = low

    for parity in range(2):

        @pl.loop(0, 3)
        def _(c):
            first = out_ref[c, 0:half]
            second = out_ref[c, half:NX]
            fill(first + second if parity == 0 else first - second)
            modes[parity, c] = jnp.dot(forward_ref[parity], stacked[...], preferred_element_type=F32)

    wave_y = waves_ref[0:1]
    wave_z = waves_ref[1:2]
    mult = waves_ref[2:3]
    flat = wave_y * wave_y + wave_z * wave_z
    group = 8

    for parity in range(2):

        @pl.loop(0, quarter // group)
        def _(index):
            row = pl.multiple_of(index * group, group)
            number = lax.broadcasted_iota(jnp.int32, (group, lanes), 0) + row
            number = (2 * number + parity).astype(F32)
            wave_x = number * (TWO_PI / NX)
            squared = wave_x * wave_x + flat
            anchor = squared == 0.0
            inverse = jnp.where(anchor, 0.0, 1.0 / jnp.where(anchor, 1.0, squared))
            factor = inverse * mult * jnp.where(number == 0.0, 1.0, 2.0)
            waves = (wave_x, wave_y, wave_z)
            values = {}
            for c in range(3):
                for tx in range(2):
                    for tyz in range(4):
                        values[c, tx, tyz // 2, tyz % 2] = modes[
                            parity,
                            c,
                            pl.ds(pl.multiple_of(tx * quarter + row, group), group),
                            tyz * lanes : (tyz + 1) * lanes,
                        ]

            def flip(state, axis):
                return tuple(1 - t if i == axis else t for i, t in enumerate(state))

            states = [(a, b, d) for a in range(2) for b in range(2) for d in range(2)]
            divergence = {}
            for state in states:
                total = None
                for axis in range(3):
                    term = waves[axis] * values[(axis,) + flip(state, axis)]
                    if state[axis]:
                        term = -term
                    total = term if total is None else total + term
                divergence[state] = total * inverse
            for state in states:
                for axis in range(3):
                    term = waves[axis] * divergence[flip(state, axis)]
                    value = values[(axis,) + state]
                    value = value - term if state[axis] else value + term
                    tyz = 2 * state[1] + state[2]
                    modes[
                        parity,
                        axis,
                        pl.ds(pl.multiple_of(state[0] * quarter + row, group), group),
                        tyz * lanes : (tyz + 1) * lanes,
                    ] = value * factor

    @pl.loop(0, 3)
    def _(c):
        fill(modes[0, c])
        even = jnp.dot(back_ref[0], stacked[...], preferred_element_type=F32)
        out_ref[c, 0:half] = even
        fill(modes[1, c])
        odd = jnp.dot(back_ref[1], stacked[...], preferred_element_type=F32)
        even = out_ref[c, 0:half]
        out_ref[c, 0:half] = even + odd
        out_ref[c, half:NX] = even - odd
        out_ref[c, NX : NX + extra] = out_ref[c, 0:extra]


def solve(pieces, ids, waves, forward, back, planes, rows):
    full = pl.BlockSpec(memory_space=pltpu.VMEM)
    cols = pieces[0].shape[2]
    return pl.pallas_call(
        functools.partial(solve_kernel, planes, rows, len(pieces)),
        in_specs=[pl.BlockSpec(memory_space=pltpu.SMEM)] + [full] * (len(pieces) + 3),
        out_specs=full,
        out_shape=jax.ShapeDtypeStruct((3, NX + 8, cols), F32),
        scratch_shapes=[
            pltpu.VMEM((2, 3, NX // 2, cols), F32),
            pltpu.VMEM((3 * NX // 2, cols), BF16),
        ],
        compiler_params=pltpu.CompilerParams(vmem_limit_bytes=SOLVE_LIMIT),
        cost_estimate=pl.CostEstimate(
            flops=36 * NX // 2 * NX // 2 * cols,
            bytes_accessed=6 * NX * cols * 4,
            transcendentals=0,
        ),
        name="solve",
    )(ids, *pieces, forward, back, waves)


def gather_kernel(planes, rows, before, kept, ids_ref, points_ref, *refs):
    basis_refs, (lines_ref, out_ref, plane) = refs[:-3], refs[-3:]
    step = pl.program_id(0)
    first = pl.multiple_of(first_plane(ids_ref[before + step], planes), 8)
    stack = jnp.concatenate([lines_ref[c, pl.ds(first, rows)] for c in range(3)], axis=0)
    if 3 * rows < LANES:
        stack = jnp.concatenate([stack, jnp.zeros((LANES - 3 * rows, lines_ref.shape[2]), F32)], axis=0)
    high, low = split(stack)
    plane[0:LANES] = high
    plane[LANES:] = low
    main, last = unpack(points_ref[0])
    count = main.shape[1]
    chunk = count // 4
    if kept:
        own_y = basis_refs[0].shape[1] // 2 - KZ
    else:
        modes_y, modes_z = [[ref[i] for i in range(7)] for ref in basis_refs]
    for index in range(4):
        at = slice(index * chunk, (index + 1) * chunk)
        if kept:
            rows_y = [basis_refs[0][0, i * own_y : (i + 1) * own_y, at] for i in range(2)]
            rows_z = [
                basis_refs[0][0, 2 * own_y + i * KZ : 2 * own_y + (i + 1) * KZ, at] for i in range(2)
            ]
        else:
            rows_y, rows_z = basis_rows(main[:, at], last[:, at], modes_y, modes_z)
        pairs = [split(value) for value in column_values(rows_y, rows_z)]
        highs = jnp.concatenate([p[0] for p in pairs], axis=0)
        lows = jnp.concatenate([p[1] for p in pairs], axis=0)
        result = jnp.dot(plane[...], highs, preferred_element_type=F32)
        small = jnp.dot(plane[0:LANES], lows, preferred_element_type=F32)
        result = result[:LANES] + result[LANES:] + small
        weight = plane_rows(main[3:4, at], spline_weights(main[6:7, at]), rows)
        out_ref[0, :, at] = jnp.concatenate(
            [
                jnp.sum(weight * result[c * rows : (c + 1) * rows], axis=0, keepdims=True)
                for c in range(3)
            ],
            axis=0,
        )


def gather(points, before, ids, basis, lines, planes, rows):
    blocks, _, width = points.shape
    count = width // 9 * 8
    cols = lines.shape[2]
    kept = len(basis) == 1
    if kept:
        basis_specs = [pl.BlockSpec((1,) + basis[0].shape[1:], lambda i: (i, 0, 0))]
    else:
        basis_specs = [pl.BlockSpec(table.shape, lambda i: (0, 0, 0)) for table in basis]
    return pl.pallas_call(
        functools.partial(gather_kernel, planes, rows, before, kept),
        grid=(blocks,),
        in_specs=[
            pl.BlockSpec(memory_space=pltpu.SMEM),
            pl.BlockSpec((1, 8, width), lambda i: (i, 0, 0)),
            *basis_specs,
            pl.BlockSpec(memory_space=pltpu.VMEM),
        ],
        out_specs=pl.BlockSpec((1, 3, count), lambda i: (i, 0, 0)),
        out_shape=jax.ShapeDtypeStruct((blocks, 3, count), F32),
        scratch_shapes=[pltpu.VMEM((2 * LANES, cols), BF16)],
        compiler_params=pltpu.CompilerParams(vmem_limit_bytes=GATHER_LIMIT),
        cost_estimate=pl.CostEstimate(
            flops=blocks * count * cols * LANES * 14,
            bytes_accessed=blocks * 12 * count * 4,
            transcendentals=0,
        ),
        name="interpolate",
    )(ids, points, *basis, lines)


def line_tables():
    half = NX // 2
    place = np.arange(half)
    forward, back = [], []
    for parity in range(2):
        number = 2 * np.arange(NX // 4) + parity
        angle = (number[:, None] * place[None, :] % NX) * (2.0 * np.pi / NX)
        table = np.concatenate([np.cos(angle), np.sin(angle)], axis=0)
        for tables, value in ((forward, table), (back, table.T)):
            high = value.astype(ml_dtypes.bfloat16)
            low = (value - high.astype(np.float64)).astype(ml_dtypes.bfloat16)
            tables.append(np.concatenate([high, low, high], axis=1))
    return np.stack(forward), np.stack(back)


def mode_table(numbers, length):
    angle = numbers * (2.0 * np.pi / length)
    rows = [numbers]
    for stencil in range(1, 4):
        rows += [np.cos(stencil * angle), np.sin(stencil * angle)]
    table = np.stack(rows, axis=1)[..., None].astype(np.float32)
    return np.broadcast_to(table, table.shape[:3] + (LANES,))


def far_tables(device, devices):
    own_y = (NY // 2) * (NZ // 2) // devices // KZ
    parts_z = NZ // 2 // KZ
    number_y = np.arange(NY // 2).reshape(-1, own_y).astype(np.float64)
    number_z = np.arange(NZ // 2).reshape(-1, KZ).astype(np.float64)
    mult_y = np.where(number_y == 0, 1.0, 2.0)
    mult_z = np.where(number_z == 0, 1.0, 2.0) / float(NX * NY * NZ)
    shape = (number_y.shape[0], parts_z, own_y, KZ)
    waves = [
        np.broadcast_to(number_y[:, None, :, None] * (TWO_PI / NY), shape),
        np.broadcast_to(number_z[None, :, None, :] * (TWO_PI / NZ), shape),
        mult_y[:, None, :, None] * mult_z[None, :, None, :],
    ]
    waves = np.stack([w.reshape(devices, own_y * KZ) for w in waves], axis=1)
    waves = np.concatenate([waves, np.zeros((devices, 5, own_y * KZ))], axis=1)

    def own(table, index):
        return lax.dynamic_index_in_dim(jnp.asarray(table, F32), index, 0, keepdims=False)

    return (
        own(mode_table(number_y, NY), device // parts_z),
        own(mode_table(number_z, NZ), device % parts_z),
        own(waves, device),
    )


def per_device(forces, stencil_start, fraction, tile_pairs, pair_count):
    groups = lax.axis_size("group")
    members = lax.axis_size("dev")
    devices = groups * members
    planes = NX // devices
    device = lax.axis_index("group") * members + lax.axis_index("dev")
    rows = max(8, planes) + 8
    first = first_plane(device, planes).reshape(1)
    own = pack(first, forces, stencil_start, fraction)

    def from_flipped(values, mask):
        pairs = [(i, i ^ mask) for i in range(devices)]
        return lax.ppermute(values, ("group", "dev"), pairs)

    near_masks = (4, 8, 12)
    parts = [own, jnp.concatenate([from_flipped(own, mask) for mask in near_masks], axis=0)]
    masks = [0, *near_masks]
    own_half = jnp.concatenate(parts, axis=0)
    last_bit = devices.bit_length() - 2
    bits = [1] + list(range(4, last_bit))
    for bit in bits:
        parts.append(from_flipped(own_half, 1 << bit))
        own_half = jnp.concatenate([own_half, parts[-1]], axis=0)
        masks = masks + [m ^ 1 << bit for m in masks]
    top = 1 << last_bit
    parts.append(from_flipped(own_half, 1))
    other = from_flipped(own_half, top)
    parts += [other, from_flipped(other, 1)]
    masks = np.array([m ^ flip for flip in (0, 1, top, top ^ 1) for m in masks], np.int32)
    ids = device ^ jnp.asarray(masks)
    modes_y, modes_z, waves = far_tables(device, devices)
    forward, back = line_tables()
    keep = keeps(own, modes_y)
    spreads = [spread(points, modes_y, modes_z, rows, keep) for points in parts]
    pieces = [result[0] for result in spreads]
    lines = solve(pieces, ids, waves, jnp.asarray(forward), jnp.asarray(back), planes, rows)
    firsts = np.cumsum([0] + [points.shape[0] for points in parts])

    def sums(part):
        basis = spreads[part][1:] if keep else [modes_y, modes_z]
        return gather(parts[part], int(firsts[part]), ids, basis, lines, planes, rows)

    count = len(parts)
    across = from_flipped(sums(count - 1), 1)
    across = from_flipped(sums(count - 2) + across, top)
    total = across + from_flipped(sums(count - 3), 1)
    for part in range(count - 4, 1, -1):
        half = total.shape[0] // 2
        total = total[:half] + from_flipped(sums(part) + total[half:], 1 << bits[part - 2])
    beside = sums(1) + total[1:]
    far = (sums(0) + total[:1])[0]
    for index, mask in enumerate(near_masks):
        far = far + from_flipped(beside[index], mask)
    return far + near_field(forces, stencil_start, fraction, tile_pairs, pair_count)


def solution(mesh):
    in_specs = (
        P(None, ("group", "dev")),
        P(None, ("group", "dev")),
        P(None, ("group", "dev")),
        P(("group", "dev"), None),
        P(("group", "dev")),
    )
    out_specs = P(None, ("group", "dev"))
    return jax.shard_map(
        per_device, mesh=mesh, in_specs=in_specs, out_specs=out_specs, check_vma=False
    )
```

```python
import functools

import jax
import jax.numpy as jnp
import ml_dtypes
import numpy as np
from jax import lax
from jax.experimental import pallas as pl
from jax.experimental.pallas import tpu as pltpu
from jax.sharding import PartitionSpec as P

NX = 1024
NY = 128
NZ = 128

TWO_PI = 6.283185307179586
EPS_SQ = 1.0
RANGE_SQ = 16.0
NEAR_SCALE = 0.25

LANES = 128
SPREAD_LIMIT = 24 * 2**20
SOLVE_LIMIT = 20 * 2**20
GATHER_LIMIT = 20 * 2**20
KEEP_BYTES = 32 * 2**20
KZ = 16
BF16 = jnp.bfloat16
F32 = jnp.float32


def wrapped(gap, length):
    gap = jnp.where(gap > length / 2, gap - length, gap)
    return jnp.where(gap < -length / 2, gap + length, gap)


def near_kernel(pairs_ref, count_ref, forces_ref, start_ref, fraction_ref, out_ref, columns):
    tiles = out_ref.shape[1] // LANES
    out_ref[...] = jnp.zeros_like(out_ref)

    @pl.loop(0, tiles)
    def _(tile):
        at = pl.ds(pl.multiple_of(tile * LANES, LANES), LANES)
        nine = jnp.concatenate(
            [start_ref[:, at].astype(F32), fraction_ref[:, at], forces_ref[:, at]], axis=0
        )
        for value in range(9):
            wide = jnp.broadcast_to(nine[value : value + 1], (LANES, LANES))
            columns[value, at] = wide.T

    @pl.loop(0, count_ref[0])
    def _(slot):
        target = pl.ds(pl.multiple_of(pairs_ref[2 * slot] * LANES, LANES), LANES)
        base = pl.multiple_of(pairs_ref[2 * slot + 1] * LANES, LANES)
        start = start_ref[:, target].astype(F32)
        fraction = fraction_ref[:, target]
        sums = [jnp.zeros((8, LANES), F32) for _ in range(3)]
        for row in range(0, LANES, 8):
            source = [columns[value, pl.ds(base + row, 8)] for value in range(9)]
            gaps = []
            for axis, length in enumerate((None, NY, NZ)):
                gap = start[axis : axis + 1] - source[axis]
                if length is not None:
                    gap = wrapped(gap, float(length))
                gaps.append(gap + (fraction[axis : axis + 1] - source[3 + axis]))
            pulled = source[6:9]
            distance = gaps[0] * gaps[0] + gaps[1] * gaps[1] + gaps[2] * gaps[2]
            inverse = lax.rsqrt(distance + EPS_SQ)
            fall = NEAR_SCALE * jnp.exp(distance * (-1.0 / RANGE_SQ)) * (inverse * inverse * inverse)
            diagonal = (distance + 2.0 * EPS_SQ) * fall
            along = fall * (gaps[0] * pulled[0] + gaps[1] * pulled[1] + gaps[2] * pulled[2])
            sums = [sums[i] + (diagonal * pulled[i] + gaps[i] * along) for i in range(3)]
        out_ref[:, target] += jnp.concatenate(
            [jnp.sum(value, axis=0, keepdims=True) for value in sums], axis=0
        )


def near_field(forces, stencil_start, fraction, tile_pairs, pair_count):
    smem = pl.BlockSpec(memory_space=pltpu.SMEM)
    vmem = pl.BlockSpec(memory_space=pltpu.VMEM)
    points = forces.shape[1]
    slots = tile_pairs.shape[0]
    return pl.pallas_call(
        near_kernel,
        in_specs=[smem, smem, vmem, vmem, vmem],
        out_specs=vmem,
        out_shape=jax.ShapeDtypeStruct((3, points), F32),
        scratch_shapes=[pltpu.VMEM((9, points, LANES), F32)],
        compiler_params=pltpu.CompilerParams(vmem_limit_bytes=16 * 2**20),
        cost_estimate=pl.CostEstimate(
            flops=slots * LANES * LANES * 6000, bytes_accessed=points * 48, transcendentals=0
        ),
        name="near",
    )(tile_pairs.reshape(-1), pair_count, forces, stencil_start, fraction)


def pack_kernel(first_ref, forces_ref, start_ref, fraction_ref, out_ref):
    points = forces_ref.shape[1]
    piece = points // 8
    start = start_ref[...]
    out_ref[0, 0:3, 0:points] = forces_ref[...]
    out_ref[0, 3:4, 0:points] = (start[0:1] - first_ref[0]).astype(F32)
    out_ref[0, 4:6, 0:points] = start[1:3].astype(F32)
    out_ref[0, 6:8, 0:points] = fraction_ref[0:2]
    for row in range(8):
        out_ref[0, row : row + 1, points:] = fraction_ref[2:3, row * piece : (row + 1) * piece]


def pack(first, forces, stencil_start, fraction):
    vmem = pl.BlockSpec(memory_space=pltpu.VMEM)
    points = forces.shape[1]
    return pl.pallas_call(
        pack_kernel,
        in_specs=[pl.BlockSpec(memory_space=pltpu.SMEM), vmem, vmem, vmem],
        out_specs=vmem,
        out_shape=jax.ShapeDtypeStruct((1, 8, points + points // 8), F32),
        name="pack",
    )(first, forces, stencil_start, fraction)


def unpack(values):
    points = values.shape[1] // 9 * 8
    pieces = [values[row : row + 1, points:] for row in range(8)]
    return values[:, :points], jnp.concatenate(pieces, axis=1)


def split(value):
    high = value.astype(BF16)
    low = (value - high.astype(F32)).astype(BF16)
    return high, low


def spline_weights(fraction):
    square = fraction * fraction
    cube = square * fraction
    rest = 1.0 - fraction
    return [
        rest * rest * rest * (1.0 / 6.0),
        (3.0 * cube - 6.0 * square + 4.0) * (1.0 / 6.0),
        (-3.0 * cube + 3.0 * square + 3.0 * fraction + 1.0) * (1.0 / 6.0),
        cube * (1.0 / 6.0),
    ]


def cos_sin_turns(turns):
    part = turns - jnp.floor(turns + 0.5)
    half = part * (0.5 * TWO_PI)
    square = half * half
    sine = half * (
        1.0
        + square
        * (
            -1.0 / 6.0
            + square
            * (1.0 / 120.0 + square * (-1.0 / 5040.0 + square * (1.0 / 362880.0 + square * (-1.0 / 39916800.0))))
        )
    )
    cosine = 1.0 + square * (
        -0.5
        + square
        * (
            1.0 / 24.0
            + square
            * (-1.0 / 720.0 + square * (1.0 / 40320.0 + square * (-1.0 / 3628800.0 + square * (1.0 / 479001600.0))))
        )
    )
    return 1.0 - 2.0 * sine * sine, 2.0 * sine * cosine


def widen(table, width):
    return jnp.concatenate([table] * (width // LANES), axis=1)


def mode_rows(start, weights, modes, length):
    width = start.shape[1]
    cosine, sine = cos_sin_turns(widen(modes[0], width) * start * (1.0 / length))
    sum_cos = weights[0] + weights[1] * widen(modes[1], width)
    sum_sin = weights[1] * widen(modes[2], width)
    sum_cos = sum_cos + weights[2] * widen(modes[3], width) + weights[3] * widen(modes[5], width)
    sum_sin = sum_sin + weights[2] * widen(modes[4], width) + weights[3] * widen(modes[6], width)
    return cosine * sum_cos - sine * sum_sin, sine * sum_cos + cosine * sum_sin


def basis_rows(main, last, modes_y, modes_z):
    weights_y = [w[1:2] for w in spline_weights(main[6:8])]
    rows_y = mode_rows(main[4:5], weights_y, modes_y, NY)
    rows_z = mode_rows(main[5:6], spline_weights(last), modes_z, NZ)
    return rows_y, rows_z


def column_values(rows_y, rows_z):
    values = []
    for ty in range(2):
        for tz in range(2):
            for iy in range(rows_y[0].shape[0]):
                values.append(rows_y[ty][iy : iy + 1] * rows_z[tz])
    return values


def plane_rows(start, weights, rows):
    iota = lax.broadcasted_iota(jnp.int32, (rows, start.shape[1]), 0).astype(F32)
    away = iota - start
    result = jnp.where(away == 0.0, weights[0], 0.0)
    for stencil in range(1, 4):
        result = jnp.where(away == float(stencil), weights[stencil], result)
    return result


def first_plane(block, planes):
    joined = max(1, 8 // planes)
    return lax.div(block, joined) * (joined * planes)


def spread_kernel(rows, points_ref, modes_y_ref, modes_z_ref, out_ref, *kept_refs):
    main, last = unpack(points_ref[0])
    count = main.shape[1]
    modes_y = [modes_y_ref[i] for i in range(7)]
    modes_z = [modes_z_ref[i] for i in range(7)]
    rows_y, rows_z = basis_rows(main, last, modes_y, modes_z)
    for kept_ref in kept_refs:
        kept_ref[0] = jnp.concatenate([*rows_y, *rows_z], axis=0)
    values = column_values(rows_y, rows_z)
    weights_x = spline_weights(main[6:7])
    weight = plane_rows(main[3:4], weights_x, rows)
    stack = jnp.concatenate([weight * main[c : c + 1] for c in range(3)], axis=0)
    if 3 * rows < LANES:
        stack = jnp.concatenate([stack, jnp.zeros((LANES - 3 * rows, count), F32)], axis=0)
    both = jnp.concatenate(split(stack), axis=0)
    parts = [split(value) for value in values]
    left = jnp.concatenate(
        [jnp.concatenate([p[i] for p in parts], axis=0) for i in range(2)], axis=1
    )
    right = jnp.concatenate([both, both], axis=1)
    acc = lax.dot_general(left, right, (((1,), (1,)), ((), ())), preferred_element_type=F32)
    total = (acc[:, :LANES] + acc[:, LANES:]).T
    out_ref[0] = total[: 3 * rows]


def keeps(points, modes_y):
    blocks_rows = 2 * (modes_y.shape[1] + KZ)
    return modes_y.shape[1] % 8 == 0 and lax.axis_size(("group", "dev")) * blocks_rows * (
        points.shape[2] // 9 * 8
    ) * 4 <= KEEP_BYTES


def spread(points, modes_y, modes_z, rows, keep):
    blocks, _, width = points.shape
    count = width // 9 * 8
    own_y = modes_y.shape[1]
    cols = 4 * own_y * KZ
    kept = 2 * (own_y + KZ)
    out_specs = [pl.BlockSpec((1, 3 * rows, cols), lambda i: (i, 0, 0))]
    out_shape = [jax.ShapeDtypeStruct((blocks, 3 * rows, cols), F32)]
    if keep:
        out_specs.append(pl.BlockSpec((1, kept, count), lambda i: (i, 0, 0)))
        out_shape.append(jax.ShapeDtypeStruct((blocks, kept, count), F32))
    return pl.pallas_call(
        functools.partial(spread_kernel, rows),
        grid=(blocks,),
        in_specs=[
            pl.BlockSpec((1, 8, width), lambda i: (i, 0, 0)),
            pl.BlockSpec(modes_y.shape, lambda i: (0, 0, 0)),
            pl.BlockSpec(modes_z.shape, lambda i: (0, 0, 0)),
        ],
        out_specs=out_specs,
        out_shape=out_shape,
        compiler_params=pltpu.CompilerParams(vmem_limit_bytes=SPREAD_LIMIT),
        cost_estimate=pl.CostEstimate(
            flops=blocks * count * cols * LANES * 14,
            bytes_accessed=blocks * (9 * count + 3 * rows * cols) * 4,
            transcendentals=0,
        ),
        name="spread",
    )(points, modes_y, modes_z)


def solve_kernel(planes, rows, parts, ids_ref, *refs):
    piece_refs = refs[:parts]
    forward_half_ref, forward_ref, back_half_ref, back_ref = refs[parts : parts + 4]
    waves_ref, out_ref, modes, stacked = refs[parts + 4 :]
    extra = 8
    out_ref[...] = jnp.zeros_like(out_ref)
    before = 0
    for piece_ref in piece_refs:

        @pl.loop(0, piece_ref.shape[0])
        def _(index):
            first = pl.multiple_of(first_plane(ids_ref[before + index], planes), 8)
            for c in range(3):
                out_ref[c, pl.ds(first, rows)] += piece_ref[index, c * rows : (c + 1) * rows]

        before += piece_ref.shape[0]
    for c in range(3):
        out_ref[c, 0:extra] += out_ref[c, NX : NX + extra]
    quarter = NX // 4
    lanes = waves_ref.shape[1]
    families = ((0, quarter // 2, 4, 0), (quarter, quarter // 2, 4, 2), (2 * quarter, quarter, 2, 1))

    def transform(table, value):
        high, low = split(value)
        size = value.shape[0]
        stacked[0:size] = high
        stacked[size : 2 * size] = high
        stacked[2 * size : 3 * size] = low
        return jnp.dot(table, stacked[0 : 3 * size], preferred_element_type=F32)

    @pl.loop(0, 3)
    def _(c):
        cuts = [out_ref[c, i * quarter : (i + 1) * quarter] for i in range(4)]
        first, second = cuts[0] + cuts[2], cuts[1] + cuts[3]
        modes[c, 0:quarter] = transform(forward_half_ref[0], first + second)
        modes[c, quarter : 2 * quarter] = transform(forward_half_ref[1], first - second)
        odd = jnp.concatenate([cuts[0] - cuts[2], cuts[1] - cuts[3]], axis=0)
        modes[c, 2 * quarter :] = transform(forward_ref[...], odd)

    wave_y = waves_ref[0:1]
    wave_z = waves_ref[1:2]
    mult = waves_ref[2:3]
    flat = wave_y * wave_y + wave_z * wave_z
    group = 8

    for base, count, stride, offset in families:

        @pl.loop(0, count // group)
        def _(index):
            row = pl.multiple_of(index * group, group)
            number = lax.broadcasted_iota(jnp.int32, (group, lanes), 0) + row
            number = (stride * number + offset).astype(F32)
            wave_x = number * (TWO_PI / NX)
            squared = wave_x * wave_x + flat
            anchor = squared == 0.0
            inverse = jnp.where(anchor, 0.0, 1.0 / jnp.where(anchor, 1.0, squared))
            factor = inverse * mult * jnp.where(number == 0.0, 1.0, 2.0)
            waves = (wave_x, wave_y, wave_z)

            def place(axis, state):
                first = pl.multiple_of(base + state[0] * count + row, group)
                tyz = 2 * state[1] + state[2]
                return axis, pl.ds(first, group), slice(tyz * lanes, (tyz + 1) * lanes)

            def flip(state, axis):
                return tuple(1 - t if i == axis else t for i, t in enumerate(state))

            states = [(a, b, d) for a in range(2) for b in range(2) for d in range(2)]
            values = {(c,) + state: modes[place(c, state)] for c in range(3) for state in states}
            divergence = {}
            for state in states:
                total = None
                for axis in range(3):
                    term = waves[axis] * values[(axis,) + flip(state, axis)]
                    if state[axis]:
                        term = -term
                    total = term if total is None else total + term
                divergence[state] = total * inverse
            for state in states:
                for axis in range(3):
                    term = waves[axis] * divergence[flip(state, axis)]
                    value = values[(axis,) + state]
                    value = value - term if state[axis] else value + term
                    modes[place(axis, state)] = value * factor

    @pl.loop(0, 3)
    def _(c):
        even = transform(back_half_ref[0], modes[c, 0:quarter])
        out_ref[c, 0:quarter] = even
        even = transform(back_half_ref[1], modes[c, quarter : 2 * quarter])
        first = out_ref[c, 0:quarter]
        out_ref[c, 0:quarter] = first + even
        out_ref[c, quarter : 2 * quarter] = first - even
        odd = transform(back_ref[...], modes[c, 2 * quarter :])
        even = out_ref[c, 0 : 2 * quarter]
        out_ref[c, 0 : 2 * quarter] = even + odd
        out_ref[c, 2 * quarter : NX] = even - odd
        out_ref[c, NX : NX + extra] = out_ref[c, 0:extra]


def solve(pieces, ids, waves, tables, planes, rows):
    full = pl.BlockSpec(memory_space=pltpu.VMEM)
    cols = pieces[0].shape[2]
    return pl.pallas_call(
        functools.partial(solve_kernel, planes, rows, len(pieces)),
        in_specs=[pl.BlockSpec(memory_space=pltpu.SMEM)] + [full] * (len(pieces) + 5),
        out_specs=full,
        out_shape=jax.ShapeDtypeStruct((3, NX + 8, cols), F32),
        scratch_shapes=[
            pltpu.VMEM((3, NX, cols), F32),
            pltpu.VMEM((3 * NX // 2, cols), BF16),
        ],
        compiler_params=pltpu.CompilerParams(vmem_limit_bytes=SOLVE_LIMIT),
        cost_estimate=pl.CostEstimate(
            flops=27 * NX // 2 * NX // 2 * cols,
            bytes_accessed=6 * NX * cols * 4,
            transcendentals=0,
        ),
        name="solve",
    )(ids, *pieces, *tables, waves)


def gather_kernel(planes, rows, before, kept, ids_ref, points_ref, *refs):
    basis_refs, (lines_ref, out_ref, plane) = refs[:-3], refs[-3:]
    step = pl.program_id(0)
    first = pl.multiple_of(first_plane(ids_ref[before + step], planes), 8)
    stack = jnp.concatenate([lines_ref[c, pl.ds(first, rows)] for c in range(3)], axis=0)
    if 3 * rows < LANES:
        stack = jnp.concatenate([stack, jnp.zeros((LANES - 3 * rows, lines_ref.shape[2]), F32)], axis=0)
    high, low = split(stack)
    plane[0:LANES] = high
    plane[LANES:] = low
    main, last = unpack(points_ref[0])
    count = main.shape[1]
    chunk = count // 4
    if kept:
        own_y = basis_refs[0].shape[1] // 2 - KZ
    else:
        modes_y, modes_z = [[ref[i] for i in range(7)] for ref in basis_refs]
    for index in range(4):
        at = slice(index * chunk, (index + 1) * chunk)
        if kept:
            rows_y = [basis_refs[0][0, i * own_y : (i + 1) * own_y, at] for i in range(2)]
            rows_z = [
                basis_refs[0][0, 2 * own_y + i * KZ : 2 * own_y + (i + 1) * KZ, at] for i in range(2)
            ]
        else:
            rows_y, rows_z = basis_rows(main[:, at], last[:, at], modes_y, modes_z)
        pairs = [split(value) for value in column_values(rows_y, rows_z)]
        highs = jnp.concatenate([p[0] for p in pairs], axis=0)
        lows = jnp.concatenate([p[1] for p in pairs], axis=0)
        result = jnp.dot(plane[...], highs, preferred_element_type=F32)
        small = jnp.dot(plane[0:LANES], lows, preferred_element_type=F32)
        result = result[:LANES] + result[LANES:] + small
        weight = plane_rows(main[3:4, at], spline_weights(main[6:7, at]), rows)
        out_ref[0, :, at] = jnp.concatenate(
            [
                jnp.sum(weight * result[c * rows : (c + 1) * rows], axis=0, keepdims=True)
                for c in range(3)
            ],
            axis=0,
        )


def gather(points, skip, blocks, before, ids, basis, lines, planes, rows):
    width = points.shape[2]
    count = width // 9 * 8
    cols = lines.shape[2]
    kept = len(basis) == 1
    if kept:
        basis_specs = [pl.BlockSpec((1,) + basis[0].shape[1:], lambda i: (i + skip, 0, 0))]
    else:
        basis_specs = [pl.BlockSpec(table.shape, lambda i: (0, 0, 0)) for table in basis]
    return pl.pallas_call(
        functools.partial(gather_kernel, planes, rows, before, kept),
        grid=(blocks,),
        in_specs=[
            pl.BlockSpec(memory_space=pltpu.SMEM),
            pl.BlockSpec((1, 8, width), lambda i: (i + skip, 0, 0)),
            *basis_specs,
            pl.BlockSpec(memory_space=pltpu.VMEM),
        ],
        out_specs=pl.BlockSpec((1, 3, count), lambda i: (i, 0, 0)),
        out_shape=jax.ShapeDtypeStruct((blocks, 3, count), F32),
        scratch_shapes=[pltpu.VMEM((2 * LANES, cols), BF16)],
        compiler_params=pltpu.CompilerParams(vmem_limit_bytes=GATHER_LIMIT),
        cost_estimate=pl.CostEstimate(
            flops=blocks * count * cols * LANES * 14,
            bytes_accessed=blocks * 12 * count * 4,
            transcendentals=0,
        ),
        name="interpolate",
    )(ids, points, *basis, lines)


def line_tables():
    def table(numbers, length):
        angle = (numbers[:, None] * np.arange(length)[None, :] % NX) * (2.0 * np.pi / NX)
        return np.concatenate([np.cos(angle), np.sin(angle)], axis=0)

    def stacked(value):
        high = value.astype(ml_dtypes.bfloat16)
        low = (value - high.astype(np.float64)).astype(ml_dtypes.bfloat16)
        return np.concatenate([high, low, high], axis=1)

    quarter = NX // 4
    even = [table(4 * np.arange(quarter // 2) + first, quarter) for first in (0, 2)]
    odd = table(2 * np.arange(quarter) + 1, 2 * quarter)
    return (
        np.stack([stacked(value) for value in even]),
        stacked(odd),
        np.stack([stacked(value.T) for value in even]),
        stacked(odd.T),
    )


def mode_table(numbers, length):
    angle = numbers * (2.0 * np.pi / length)
    rows = [numbers]
    for stencil in range(1, 4):
        rows += [np.cos(stencil * angle), np.sin(stencil * angle)]
    table = np.stack(rows, axis=1)[..., None].astype(np.float32)
    return np.broadcast_to(table, table.shape[:3] + (LANES,))


def far_tables(device, devices):
    own_y = (NY // 2) * (NZ // 2) // devices // KZ
    parts_z = NZ // 2 // KZ
    number_y = np.arange(NY // 2).reshape(-1, own_y).astype(np.float64)
    number_z = np.arange(NZ // 2).reshape(-1, KZ).astype(np.float64)
    mult_y = np.where(number_y == 0, 1.0, 2.0)
    mult_z = np.where(number_z == 0, 1.0, 2.0) / float(NX * NY * NZ)
    shape = (number_y.shape[0], parts_z, own_y, KZ)
    waves = [
        np.broadcast_to(number_y[:, None, :, None] * (TWO_PI / NY), shape),
        np.broadcast_to(number_z[None, :, None, :] * (TWO_PI / NZ), shape),
        mult_y[:, None, :, None] * mult_z[None, :, None, :],
    ]
    waves = np.stack([w.reshape(devices, own_y * KZ) for w in waves], axis=1)
    waves = np.concatenate([waves, np.zeros((devices, 5, own_y * KZ))], axis=1)

    def own(table, index):
        return lax.dynamic_index_in_dim(jnp.asarray(table, F32), index, 0, keepdims=False)

    return (
        own(mode_table(number_y, NY), device // parts_z),
        own(mode_table(number_z, NZ), device % parts_z),
        own(waves, device),
    )


def per_device(forces, stencil_start, fraction, tile_pairs, pair_count):
    groups = lax.axis_size("group")
    members = lax.axis_size("dev")
    devices = groups * members
    planes = NX // devices
    device = lax.axis_index("group") * members + lax.axis_index("dev")
    rows = max(8, planes) + 8
    first = first_plane(device, planes).reshape(1)
    own = pack(first, forces, stencil_start, fraction)

    def from_flipped(values, mask):
        pairs = [(i, i ^ mask) for i in range(devices)]
        return lax.ppermute(values, ("group", "dev"), pairs)

    near_masks = (4, 8, 12)
    parts = [own, jnp.concatenate([from_flipped(own, mask) for mask in near_masks], axis=0)]
    masks = [0, *near_masks]
    own_half = jnp.concatenate(parts, axis=0)
    last_bit = devices.bit_length() - 2
    bits = [1] + list(range(4, last_bit))
    for bit in bits:
        parts.append(from_flipped(own_half, 1 << bit))
        own_half = jnp.concatenate([own_half, parts[-1]], axis=0)
        masks = masks + [m ^ 1 << bit for m in masks]
    top = 1 << last_bit
    parts.append(from_flipped(own_half, 1))
    other = from_flipped(own_half, top)
    parts += [other, from_flipped(other, 1)]
    masks = np.array([m ^ flip for flip in (0, 1, top, top ^ 1) for m in masks], np.int32)
    ids = device ^ jnp.asarray(masks)
    modes_y, modes_z, waves = far_tables(device, devices)
    tables = [jnp.asarray(table) for table in line_tables()]
    keep = keeps(own, modes_y)
    spreads = [spread(points, modes_y, modes_z, rows, keep) for points in parts]
    pieces = [result[0] for result in spreads]
    lines = solve(pieces, ids, waves, tables, planes, rows)
    firsts = np.cumsum([0] + [points.shape[0] for points in parts])

    def sums(part, after, skip=0, blocks=None):
        basis = spreads[part][1:] if keep else [modes_y, modes_z]
        blocks = blocks or parts[part].shape[0]
        return gather(
            parts[part], skip, blocks, int(firsts[part]) + skip, after, basis, lines, planes, rows
        )

    def then(value):
        return lax.optimization_barrier((value, ids))

    count = len(parts)
    across, after = then(sums(count - 1, ids))
    across = sums(count - 2, after) + from_flipped(across, 1)
    across, after = then(across)
    across, beside = from_flipped(across, top), sums(count - 3, after)
    (across, beside), after = then((across, beside))
    beside = from_flipped(beside, 1)
    total = None
    for part in range(count - 4, 1, -1):
        given = sums(part, after)
        if total is None:
            (beside, given), after = then((beside, given))
            total = across + beside
        half = total.shape[0] // 2
        given = given + total[half:]
        if part == 2:
            given, after = then(given)
            far_pair = sums(1, after, 1, 2)
        given = from_flipped(given, 1 << bits[part - 2])
        if part == 2:
            (given, far_pair), after = then((given, far_pair))
        total = total[:half] + given
    far_pair, after = then(far_pair + total[2:])
    far_pair = from_flipped(far_pair, 8)
    last, far = sums(1, after, 0, 1), sums(0, after)
    (far_pair, last, far), after = then((far_pair, last, far))
    last = last + total[1:2] + far_pair[1:]
    far = far + total[:1] + far_pair[:1]
    forces, count_late, last = lax.optimization_barrier((forces, pair_count, last))
    near = near_field(forces, stencil_start, fraction, tile_pairs, count_late)
    return far[0] + from_flipped(last, 4)[0] + near


def solution(mesh):
    in_specs = (
        P(None, ("group", "dev")),
        P(None, ("group", "dev")),
        P(None, ("group", "dev")),
        P(("group", "dev"), None),
        P(("group", "dev")),
    )
    out_specs = P(None, ("group", "dev"))
    return jax.shard_map(
        per_device, mesh=mesh, in_specs=in_specs, out_specs=out_specs, check_vma=False
    )
```

```python
import functools

import jax
import jax.numpy as jnp
import ml_dtypes
import numpy as np
from jax import lax
from jax.experimental import pallas as pl
from jax.experimental.pallas import tpu as pltpu
from jax.sharding import PartitionSpec as P

NX = 1024
NY = 128
NZ = 128

TWO_PI = 6.283185307179586
EPS_SQ = 1.0
RANGE_SQ = 16.0
NEAR_SCALE = 0.25

LANES = 128
SPREAD_LIMIT = 24 * 2**20
SOLVE_LIMIT = 20 * 2**20
GATHER_LIMIT = 20 * 2**20
KEEP_BYTES = 32 * 2**20
KZ = 16
BF16 = jnp.bfloat16
F32 = jnp.float32


def wrapped(gap, length):
    gap = jnp.where(gap > length / 2, gap - length, gap)
    return jnp.where(gap < -length / 2, gap + length, gap)


def near_kernel(pairs_ref, count_ref, forces_ref, start_ref, fraction_ref, out_ref, columns):
    tiles = out_ref.shape[1] // LANES
    out_ref[...] = jnp.zeros_like(out_ref)

    @pl.loop(0, tiles)
    def _(tile):
        at = pl.ds(pl.multiple_of(tile * LANES, LANES), LANES)
        nine = jnp.concatenate(
            [start_ref[:, at].astype(F32), fraction_ref[:, at], forces_ref[:, at]], axis=0
        )
        for value in range(9):
            wide = jnp.broadcast_to(nine[value : value + 1], (LANES, LANES))
            columns[value, at] = wide.T

    @pl.loop(0, count_ref[0])
    def _(slot):
        target = pl.ds(pl.multiple_of(pairs_ref[2 * slot] * LANES, LANES), LANES)
        base = pl.multiple_of(pairs_ref[2 * slot + 1] * LANES, LANES)
        start = start_ref[:, target].astype(F32)
        fraction = fraction_ref[:, target]
        sums = [jnp.zeros((8, LANES), F32) for _ in range(3)]
        for row in range(0, LANES, 8):
            source = [columns[value, pl.ds(base + row, 8)] for value in range(9)]
            gaps = []
            for axis, length in enumerate((None, NY, NZ)):
                gap = start[axis : axis + 1] - source[axis]
                if length is not None:
                    gap = wrapped(gap, float(length))
                gaps.append(gap + (fraction[axis : axis + 1] - source[3 + axis]))
            pulled = source[6:9]
            distance = gaps[0] * gaps[0] + gaps[1] * gaps[1] + gaps[2] * gaps[2]
            inverse = lax.rsqrt(distance + EPS_SQ)
            fall = NEAR_SCALE * jnp.exp(distance * (-1.0 / RANGE_SQ)) * (inverse * inverse * inverse)
            diagonal = (distance + 2.0 * EPS_SQ) * fall
            along = fall * (gaps[0] * pulled[0] + gaps[1] * pulled[1] + gaps[2] * pulled[2])
            sums = [sums[i] + (diagonal * pulled[i] + gaps[i] * along) for i in range(3)]
        out_ref[:, target] += jnp.concatenate(
            [jnp.sum(value, axis=0, keepdims=True) for value in sums], axis=0
        )


def near_field(forces, stencil_start, fraction, tile_pairs, pair_count):
    smem = pl.BlockSpec(memory_space=pltpu.SMEM)
    vmem = pl.BlockSpec(memory_space=pltpu.VMEM)
    points = forces.shape[1]
    slots = tile_pairs.shape[0]
    return pl.pallas_call(
        near_kernel,
        in_specs=[smem, smem, vmem, vmem, vmem],
        out_specs=vmem,
        out_shape=jax.ShapeDtypeStruct((3, points), F32),
        scratch_shapes=[pltpu.VMEM((9, points, LANES), F32)],
        compiler_params=pltpu.CompilerParams(vmem_limit_bytes=16 * 2**20),
        cost_estimate=pl.CostEstimate(
            flops=slots * LANES * LANES * 6000, bytes_accessed=points * 48, transcendentals=0
        ),
        name="near",
    )(tile_pairs.reshape(-1), pair_count, forces, stencil_start, fraction)


def pack_kernel(first_ref, forces_ref, start_ref, fraction_ref, out_ref):
    points = forces_ref.shape[1]
    piece = points // 8
    start = start_ref[...]
    out_ref[0, 0:3, 0:points] = forces_ref[...]
    out_ref[0, 3:4, 0:points] = (start[0:1] - first_ref[0]).astype(F32)
    out_ref[0, 4:6, 0:points] = start[1:3].astype(F32)
    out_ref[0, 6:8, 0:points] = fraction_ref[0:2]
    for row in range(8):
        out_ref[0, row : row + 1, points:] = fraction_ref[2:3, row * piece : (row + 1) * piece]


def pack(first, forces, stencil_start, fraction):
    vmem = pl.BlockSpec(memory_space=pltpu.VMEM)
    points = forces.shape[1]
    return pl.pallas_call(
        pack_kernel,
        in_specs=[pl.BlockSpec(memory_space=pltpu.SMEM), vmem, vmem, vmem],
        out_specs=vmem,
        out_shape=jax.ShapeDtypeStruct((1, 8, points + points // 8), F32),
        name="pack",
    )(first, forces, stencil_start, fraction)


def unpack(values):
    points = values.shape[1] // 9 * 8
    pieces = [values[row : row + 1, points:] for row in range(8)]
    return values[:, :points], jnp.concatenate(pieces, axis=1)


def split(value):
    high = value.astype(BF16)
    low = (value - high.astype(F32)).astype(BF16)
    return high, low


def spline_weights(fraction):
    square = fraction * fraction
    cube = square * fraction
    rest = 1.0 - fraction
    return [
        rest * rest * rest * (1.0 / 6.0),
        (3.0 * cube - 6.0 * square + 4.0) * (1.0 / 6.0),
        (-3.0 * cube + 3.0 * square + 3.0 * fraction + 1.0) * (1.0 / 6.0),
        cube * (1.0 / 6.0),
    ]


def cos_sin_turns(turns):
    part = turns - jnp.floor(turns + 0.5)
    half = part * (0.5 * TWO_PI)
    square = half * half
    sine = half * (
        1.0
        + square
        * (
            -1.0 / 6.0
            + square
            * (1.0 / 120.0 + square * (-1.0 / 5040.0 + square * (1.0 / 362880.0 + square * (-1.0 / 39916800.0))))
        )
    )
    cosine = 1.0 + square * (
        -0.5
        + square
        * (
            1.0 / 24.0
            + square
            * (-1.0 / 720.0 + square * (1.0 / 40320.0 + square * (-1.0 / 3628800.0 + square * (1.0 / 479001600.0))))
        )
    )
    return 1.0 - 2.0 * sine * sine, 2.0 * sine * cosine


def widen(table, width):
    return jnp.concatenate([table] * (width // LANES), axis=1)


def mode_rows(start, weights, modes, length):
    width = start.shape[1]
    cosine, sine = cos_sin_turns(widen(modes[0], width) * start * (1.0 / length))
    sum_cos = weights[0] + weights[1] * widen(modes[1], width)
    sum_sin = weights[1] * widen(modes[2], width)
    sum_cos = sum_cos + weights[2] * widen(modes[3], width) + weights[3] * widen(modes[5], width)
    sum_sin = sum_sin + weights[2] * widen(modes[4], width) + weights[3] * widen(modes[6], width)
    return cosine * sum_cos - sine * sum_sin, sine * sum_cos + cosine * sum_sin


def basis_rows(main, last, modes_y, modes_z):
    weights_y = [w[1:2] for w in spline_weights(main[6:8])]
    rows_y = mode_rows(main[4:5], weights_y, modes_y, NY)
    rows_z = mode_rows(main[5:6], spline_weights(last), modes_z, NZ)
    return rows_y, rows_z


def column_values(rows_y, rows_z):
    values = []
    for ty in range(2):
        for tz in range(2):
            for iy in range(rows_y[0].shape[0]):
                values.append(rows_y[ty][iy : iy + 1] * rows_z[tz])
    return values


def plane_rows(start, weights, rows):
    iota = lax.broadcasted_iota(jnp.int32, (rows, start.shape[1]), 0).astype(F32)
    away = iota - start
    result = jnp.where(away == 0.0, weights[0], 0.0)
    for stencil in range(1, 4):
        result = jnp.where(away == float(stencil), weights[stencil], result)
    return result


def first_plane(block, planes):
    joined = max(1, 8 // planes)
    return lax.div(block, joined) * (joined * planes)


def spread_kernel(rows, points_ref, modes_y_ref, modes_z_ref, out_ref, *kept_refs):
    main, last = unpack(points_ref[0])
    count = main.shape[1]
    modes_y = [modes_y_ref[i] for i in range(7)]
    modes_z = [modes_z_ref[i] for i in range(7)]
    rows_y, rows_z = basis_rows(main, last, modes_y, modes_z)
    for kept_ref in kept_refs:
        kept_ref[0] = jnp.concatenate([*rows_y, *rows_z], axis=0)
    values = column_values(rows_y, rows_z)
    weights_x = spline_weights(main[6:7])
    weight = plane_rows(main[3:4], weights_x, rows)
    stack = jnp.concatenate([weight * main[c : c + 1] for c in range(3)], axis=0)
    if 3 * rows < LANES:
        stack = jnp.concatenate([stack, jnp.zeros((LANES - 3 * rows, count), F32)], axis=0)
    both = jnp.concatenate(split(stack), axis=0)
    parts = [split(value) for value in values]
    left = jnp.concatenate(
        [jnp.concatenate([p[i] for p in parts], axis=0) for i in range(2)], axis=1
    )
    right = jnp.concatenate([both, both], axis=1)
    acc = lax.dot_general(left, right, (((1,), (1,)), ((), ())), preferred_element_type=F32)
    total = (acc[:, :LANES] + acc[:, LANES:]).T
    out_ref[0] = total[: 3 * rows]


def keeps(points, modes_y):
    blocks_rows = 2 * (modes_y.shape[1] + KZ)
    return modes_y.shape[1] % 8 == 0 and lax.axis_size(("group", "dev")) * blocks_rows * (
        points.shape[2] // 9 * 8
    ) * 4 <= KEEP_BYTES


def spread(points, modes_y, modes_z, rows, keep):
    blocks, _, width = points.shape
    count = width // 9 * 8
    own_y = modes_y.shape[1]
    cols = 4 * own_y * KZ
    kept = 2 * (own_y + KZ)
    out_specs = [pl.BlockSpec((1, 3 * rows, cols), lambda i: (i, 0, 0))]
    out_shape = [jax.ShapeDtypeStruct((blocks, 3 * rows, cols), F32)]
    if keep:
        out_specs.append(pl.BlockSpec((1, kept, count), lambda i: (i, 0, 0)))
        out_shape.append(jax.ShapeDtypeStruct((blocks, kept, count), F32))
    return pl.pallas_call(
        functools.partial(spread_kernel, rows),
        grid=(blocks,),
        in_specs=[
            pl.BlockSpec((1, 8, width), lambda i: (i, 0, 0)),
            pl.BlockSpec(modes_y.shape, lambda i: (0, 0, 0)),
            pl.BlockSpec(modes_z.shape, lambda i: (0, 0, 0)),
        ],
        out_specs=out_specs,
        out_shape=out_shape,
        compiler_params=pltpu.CompilerParams(vmem_limit_bytes=SPREAD_LIMIT),
        cost_estimate=pl.CostEstimate(
            flops=blocks * count * cols * LANES * 14,
            bytes_accessed=blocks * (9 * count + 3 * rows * cols) * 4,
            transcendentals=0,
        ),
        name="spread",
    )(points, modes_y, modes_z)


def solve_kernel(planes, rows, parts, ids_ref, *refs):
    piece_refs = refs[:parts]
    forward_half_ref, forward_ref, back_half_ref, back_ref = refs[parts : parts + 4]
    waves_ref, out_ref, modes, stacked = refs[parts + 4 :]
    extra = 8
    out_ref[...] = jnp.zeros_like(out_ref)
    before = 0
    for piece_ref in piece_refs:

        @pl.loop(0, piece_ref.shape[0])
        def _(index):
            first = pl.multiple_of(first_plane(ids_ref[before + index], planes), 8)
            for c in range(3):
                out_ref[c, pl.ds(first, rows)] += piece_ref[index, c * rows : (c + 1) * rows]

        before += piece_ref.shape[0]
    for c in range(3):
        out_ref[c, 0:extra] += out_ref[c, NX : NX + extra]
    quarter = NX // 4
    lanes = waves_ref.shape[1]
    families = ((0, quarter // 2, 4, 0), (quarter, quarter // 2, 4, 2), (2 * quarter, quarter, 2, 1))

    def transform(table, value):
        high, low = split(value)
        size = value.shape[0]
        stacked[0:size] = high
        stacked[size : 2 * size] = high
        stacked[2 * size : 3 * size] = low
        return jnp.dot(table, stacked[0 : 3 * size], preferred_element_type=F32)

    @pl.loop(0, 3)
    def _(c):
        cuts = [out_ref[c, i * quarter : (i + 1) * quarter] for i in range(4)]
        first, second = cuts[0] + cuts[2], cuts[1] + cuts[3]
        modes[c, 0:quarter] = transform(forward_half_ref[0], first + second)
        modes[c, quarter : 2 * quarter] = transform(forward_half_ref[1], first - second)
        odd = jnp.concatenate([cuts[0] - cuts[2], cuts[1] - cuts[3]], axis=0)
        modes[c, 2 * quarter :] = transform(forward_ref[...], odd)

    wave_y = waves_ref[0:1]
    wave_z = waves_ref[1:2]
    mult = waves_ref[2:3]
    flat = wave_y * wave_y + wave_z * wave_z
    group = 8

    for base, count, stride, offset in families:

        @pl.loop(0, count // group)
        def _(index):
            row = pl.multiple_of(index * group, group)
            number = lax.broadcasted_iota(jnp.int32, (group, lanes), 0) + row
            number = (stride * number + offset).astype(F32)
            wave_x = number * (TWO_PI / NX)
            squared = wave_x * wave_x + flat
            anchor = squared == 0.0
            inverse = jnp.where(anchor, 0.0, 1.0 / jnp.where(anchor, 1.0, squared))
            factor = inverse * mult * jnp.where(number == 0.0, 1.0, 2.0)
            waves = (wave_x, wave_y, wave_z)

            def place(axis, state):
                first = pl.multiple_of(base + state[0] * count + row, group)
                tyz = 2 * state[1] + state[2]
                return axis, pl.ds(first, group), slice(tyz * lanes, (tyz + 1) * lanes)

            def flip(state, axis):
                return tuple(1 - t if i == axis else t for i, t in enumerate(state))

            states = [(a, b, d) for a in range(2) for b in range(2) for d in range(2)]
            values = {(c,) + state: modes[place(c, state)] for c in range(3) for state in states}
            divergence = {}
            for state in states:
                total = None
                for axis in range(3):
                    term = waves[axis] * values[(axis,) + flip(state, axis)]
                    if state[axis]:
                        term = -term
                    total = term if total is None else total + term
                divergence[state] = total * inverse
            for state in states:
                for axis in range(3):
                    term = waves[axis] * divergence[flip(state, axis)]
                    value = values[(axis,) + state]
                    value = value - term if state[axis] else value + term
                    modes[place(axis, state)] = value * factor

    @pl.loop(0, 3)
    def _(c):
        even = transform(back_half_ref[0], modes[c, 0:quarter])
        out_ref[c, 0:quarter] = even
        even = transform(back_half_ref[1], modes[c, quarter : 2 * quarter])
        first = out_ref[c, 0:quarter]
        out_ref[c, 0:quarter] = first + even
        out_ref[c, quarter : 2 * quarter] = first - even
        odd = transform(back_ref[...], modes[c, 2 * quarter :])
        even = out_ref[c, 0 : 2 * quarter]
        out_ref[c, 0 : 2 * quarter] = even + odd
        out_ref[c, 2 * quarter : NX] = even - odd
        out_ref[c, NX : NX + extra] = out_ref[c, 0:extra]


def solve(pieces, ids, waves, tables, planes, rows):
    full = pl.BlockSpec(memory_space=pltpu.VMEM)
    cols = pieces[0].shape[2]
    return pl.pallas_call(
        functools.partial(solve_kernel, planes, rows, len(pieces)),
        in_specs=[pl.BlockSpec(memory_space=pltpu.SMEM)] + [full] * (len(pieces) + 5),
        out_specs=full,
        out_shape=jax.ShapeDtypeStruct((3, NX + 8, cols), F32),
        scratch_shapes=[
            pltpu.VMEM((3, NX, cols), F32),
            pltpu.VMEM((3 * NX // 2, cols), BF16),
        ],
        compiler_params=pltpu.CompilerParams(vmem_limit_bytes=SOLVE_LIMIT),
        cost_estimate=pl.CostEstimate(
            flops=27 * NX // 2 * NX // 2 * cols,
            bytes_accessed=6 * NX * cols * 4,
            transcendentals=0,
        ),
        name="solve",
    )(ids, *pieces, *tables, waves)


def gather_kernel(planes, rows, before, kept, ids_ref, points_ref, *refs):
    basis_refs, (lines_ref, out_ref, plane) = refs[:-3], refs[-3:]
    step = pl.program_id(0)
    first = pl.multiple_of(first_plane(ids_ref[before + step], planes), 8)
    stack = jnp.concatenate([lines_ref[c, pl.ds(first, rows)] for c in range(3)], axis=0)
    if 3 * rows < LANES:
        stack = jnp.concatenate([stack, jnp.zeros((LANES - 3 * rows, lines_ref.shape[2]), F32)], axis=0)
    high, low = split(stack)
    plane[0:LANES] = high
    plane[LANES:] = low
    main, last = unpack(points_ref[0])
    count = main.shape[1]
    chunk = count // 2
    if kept:
        own_y = basis_refs[0].shape[1] // 2 - KZ
    else:
        modes_y, modes_z = [[ref[i] for i in range(7)] for ref in basis_refs]
    for index in range(2):
        at = slice(index * chunk, (index + 1) * chunk)
        if kept:
            rows_y = [basis_refs[0][0, i * own_y : (i + 1) * own_y, at] for i in range(2)]
            rows_z = [
                basis_refs[0][0, 2 * own_y + i * KZ : 2 * own_y + (i + 1) * KZ, at] for i in range(2)
            ]
        else:
            rows_y, rows_z = basis_rows(main[:, at], last[:, at], modes_y, modes_z)
        pairs = [split(value) for value in column_values(rows_y, rows_z)]
        highs = jnp.concatenate([p[0] for p in pairs], axis=0)
        lows = jnp.concatenate([p[1] for p in pairs], axis=0)
        result = jnp.dot(plane[...], highs, preferred_element_type=F32)
        small = jnp.dot(plane[0:LANES], lows, preferred_element_type=F32)
        result = result[:LANES] + result[LANES:] + small
        weight = plane_rows(main[3:4, at], spline_weights(main[6:7, at]), rows)
        out_ref[0, :, at] = jnp.concatenate(
            [
                jnp.sum(weight * result[c * rows : (c + 1) * rows], axis=0, keepdims=True)
                for c in range(3)
            ],
            axis=0,
        )


def gather(points, skip, blocks, before, ids, basis, lines, planes, rows):
    width = points.shape[2]
    count = width // 9 * 8
    cols = lines.shape[2]
    kept = len(basis) == 1
    if kept:
        basis_specs = [pl.BlockSpec((1,) + basis[0].shape[1:], lambda i: (i + skip, 0, 0))]
    else:
        basis_specs = [pl.BlockSpec(table.shape, lambda i: (0, 0, 0)) for table in basis]
    return pl.pallas_call(
        functools.partial(gather_kernel, planes, rows, before, kept),
        grid=(blocks,),
        in_specs=[
            pl.BlockSpec(memory_space=pltpu.SMEM),
            pl.BlockSpec((1, 8, width), lambda i: (i + skip, 0, 0)),
            *basis_specs,
            pl.BlockSpec(memory_space=pltpu.VMEM),
        ],
        out_specs=pl.BlockSpec((1, 3, count), lambda i: (i, 0, 0)),
        out_shape=jax.ShapeDtypeStruct((blocks, 3, count), F32),
        scratch_shapes=[pltpu.VMEM((2 * LANES, cols), BF16)],
        compiler_params=pltpu.CompilerParams(vmem_limit_bytes=GATHER_LIMIT),
        cost_estimate=pl.CostEstimate(
            flops=blocks * count * cols * LANES * 14,
            bytes_accessed=blocks * 12 * count * 4,
            transcendentals=0,
        ),
        name="interpolate",
    )(ids, points, *basis, lines)


def line_tables():
    def table(numbers, length):
        angle = (numbers[:, None] * np.arange(length)[None, :] % NX) * (2.0 * np.pi / NX)
        return np.concatenate([np.cos(angle), np.sin(angle)], axis=0)

    def stacked(value):
        high = value.astype(ml_dtypes.bfloat16)
        low = (value - high.astype(np.float64)).astype(ml_dtypes.bfloat16)
        return np.concatenate([high, low, high], axis=1)

    quarter = NX // 4
    even = [table(4 * np.arange(quarter // 2) + first, quarter) for first in (0, 2)]
    odd = table(2 * np.arange(quarter) + 1, 2 * quarter)
    return (
        np.stack([stacked(value) for value in even]),
        stacked(odd),
        np.stack([stacked(value.T) for value in even]),
        stacked(odd.T),
    )


def mode_table(numbers, length):
    angle = numbers * (2.0 * np.pi / length)
    rows = [numbers]
    for stencil in range(1, 4):
        rows += [np.cos(stencil * angle), np.sin(stencil * angle)]
    table = np.stack(rows, axis=1)[..., None].astype(np.float32)
    return np.broadcast_to(table, table.shape[:3] + (LANES,))


def far_tables(device, devices):
    own_y = (NY // 2) * (NZ // 2) // devices // KZ
    parts_z = NZ // 2 // KZ
    number_y = np.arange(NY // 2).reshape(-1, own_y).astype(np.float64)
    number_z = np.arange(NZ // 2).reshape(-1, KZ).astype(np.float64)
    mult_y = np.where(number_y == 0, 1.0, 2.0)
    mult_z = np.where(number_z == 0, 1.0, 2.0) / float(NX * NY * NZ)
    shape = (number_y.shape[0], parts_z, own_y, KZ)
    waves = [
        np.broadcast_to(number_y[:, None, :, None] * (TWO_PI / NY), shape),
        np.broadcast_to(number_z[None, :, None, :] * (TWO_PI / NZ), shape),
        mult_y[:, None, :, None] * mult_z[None, :, None, :],
    ]
    waves = np.stack([w.reshape(devices, own_y * KZ) for w in waves], axis=1)
    waves = np.concatenate([waves, np.zeros((devices, 5, own_y * KZ))], axis=1)

    def own(table, index):
        return lax.dynamic_index_in_dim(jnp.asarray(table, F32), index, 0, keepdims=False)

    return (
        own(mode_table(number_y, NY), device // parts_z),
        own(mode_table(number_z, NZ), device % parts_z),
        own(waves, device),
    )


def per_device(forces, stencil_start, fraction, tile_pairs, pair_count):
    groups = lax.axis_size("group")
    members = lax.axis_size("dev")
    devices = groups * members
    planes = NX // devices
    device = lax.axis_index("group") * members + lax.axis_index("dev")
    rows = max(8, planes) + 8
    first = first_plane(device, planes).reshape(1)
    own = pack(first, forces, stencil_start, fraction)

    def from_flipped(values, mask):
        pairs = [(i, i ^ mask) for i in range(devices)]
        return lax.ppermute(values, ("group", "dev"), pairs)

    near_masks = (4, 8, 12)
    parts = [own, jnp.concatenate([from_flipped(own, mask) for mask in near_masks], axis=0)]
    masks = [0, *near_masks]
    own_half = jnp.concatenate(parts, axis=0)
    last_bit = devices.bit_length() - 2
    bits = [1] + list(range(4, last_bit))
    for bit in bits:
        parts.append(from_flipped(own_half, 1 << bit))
        own_half = jnp.concatenate([own_half, parts[-1]], axis=0)
        masks = masks + [m ^ 1 << bit for m in masks]
    top = 1 << last_bit
    parts.append(from_flipped(own_half, 1))
    other = from_flipped(own_half, top)
    parts += [other, from_flipped(other, 1)]
    masks = np.array([m ^ flip for flip in (0, 1, top, top ^ 1) for m in masks], np.int32)
    ids = device ^ jnp.asarray(masks)
    modes_y, modes_z, waves = far_tables(device, devices)
    tables = [jnp.asarray(table) for table in line_tables()]
    keep = keeps(own, modes_y)
    spreads = []
    modes = modes_y
    for points in parts:
        result = spread(points, modes, modes_z, rows, keep)
        piece, modes = lax.optimization_barrier((result[0], modes_y))
        spreads.append([piece, *result[1:]])
    pieces = [result[0] for result in spreads]
    lines = solve(pieces, ids, waves, tables, planes, rows)
    firsts = np.cumsum([0] + [points.shape[0] for points in parts])

    def sums(part, after, skip=0, blocks=None):
        basis = spreads[part][1:] if keep else [modes_y, modes_z]
        blocks = blocks or parts[part].shape[0]
        return gather(
            parts[part], skip, blocks, int(firsts[part]) + skip, after, basis, lines, planes, rows
        )

    def then(value):
        return lax.optimization_barrier((value, ids))

    count = len(parts)
    across, after = then(sums(count - 1, ids))
    across = sums(count - 2, after) + from_flipped(across, 1)
    across, after = then(across)
    across, beside = from_flipped(across, top), sums(count - 3, after)
    (across, beside), after = then((across, beside))
    beside = from_flipped(beside, 1)
    total = None
    for part in range(count - 4, 1, -1):
        given = sums(part, after)
        if total is None:
            (beside, given), after = then((beside, given))
            total = across + beside
        half = total.shape[0] // 2
        given = given + total[half:]
        if part == 2:
            given, after = then(given)
            far_pair = sums(1, after, 1, 2)
        given = from_flipped(given, 1 << bits[part - 2])
        if part == 2:
            (given, far_pair), after = then((given, far_pair))
        total = total[:half] + given
    far_pair, after = then(far_pair + total[2:])
    far_pair = from_flipped(far_pair, 8)
    last, far = sums(1, after, 0, 1), sums(0, after)
    (far_pair, last, far), after = then((far_pair, last, far))
    last = last + total[1:2] + far_pair[1:]
    far = far + total[:1] + far_pair[:1]
    forces, count_late, last = lax.optimization_barrier((forces, pair_count, last))
    near = near_field(forces, stencil_start, fraction, tile_pairs, count_late)
    return far[0] + from_flipped(last, 4)[0] + near


def solution(mesh):
    in_specs = (
        P(None, ("group", "dev")),
        P(None, ("group", "dev")),
        P(None, ("group", "dev")),
        P(("group", "dev"), None),
        P(("group", "dev")),
    )
    out_specs = P(None, ("group", "dev"))
    return jax.shard_map(
        per_device, mesh=mesh, in_specs=in_specs, out_specs=out_specs, check_vma=False
    )
```

```python
import functools

import jax
import jax.numpy as jnp
import ml_dtypes
import numpy as np
from jax import lax
from jax.experimental import pallas as pl
from jax.experimental.pallas import tpu as pltpu
from jax.sharding import PartitionSpec as P

NX = 1024
NY = 128
NZ = 128

TWO_PI = 6.283185307179586
EPS_SQ = 1.0
RANGE_SQ = 16.0
NEAR_SCALE = 0.25

LANES = 128
SPREAD_LIMIT = 24 * 2**20
SOLVE_LIMIT = 15 * 2**20
GATHER_LIMIT = 20 * 2**20
WIDE_PART = 3
KEEP_BYTES = 32 * 2**20
KZ = 16
BF16 = jnp.bfloat16
F32 = jnp.float32


def wrapped(gap, length):
    gap = jnp.where(gap > length / 2, gap - length, gap)
    return jnp.where(gap < -length / 2, gap + length, gap)


def tile_rows(own_ref, tile, points):
    per = points // 8 // LANES
    at = pl.ds(pl.multiple_of(tile * LANES, LANES), LANES)
    last_at = pl.ds(pl.multiple_of(points + lax.rem(tile, per) * LANES, LANES), LANES)
    pieces = own_ref[0, :, last_at]
    here = lax.broadcasted_iota(jnp.int32, pieces.shape, 0) == lax.div(tile, per)
    return own_ref[0, :, at], jnp.sum(jnp.where(here, pieces, 0.0), axis=0, keepdims=True)


def near_kernel(pairs_ref, count_ref, own_ref, wide_ref, out_ref):
    points = out_ref.shape[1]
    out_ref[...] = jnp.zeros_like(out_ref)

    @pl.loop(0, count_ref[0])
    def _(slot):
        tile = pairs_ref[2 * slot]
        target = pl.ds(pl.multiple_of(tile * LANES, LANES), LANES)
        base = pl.multiple_of(pairs_ref[2 * slot + 1] * LANES, LANES)
        main, last = tile_rows(own_ref, tile, points)
        start = [main[3 + axis : 4 + axis] for axis in range(3)]
        fraction = [main[6:7], main[7:8], last]
        sums = [jnp.zeros((8, LANES), F32) for _ in range(3)]
        for row in range(0, LANES, 8):
            source = [wide_ref[value, pl.ds(base + row, 8)] for value in range(9)]
            gaps = []
            for axis, length in enumerate((None, NY, NZ)):
                gap = start[axis] - source[3 + axis]
                if length is not None:
                    gap = wrapped(gap, float(length))
                gaps.append(gap + (fraction[axis] - source[6 + axis]))
            pulled = source[0:3]
            distance = gaps[0] * gaps[0] + gaps[1] * gaps[1] + gaps[2] * gaps[2]
            inverse = lax.rsqrt(distance + EPS_SQ)
            fall = NEAR_SCALE * jnp.exp(distance * (-1.0 / RANGE_SQ)) * (inverse * inverse * inverse)
            diagonal = (distance + 2.0 * EPS_SQ) * fall
            along = fall * (gaps[0] * pulled[0] + gaps[1] * pulled[1] + gaps[2] * pulled[2])
            sums = [sums[i] + (diagonal * pulled[i] + gaps[i] * along) for i in range(3)]
        out_ref[:, target] += jnp.concatenate(
            [jnp.sum(value, axis=0, keepdims=True) for value in sums], axis=0
        )


def near_field(own, wide, tile_pairs, pair_count):
    smem = pl.BlockSpec(memory_space=pltpu.SMEM)
    vmem = pl.BlockSpec(memory_space=pltpu.VMEM)
    points = wide.shape[1]
    slots = tile_pairs.shape[0]
    return pl.pallas_call(
        near_kernel,
        in_specs=[smem, smem, vmem, vmem],
        out_specs=vmem,
        out_shape=jax.ShapeDtypeStruct((3, points), F32),
        compiler_params=pltpu.CompilerParams(vmem_limit_bytes=16 * 2**20),
        cost_estimate=pl.CostEstimate(
            flops=slots * LANES * LANES * 6000, bytes_accessed=points * 48, transcendentals=0
        ),
        name="near",
    )(tile_pairs.reshape(-1), pair_count, own, wide)


def pack_kernel(first_ref, forces_ref, start_ref, fraction_ref, out_ref):
    points = forces_ref.shape[1]
    piece = points // 8
    start = start_ref[...]
    out_ref[0, 0:3, 0:points] = forces_ref[...]
    out_ref[0, 3:4, 0:points] = (start[0:1] - first_ref[0]).astype(F32)
    out_ref[0, 4:6, 0:points] = start[1:3].astype(F32)
    out_ref[0, 6:8, 0:points] = fraction_ref[0:2]
    for row in range(8):
        out_ref[0, row : row + 1, points:] = fraction_ref[2:3, row * piece : (row + 1) * piece]


def pack(first, forces, stencil_start, fraction):
    vmem = pl.BlockSpec(memory_space=pltpu.VMEM)
    points = forces.shape[1]
    return pl.pallas_call(
        pack_kernel,
        in_specs=[pl.BlockSpec(memory_space=pltpu.SMEM), vmem, vmem, vmem],
        out_specs=vmem,
        out_shape=jax.ShapeDtypeStruct((1, 8, points + points // 8), F32),
        name="pack",
    )(first, forces, stencil_start, fraction)


def unpacked(width):
    return width // 9 * 8


def unpack(values):
    points = unpacked(values.shape[1])
    pieces = [values[row : row + 1, points:] for row in range(8)]
    return values[:, :points], jnp.concatenate(pieces, axis=1)


def split(value):
    high = value.astype(BF16)
    low = (value - high.astype(F32)).astype(BF16)
    return high, low


def spline_weights(fraction):
    square = fraction * fraction
    cube = square * fraction
    rest = 1.0 - fraction
    return [
        rest * rest * rest * (1.0 / 6.0),
        (3.0 * cube - 6.0 * square + 4.0) * (1.0 / 6.0),
        (-3.0 * cube + 3.0 * square + 3.0 * fraction + 1.0) * (1.0 / 6.0),
        cube * (1.0 / 6.0),
    ]


def cos_sin_turns(turns):
    part = turns - jnp.floor(turns + 0.5)
    half = part * (0.5 * TWO_PI)
    square = half * half
    sine = half * (
        1.0
        + square
        * (
            -1.0 / 6.0
            + square
            * (1.0 / 120.0 + square * (-1.0 / 5040.0 + square * (1.0 / 362880.0 + square * (-1.0 / 39916800.0))))
        )
    )
    cosine = 1.0 + square * (
        -0.5
        + square
        * (
            1.0 / 24.0
            + square
            * (-1.0 / 720.0 + square * (1.0 / 40320.0 + square * (-1.0 / 3628800.0 + square * (1.0 / 479001600.0))))
        )
    )
    return 1.0 - 2.0 * sine * sine, 2.0 * sine * cosine


def widen(table, width):
    return jnp.concatenate([table] * (width // LANES), axis=1)


def mode_rows(start, weights, modes, length):
    width = start.shape[1]
    cosine, sine = cos_sin_turns(widen(modes[0], width) * start * (1.0 / length))
    sum_cos = weights[0] + weights[1] * widen(modes[1], width)
    sum_sin = weights[1] * widen(modes[2], width)
    sum_cos = sum_cos + weights[2] * widen(modes[3], width) + weights[3] * widen(modes[5], width)
    sum_sin = sum_sin + weights[2] * widen(modes[4], width) + weights[3] * widen(modes[6], width)
    return cosine * sum_cos - sine * sum_sin, sine * sum_cos + cosine * sum_sin


def basis_rows(main, last, modes_y, modes_z):
    weights_y = [w[1:2] for w in spline_weights(main[6:8])]
    rows_y = mode_rows(main[4:5], weights_y, modes_y, NY)
    rows_z = mode_rows(main[5:6], spline_weights(last), modes_z, NZ)
    return rows_y, rows_z


def column_values(rows_y, rows_z):
    values = []
    for ty in range(2):
        for tz in range(2):
            for iy in range(rows_y[0].shape[0]):
                values.append(rows_y[ty][iy : iy + 1] * rows_z[tz])
    return values


def plane_rows(start, weights, rows):
    iota = lax.broadcasted_iota(jnp.int32, (rows, start.shape[1]), 0).astype(F32)
    away = iota - start
    result = jnp.where(away == 0.0, weights[0], 0.0)
    for stencil in range(1, 4):
        result = jnp.where(away == float(stencil), weights[stencil], result)
    return result


def first_plane(block, planes):
    joined = max(1, 8 // planes)
    return lax.div(block, joined) * (joined * planes)


def spread_kernel(rows, tiles, points_ref, modes_y_ref, modes_z_ref, *refs):
    if tiles:
        own_ref, out_ref, *kept_refs, wide_ref = refs
        last_tile = unpacked(own_ref.shape[2]) // LANES - 1
        for index in range(tiles):
            tile = jnp.minimum(pl.program_id(0) * tiles + index, last_tile)
            eight, ninth = tile_rows(own_ref, tile, unpacked(own_ref.shape[2]))
            nine = jnp.concatenate([eight, ninth], axis=0)
            for value in range(9):
                wide = jnp.broadcast_to(nine[value : value + 1], (LANES, LANES))
                wide_ref[value, index * LANES : (index + 1) * LANES] = wide.T
    else:
        out_ref, *kept_refs = refs
    main, last = unpack(points_ref[0])
    count = main.shape[1]
    modes_y = [modes_y_ref[i] for i in range(7)]
    modes_z = [modes_z_ref[i] for i in range(7)]
    rows_y, rows_z = basis_rows(main, last, modes_y, modes_z)
    for kept_ref in kept_refs:
        kept_ref[0] = jnp.concatenate([*rows_y, *rows_z], axis=0)
    values = column_values(rows_y, rows_z)
    weights_x = spline_weights(main[6:7])
    weight = plane_rows(main[3:4], weights_x, rows)
    stack = jnp.concatenate([weight * main[c : c + 1] for c in range(3)], axis=0)
    if 3 * rows < LANES:
        stack = jnp.concatenate([stack, jnp.zeros((LANES - 3 * rows, count), F32)], axis=0)
    both = jnp.concatenate(split(stack), axis=0)
    parts = [split(value) for value in values]
    left = jnp.concatenate(
        [jnp.concatenate([p[i] for p in parts], axis=0) for i in range(2)], axis=1
    )
    right = jnp.concatenate([both, both], axis=1)
    acc = lax.dot_general(left, right, (((1,), (1,)), ((), ())), preferred_element_type=F32)
    total = (acc[:, :LANES] + acc[:, LANES:]).T
    out_ref[0] = total[: 3 * rows]


def keeps(points, modes_y):
    blocks_rows = 2 * (modes_y.shape[1] + KZ)
    return modes_y.shape[1] % 8 == 0 and lax.axis_size(("group", "dev")) * blocks_rows * (
        points.shape[2] // 9 * 8
    ) * 4 <= KEEP_BYTES


def spread(points, modes_y, modes_z, rows, keep, own=None):
    blocks, _, width = points.shape
    count = width // 9 * 8
    own_y = modes_y.shape[1]
    cols = 4 * own_y * KZ
    kept = 2 * (own_y + KZ)
    out_specs = [pl.BlockSpec((1, 3 * rows, cols), lambda i: (i, 0, 0))]
    out_shape = [jax.ShapeDtypeStruct((blocks, 3 * rows, cols), F32)]
    if keep:
        out_specs.append(pl.BlockSpec((1, kept, count), lambda i: (i, 0, 0)))
        out_shape.append(jax.ShapeDtypeStruct((blocks, kept, count), F32))
    in_specs = [
        pl.BlockSpec((1, 8, width), lambda i: (i, 0, 0)),
        pl.BlockSpec(modes_y.shape, lambda i: (0, 0, 0)),
        pl.BlockSpec(modes_z.shape, lambda i: (0, 0, 0)),
    ]
    operands = [points, modes_y, modes_z]
    tiles = 0
    if own is not None:
        tiles = max(1, count // LANES // blocks)
        last = count // LANES // tiles - 1
        in_specs.append(pl.BlockSpec((1, 8, width), lambda i: (0, 0, 0)))
        operands.append(own)
        out_specs.append(
            pl.BlockSpec((9, tiles * LANES, LANES), lambda i: (0, jnp.minimum(i, last), 0))
        )
        out_shape.append(jax.ShapeDtypeStruct((9, count, LANES), F32))
    return pl.pallas_call(
        functools.partial(spread_kernel, rows, tiles),
        grid=(blocks,),
        in_specs=in_specs,
        out_specs=out_specs,
        out_shape=out_shape,
        compiler_params=pltpu.CompilerParams(vmem_limit_bytes=SPREAD_LIMIT),
        cost_estimate=pl.CostEstimate(
            flops=blocks * count * cols * LANES * 14,
            bytes_accessed=blocks * (9 * count + 3 * rows * cols) * 4,
            transcendentals=0,
        ),
        name="spread",
    )(*operands)


def solve_kernel(planes, rows, parts, ids_ref, *refs):
    piece_refs = refs[:parts]
    forward_half_ref, forward_ref, back_half_ref, back_ref = refs[parts : parts + 4]
    waves_ref, out_ref, modes, stacked = refs[parts + 4 :]
    extra = 8
    out_ref[...] = jnp.zeros_like(out_ref)
    before = 0
    for piece_ref in piece_refs:

        @pl.loop(0, piece_ref.shape[0])
        def _(index):
            first = pl.multiple_of(first_plane(ids_ref[before + index], planes), 8)
            for c in range(3):
                out_ref[c, pl.ds(first, rows)] += piece_ref[index, c * rows : (c + 1) * rows]

        before += piece_ref.shape[0]
    for c in range(3):
        out_ref[c, 0:extra] += out_ref[c, NX : NX + extra]
    quarter = NX // 4
    lanes = waves_ref.shape[1]
    families = ((0, quarter // 2, 4, 0), (quarter, quarter // 2, 4, 2), (2 * quarter, quarter, 2, 1))

    def transform(table, value):
        high, low = split(value)
        size = value.shape[0]
        stacked[0:size] = high
        stacked[size : 2 * size] = high
        stacked[2 * size : 3 * size] = low
        return jnp.dot(table, stacked[0 : 3 * size], preferred_element_type=F32)

    @pl.loop(0, 3)
    def _(c):
        cuts = [out_ref[c, i * quarter : (i + 1) * quarter] for i in range(4)]
        first, second = cuts[0] + cuts[2], cuts[1] + cuts[3]
        modes[c, 0:quarter] = transform(forward_half_ref[0], first + second)
        modes[c, quarter : 2 * quarter] = transform(forward_half_ref[1], first - second)
        odd = jnp.concatenate([cuts[0] - cuts[2], cuts[1] - cuts[3]], axis=0)
        modes[c, 2 * quarter :] = transform(forward_ref[...], odd)

    wave_y = waves_ref[0:1]
    wave_z = waves_ref[1:2]
    mult = waves_ref[2:3]
    flat = wave_y * wave_y + wave_z * wave_z
    group = 8

    for base, count, stride, offset in families:

        @pl.loop(0, count // group)
        def _(index):
            row = pl.multiple_of(index * group, group)
            number = lax.broadcasted_iota(jnp.int32, (group, lanes), 0) + row
            number = (stride * number + offset).astype(F32)
            wave_x = number * (TWO_PI / NX)
            squared = wave_x * wave_x + flat
            anchor = squared == 0.0
            inverse = jnp.where(anchor, 0.0, 1.0 / jnp.where(anchor, 1.0, squared))
            factor = inverse * mult * jnp.where(number == 0.0, 1.0, 2.0)
            waves = (wave_x, wave_y, wave_z)

            def place(axis, state):
                first = pl.multiple_of(base + state[0] * count + row, group)
                tyz = 2 * state[1] + state[2]
                return axis, pl.ds(first, group), slice(tyz * lanes, (tyz + 1) * lanes)

            def flip(state, axis):
                return tuple(1 - t if i == axis else t for i, t in enumerate(state))

            states = [(a, b, d) for a in range(2) for b in range(2) for d in range(2)]
            values = {(c,) + state: modes[place(c, state)] for c in range(3) for state in states}
            divergence = {}
            for state in states:
                total = None
                for axis in range(3):
                    term = waves[axis] * values[(axis,) + flip(state, axis)]
                    if state[axis]:
                        term = -term
                    total = term if total is None else total + term
                divergence[state] = total * inverse
            for state in states:
                for axis in range(3):
                    term = waves[axis] * divergence[flip(state, axis)]
                    value = values[(axis,) + state]
                    value = value - term if state[axis] else value + term
                    modes[place(axis, state)] = value * factor

    @pl.loop(0, 3)
    def _(c):
        even = transform(back_half_ref[0], modes[c, 0:quarter])
        out_ref[c, 0:quarter] = even
        even = transform(back_half_ref[1], modes[c, quarter : 2 * quarter])
        first = out_ref[c, 0:quarter]
        out_ref[c, 0:quarter] = first + even
        out_ref[c, quarter : 2 * quarter] = first - even
        odd = transform(back_ref[...], modes[c, 2 * quarter :])
        even = out_ref[c, 0 : 2 * quarter]
        out_ref[c, 0 : 2 * quarter] = even + odd
        out_ref[c, 2 * quarter : NX] = even - odd
        out_ref[c, NX : NX + extra] = out_ref[c, 0:extra]


def solve(pieces, ids, waves, tables, planes, rows):
    full = pl.BlockSpec(memory_space=pltpu.VMEM)
    cols = pieces[0].shape[2]
    return pl.pallas_call(
        functools.partial(solve_kernel, planes, rows, len(pieces)),
        in_specs=[pl.BlockSpec(memory_space=pltpu.SMEM)] + [full] * (len(pieces) + 5),
        out_specs=full,
        out_shape=jax.ShapeDtypeStruct((3, NX + 8, cols), F32),
        scratch_shapes=[
            pltpu.VMEM((3, NX, cols), F32),
            pltpu.VMEM((3 * NX // 2, cols), BF16),
        ],
        compiler_params=pltpu.CompilerParams(vmem_limit_bytes=SOLVE_LIMIT),
        cost_estimate=pl.CostEstimate(
            flops=27 * NX // 2 * NX // 2 * cols,
            bytes_accessed=6 * NX * cols * 4,
            transcendentals=0,
        ),
        name="solve",
    )(ids, *pieces, *tables, waves)


def gather_kernel(planes, rows, before, kept, ids_ref, points_ref, *refs):
    basis_refs, (lines_ref, out_ref, plane) = refs[:-3], refs[-3:]
    step = pl.program_id(0)
    first = pl.multiple_of(first_plane(ids_ref[before + step], planes), 8)
    stack = jnp.concatenate([lines_ref[c, pl.ds(first, rows)] for c in range(3)], axis=0)
    if 3 * rows < LANES:
        stack = jnp.concatenate([stack, jnp.zeros((LANES - 3 * rows, lines_ref.shape[2]), F32)], axis=0)
    high, low = split(stack)
    plane[0:LANES] = high
    plane[LANES:] = low
    main, last = unpack(points_ref[0])
    count = main.shape[1]
    chunk = count // 2
    if kept:
        own_y = basis_refs[0].shape[1] // 2 - KZ
    else:
        modes_y, modes_z = [[ref[i] for i in range(7)] for ref in basis_refs]
    for index in range(2):
        at = slice(index * chunk, (index + 1) * chunk)
        if kept:
            rows_y = [basis_refs[0][0, i * own_y : (i + 1) * own_y, at] for i in range(2)]
            rows_z = [
                basis_refs[0][0, 2 * own_y + i * KZ : 2 * own_y + (i + 1) * KZ, at] for i in range(2)
            ]
        else:
            rows_y, rows_z = basis_rows(main[:, at], last[:, at], modes_y, modes_z)
        pairs = [split(value) for value in column_values(rows_y, rows_z)]
        highs = jnp.concatenate([p[0] for p in pairs], axis=0)
        lows = jnp.concatenate([p[1] for p in pairs], axis=0)
        result = jnp.dot(plane[...], highs, preferred_element_type=F32)
        small = jnp.dot(plane[0:LANES], lows, preferred_element_type=F32)
        result = result[:LANES] + result[LANES:] + small
        weight = plane_rows(main[3:4, at], spline_weights(main[6:7, at]), rows)
        out_ref[0, :, at] = jnp.concatenate(
            [
                jnp.sum(weight * result[c * rows : (c + 1) * rows], axis=0, keepdims=True)
                for c in range(3)
            ],
            axis=0,
        )


def gather(points, skip, blocks, before, ids, basis, lines, planes, rows):
    width = points.shape[2]
    count = width // 9 * 8
    cols = lines.shape[2]
    kept = len(basis) == 1
    if kept:
        basis_specs = [pl.BlockSpec((1,) + basis[0].shape[1:], lambda i: (i + skip, 0, 0))]
    else:
        basis_specs = [pl.BlockSpec(table.shape, lambda i: (0, 0, 0)) for table in basis]
    return pl.pallas_call(
        functools.partial(gather_kernel, planes, rows, before, kept),
        grid=(blocks,),
        in_specs=[
            pl.BlockSpec(memory_space=pltpu.SMEM),
            pl.BlockSpec((1, 8, width), lambda i: (i + skip, 0, 0)),
            *basis_specs,
            pl.BlockSpec(memory_space=pltpu.VMEM),
        ],
        out_specs=pl.BlockSpec((1, 3, count), lambda i: (i, 0, 0)),
        out_shape=jax.ShapeDtypeStruct((blocks, 3, count), F32),
        scratch_shapes=[pltpu.VMEM((2 * LANES, cols), BF16)],
        compiler_params=pltpu.CompilerParams(vmem_limit_bytes=GATHER_LIMIT),
        cost_estimate=pl.CostEstimate(
            flops=blocks * count * cols * LANES * 14,
            bytes_accessed=blocks * 12 * count * 4,
            transcendentals=0,
        ),
        name="interpolate",
    )(ids, points, *basis, lines)


def line_tables():
    def table(numbers, length):
        angle = (numbers[:, None] * np.arange(length)[None, :] % NX) * (2.0 * np.pi / NX)
        return np.concatenate([np.cos(angle), np.sin(angle)], axis=0)

    def stacked(value):
        high = value.astype(ml_dtypes.bfloat16)
        low = (value - high.astype(np.float64)).astype(ml_dtypes.bfloat16)
        return np.concatenate([high, low, high], axis=1)

    quarter = NX // 4
    even = [table(4 * np.arange(quarter // 2) + first, quarter) for first in (0, 2)]
    odd = table(2 * np.arange(quarter) + 1, 2 * quarter)
    return (
        np.stack([stacked(value) for value in even]),
        stacked(odd),
        np.stack([stacked(value.T) for value in even]),
        stacked(odd.T),
    )


def mode_table(numbers, length):
    angle = numbers * (2.0 * np.pi / length)
    rows = [numbers]
    for stencil in range(1, 4):
        rows += [np.cos(stencil * angle), np.sin(stencil * angle)]
    table = np.stack(rows, axis=1)[..., None].astype(np.float32)
    return np.broadcast_to(table, table.shape[:3] + (LANES,))


def far_tables(device, devices):
    own_y = (NY // 2) * (NZ // 2) // devices // KZ
    parts_z = NZ // 2 // KZ
    number_y = np.arange(NY // 2).reshape(-1, own_y).astype(np.float64)
    number_z = np.arange(NZ // 2).reshape(-1, KZ).astype(np.float64)
    mult_y = np.where(number_y == 0, 1.0, 2.0)
    mult_z = np.where(number_z == 0, 1.0, 2.0) / float(NX * NY * NZ)
    shape = (number_y.shape[0], parts_z, own_y, KZ)
    waves = [
        np.broadcast_to(number_y[:, None, :, None] * (TWO_PI / NY), shape),
        np.broadcast_to(number_z[None, :, None, :] * (TWO_PI / NZ), shape),
        mult_y[:, None, :, None] * mult_z[None, :, None, :],
    ]
    waves = np.stack([w.reshape(devices, own_y * KZ) for w in waves], axis=1)
    waves = np.concatenate([waves, np.zeros((devices, 5, own_y * KZ))], axis=1)

    def own(table, index):
        return lax.dynamic_index_in_dim(jnp.asarray(table, F32), index, 0, keepdims=False)

    return (
        own(mode_table(number_y, NY), device // parts_z),
        own(mode_table(number_z, NZ), device % parts_z),
        own(waves, device),
    )


def per_device(forces, stencil_start, fraction, tile_pairs, pair_count):
    groups = lax.axis_size("group")
    members = lax.axis_size("dev")
    devices = groups * members
    planes = NX // devices
    device = lax.axis_index("group") * members + lax.axis_index("dev")
    rows = max(8, planes) + 8
    first = first_plane(device, planes).reshape(1)
    own = pack(first, forces, stencil_start, fraction)

    def from_flipped(values, mask):
        pairs = [(i, i ^ mask) for i in range(devices)]
        return lax.ppermute(values, ("group", "dev"), pairs)

    near_masks = (4, 8, 12)
    parts = [own, jnp.concatenate([from_flipped(own, mask) for mask in near_masks], axis=0)]
    masks = [0, *near_masks]
    own_half = jnp.concatenate(parts, axis=0)
    last_bit = devices.bit_length() - 2
    bits = [1] + list(range(4, last_bit))
    for bit in bits:
        parts.append(from_flipped(own_half, 1 << bit))
        own_half = jnp.concatenate([own_half, parts[-1]], axis=0)
        masks = masks + [m ^ 1 << bit for m in masks]
    top = 1 << last_bit
    parts.append(from_flipped(own_half, 1))
    other = from_flipped(own_half, top)
    parts += [other, from_flipped(other, 1)]
    masks = np.array([m ^ flip for flip in (0, 1, top, top ^ 1) for m in masks], np.int32)
    ids = device ^ jnp.asarray(masks)
    modes_y, modes_z, waves = far_tables(device, devices)
    tables = [jnp.asarray(table) for table in line_tables()]
    keep = keeps(own, modes_y)
    spreads = []
    modes = modes_y
    for part, points in enumerate(parts):
        wide_own = own if part == len(parts) - WIDE_PART else None
        result = spread(points, modes, modes_z, rows, keep, wide_own)
        if wide_own is not None:
            *result, wide = result
        piece, modes = lax.optimization_barrier((result[0], modes_y))
        spreads.append([piece, *result[1:]])
    pieces = [result[0] for result in spreads]
    lines = solve(pieces, ids, waves, tables, planes, rows)
    firsts = np.cumsum([0] + [points.shape[0] for points in parts])

    def sums(part, after, skip=0, blocks=None):
        basis = spreads[part][1:] if keep else [modes_y, modes_z]
        blocks = blocks or parts[part].shape[0]
        return gather(
            parts[part], skip, blocks, int(firsts[part]) + skip, after, basis, lines, planes, rows
        )

    def then(value):
        return lax.optimization_barrier((value, ids))

    count = len(parts)
    across, after = then(sums(count - 1, ids))
    across = sums(count - 2, after) + from_flipped(across, 1)
    across, after = then(across)
    across, beside = from_flipped(across, top), sums(count - 3, after)
    (across, beside), after = then((across, beside))
    beside = from_flipped(beside, 1)
    total = None
    for part in range(count - 4, 1, -1):
        given = sums(part, after)
        if total is None:
            (beside, given), after = then((beside, given))
            total = across + beside
        half = total.shape[0] // 2
        given = given + total[half:]
        if part == 2:
            given, after = then(given)
            far_pair = sums(1, after, 1, 2)
        given = from_flipped(given, 1 << bits[part - 2])
        if part == 2:
            (given, far_pair), after = then((given, far_pair))
        total = total[:half] + given
    far_pair, after = then(far_pair + total[2:])
    far_pair = from_flipped(far_pair, 8)
    last, far = sums(1, after, 0, 1), sums(0, after)
    (far_pair, last, far), after = then((far_pair, last, far))
    last = last + total[1:2] + far_pair[1:]
    far = far + total[:1] + far_pair[:1]
    count_late, last = lax.optimization_barrier((pair_count, last))
    near = near_field(own, wide, tile_pairs, count_late)
    return far[0] + from_flipped(last, 4)[0] + near


def solution(mesh):
    in_specs = (
        P(None, ("group", "dev")),
        P(None, ("group", "dev")),
        P(None, ("group", "dev")),
        P(("group", "dev"), None),
        P(("group", "dev")),
    )
    out_specs = P(None, ("group", "dev"))
    return jax.shard_map(
        per_device, mesh=mesh, in_specs=in_specs, out_specs=out_specs, check_vma=False
    )
```

```python
import functools

import jax
import jax.numpy as jnp
import ml_dtypes
import numpy as np
from jax import lax
from jax.experimental import pallas as pl
from jax.experimental.pallas import tpu as pltpu
from jax.sharding import PartitionSpec as P

NX = 1024
NY = 128
NZ = 128

TWO_PI = 6.283185307179586
EPS_SQ = 1.0
RANGE_SQ = 16.0
NEAR_SCALE = 0.25

LANES = 128
SPREAD_LIMIT = 16 * 2**20
SOLVE_LIMIT = 8 * 2**20
GATHER_LIMIT = 12 * 2**20
WIDE_PART = 3
KEEP_BYTES = 32 * 2**20
KZ = 16
BF16 = jnp.bfloat16
F32 = jnp.float32


def wrapped(gap, length):
    gap = jnp.where(gap > length / 2, gap - length, gap)
    return jnp.where(gap < -length / 2, gap + length, gap)


def tile_rows(own_ref, tile, points):
    per = points // 8 // LANES
    at = pl.ds(pl.multiple_of(tile * LANES, LANES), LANES)
    last_at = pl.ds(pl.multiple_of(points + lax.rem(tile, per) * LANES, LANES), LANES)
    pieces = own_ref[0, :, last_at]
    here = lax.broadcasted_iota(jnp.int32, pieces.shape, 0) == lax.div(tile, per)
    return own_ref[0, :, at], jnp.sum(jnp.where(here, pieces, 0.0), axis=0, keepdims=True)


def near_kernel(pairs_ref, count_ref, own_ref, wide_ref, out_ref):
    points = out_ref.shape[1]
    out_ref[...] = jnp.zeros_like(out_ref)

    @pl.loop(0, count_ref[0])
    def _(slot):
        tile = pairs_ref[2 * slot]
        target = pl.ds(pl.multiple_of(tile * LANES, LANES), LANES)
        base = pl.multiple_of(pairs_ref[2 * slot + 1] * LANES, LANES)
        main, last = tile_rows(own_ref, tile, points)
        start = [main[3 + axis : 4 + axis] for axis in range(3)]
        fraction = [main[6:7], main[7:8], last]
        sums = [jnp.zeros((8, LANES), F32) for _ in range(3)]
        for row in range(0, LANES, 8):
            source = [wide_ref[value, pl.ds(base + row, 8)] for value in range(9)]
            gaps = []
            for axis, length in enumerate((None, NY, NZ)):
                gap = start[axis] - source[3 + axis]
                if length is not None:
                    gap = wrapped(gap, float(length))
                gaps.append(gap + (fraction[axis] - source[6 + axis]))
            pulled = source[0:3]
            distance = gaps[0] * gaps[0] + gaps[1] * gaps[1] + gaps[2] * gaps[2]
            inverse = lax.rsqrt(distance + EPS_SQ)
            fall = NEAR_SCALE * jnp.exp(distance * (-1.0 / RANGE_SQ)) * (inverse * inverse * inverse)
            diagonal = (distance + 2.0 * EPS_SQ) * fall
            along = fall * (gaps[0] * pulled[0] + gaps[1] * pulled[1] + gaps[2] * pulled[2])
            sums = [sums[i] + (diagonal * pulled[i] + gaps[i] * along) for i in range(3)]
        out_ref[:, target] += jnp.concatenate(
            [jnp.sum(value, axis=0, keepdims=True) for value in sums], axis=0
        )


def near_field(own, wide, tile_pairs, pair_count):
    smem = pl.BlockSpec(memory_space=pltpu.SMEM)
    vmem = pl.BlockSpec(memory_space=pltpu.VMEM)
    points = wide.shape[1]
    slots = tile_pairs.shape[0]
    return pl.pallas_call(
        near_kernel,
        in_specs=[smem, smem, vmem, vmem],
        out_specs=vmem,
        out_shape=jax.ShapeDtypeStruct((3, points), F32),
        compiler_params=pltpu.CompilerParams(vmem_limit_bytes=16 * 2**20),
        cost_estimate=pl.CostEstimate(
            flops=slots * LANES * LANES * 6000, bytes_accessed=points * 48, transcendentals=0
        ),
        name="near",
    )(tile_pairs.reshape(-1), pair_count, own, wide)


def pack_kernel(first_ref, forces_ref, start_ref, fraction_ref, out_ref):
    points = forces_ref.shape[1]
    piece = points // 8
    start = start_ref[...]
    out_ref[0, 0:3, 0:points] = forces_ref[...]
    out_ref[0, 3:4, 0:points] = (start[0:1] - first_ref[0]).astype(F32)
    out_ref[0, 4:6, 0:points] = start[1:3].astype(F32)
    out_ref[0, 6:8, 0:points] = fraction_ref[0:2]
    for row in range(8):
        out_ref[0, row : row + 1, points:] = fraction_ref[2:3, row * piece : (row + 1) * piece]


def pack(first, forces, stencil_start, fraction):
    vmem = pl.BlockSpec(memory_space=pltpu.VMEM)
    points = forces.shape[1]
    return pl.pallas_call(
        pack_kernel,
        in_specs=[pl.BlockSpec(memory_space=pltpu.SMEM), vmem, vmem, vmem],
        out_specs=vmem,
        out_shape=jax.ShapeDtypeStruct((1, 8, points + points // 8), F32),
        name="pack",
    )(first, forces, stencil_start, fraction)


def unpacked(width):
    return width // 9 * 8


def unpack(values):
    points = unpacked(values.shape[1])
    pieces = [values[row : row + 1, points:] for row in range(8)]
    return values[:, :points], jnp.concatenate(pieces, axis=1)


def split(value):
    high = value.astype(BF16)
    low = (value - high.astype(F32)).astype(BF16)
    return high, low


def spline_weights(fraction):
    square = fraction * fraction
    cube = square * fraction
    rest = 1.0 - fraction
    return [
        rest * rest * rest * (1.0 / 6.0),
        (3.0 * cube - 6.0 * square + 4.0) * (1.0 / 6.0),
        (-3.0 * cube + 3.0 * square + 3.0 * fraction + 1.0) * (1.0 / 6.0),
        cube * (1.0 / 6.0),
    ]


def cos_sin_turns(turns):
    part = turns - jnp.floor(turns + 0.5)
    half = part * (0.5 * TWO_PI)
    square = half * half
    sine = half * (
        1.0
        + square
        * (
            -1.0 / 6.0
            + square
            * (1.0 / 120.0 + square * (-1.0 / 5040.0 + square * (1.0 / 362880.0 + square * (-1.0 / 39916800.0))))
        )
    )
    cosine = 1.0 + square * (
        -0.5
        + square
        * (
            1.0 / 24.0
            + square
            * (-1.0 / 720.0 + square * (1.0 / 40320.0 + square * (-1.0 / 3628800.0 + square * (1.0 / 479001600.0))))
        )
    )
    return 1.0 - 2.0 * sine * sine, 2.0 * sine * cosine


def widen(table, width):
    return jnp.concatenate([table] * (width // LANES), axis=1)


def mode_rows(start, weights, modes, length):
    width = start.shape[1]
    cosine, sine = cos_sin_turns(widen(modes[0], width) * start * (1.0 / length))
    sum_cos = weights[0] + weights[1] * widen(modes[1], width)
    sum_sin = weights[1] * widen(modes[2], width)
    sum_cos = sum_cos + weights[2] * widen(modes[3], width) + weights[3] * widen(modes[5], width)
    sum_sin = sum_sin + weights[2] * widen(modes[4], width) + weights[3] * widen(modes[6], width)
    return cosine * sum_cos - sine * sum_sin, sine * sum_cos + cosine * sum_sin


def basis_rows(main, last, modes_y, modes_z):
    weights_y = [w[1:2] for w in spline_weights(main[6:8])]
    rows_y = mode_rows(main[4:5], weights_y, modes_y, NY)
    rows_z = mode_rows(main[5:6], spline_weights(last), modes_z, NZ)
    return rows_y, rows_z


def column_values(rows_y, rows_z):
    values = []
    for ty in range(2):
        for tz in range(2):
            for iy in range(rows_y[0].shape[0]):
                values.append(rows_y[ty][iy : iy + 1] * rows_z[tz])
    return values


def plane_rows(start, weights, rows):
    iota = lax.broadcasted_iota(jnp.int32, (rows, start.shape[1]), 0).astype(F32)
    away = iota - start
    result = jnp.where(away == 0.0, weights[0], 0.0)
    for stencil in range(1, 4):
        result = jnp.where(away == float(stencil), weights[stencil], result)
    return result


def first_plane(block, planes):
    joined = max(1, 8 // planes)
    return lax.div(block, joined) * (joined * planes)


def spread_kernel(rows, tiles, points_ref, modes_y_ref, modes_z_ref, *refs):
    if tiles:
        own_ref, out_ref, *kept_refs, wide_ref = refs
        last_tile = unpacked(own_ref.shape[2]) // LANES - 1
        for index in range(tiles):
            tile = jnp.minimum(pl.program_id(0) * tiles + index, last_tile)
            eight, ninth = tile_rows(own_ref, tile, unpacked(own_ref.shape[2]))
            nine = jnp.concatenate([eight, ninth], axis=0)
            for value in range(9):
                wide = jnp.broadcast_to(nine[value : value + 1], (LANES, LANES))
                wide_ref[value, index * LANES : (index + 1) * LANES] = wide.T
    else:
        out_ref, *kept_refs = refs
    main, last = unpack(points_ref[0])
    count = main.shape[1]
    modes_y = [modes_y_ref[i] for i in range(7)]
    modes_z = [modes_z_ref[i] for i in range(7)]
    rows_y, rows_z = basis_rows(main, last, modes_y, modes_z)
    for kept_ref in kept_refs:
        kept_ref[0] = jnp.concatenate([*rows_y, *rows_z], axis=0)
    values = column_values(rows_y, rows_z)
    weights_x = spline_weights(main[6:7])
    weight = plane_rows(main[3:4], weights_x, rows)
    stack = jnp.concatenate([weight * main[c : c + 1] for c in range(3)], axis=0)
    if 3 * rows < LANES:
        stack = jnp.concatenate([stack, jnp.zeros((LANES - 3 * rows, count), F32)], axis=0)
    both = jnp.concatenate(split(stack), axis=0)
    parts = [split(value) for value in values]
    left = jnp.concatenate(
        [jnp.concatenate([p[i] for p in parts], axis=0) for i in range(2)], axis=1
    )
    right = jnp.concatenate([both, both], axis=1)
    acc = lax.dot_general(left, right, (((1,), (1,)), ((), ())), preferred_element_type=F32)
    total = (acc[:, :LANES] + acc[:, LANES:]).T
    out_ref[0] = total[: 3 * rows]


def keeps(points, modes_y):
    blocks_rows = 2 * (modes_y.shape[1] + KZ)
    return modes_y.shape[1] % 8 == 0 and lax.axis_size(("group", "dev")) * blocks_rows * (
        points.shape[2] // 9 * 8
    ) * 4 <= KEEP_BYTES


def spread(points, modes_y, modes_z, rows, keep, own=None):
    blocks, _, width = points.shape
    count = width // 9 * 8
    own_y = modes_y.shape[1]
    cols = 4 * own_y * KZ
    kept = 2 * (own_y + KZ)
    out_specs = [pl.BlockSpec((1, 3 * rows, cols), lambda i: (i, 0, 0))]
    out_shape = [jax.ShapeDtypeStruct((blocks, 3 * rows, cols), F32)]
    if keep:
        out_specs.append(pl.BlockSpec((1, kept, count), lambda i: (i, 0, 0)))
        out_shape.append(jax.ShapeDtypeStruct((blocks, kept, count), F32))
    in_specs = [
        pl.BlockSpec((1, 8, width), lambda i: (i, 0, 0)),
        pl.BlockSpec(modes_y.shape, lambda i: (0, 0, 0)),
        pl.BlockSpec(modes_z.shape, lambda i: (0, 0, 0)),
    ]
    operands = [points, modes_y, modes_z]
    tiles = 0
    if own is not None:
        tiles = max(1, count // LANES // blocks)
        last = count // LANES // tiles - 1
        in_specs.append(pl.BlockSpec((1, 8, width), lambda i: (0, 0, 0)))
        operands.append(own)
        out_specs.append(
            pl.BlockSpec((9, tiles * LANES, LANES), lambda i: (0, jnp.minimum(i, last), 0))
        )
        out_shape.append(jax.ShapeDtypeStruct((9, count, LANES), F32))
    return pl.pallas_call(
        functools.partial(spread_kernel, rows, tiles),
        grid=(blocks,),
        in_specs=in_specs,
        out_specs=out_specs,
        out_shape=out_shape,
        compiler_params=pltpu.CompilerParams(vmem_limit_bytes=SPREAD_LIMIT),
        cost_estimate=pl.CostEstimate(
            flops=blocks * count * cols * LANES * 14,
            bytes_accessed=blocks * (9 * count + 3 * rows * cols) * 4,
            transcendentals=0,
        ),
        name="spread",
    )(*operands)


def solve_kernel(planes, rows, parts, ids_ref, *refs):
    piece_refs = refs[:parts]
    forward_half_ref, forward_ref, back_half_ref, back_ref = refs[parts : parts + 4]
    waves_ref, out_ref, stacked = refs[parts + 4 :]
    extra = 8
    out_ref[...] = jnp.zeros_like(out_ref)
    before = 0
    for piece_ref in piece_refs:

        @pl.loop(0, piece_ref.shape[0])
        def _(index):
            first = pl.multiple_of(first_plane(ids_ref[before + index], planes), 8)
            for c in range(3):
                out_ref[c, pl.ds(first, rows)] += piece_ref[index, c * rows : (c + 1) * rows]

        before += piece_ref.shape[0]
    for c in range(3):
        out_ref[c, 0:extra] += out_ref[c, NX : NX + extra]
    quarter = NX // 4
    lanes = waves_ref.shape[1]
    families = ((0, quarter // 2, 4, 0), (quarter, quarter // 2, 4, 2), (2 * quarter, quarter, 2, 1))

    def transform(table, value):
        high, low = split(value)
        size = value.shape[0]
        stacked[0:size] = high
        stacked[size : 2 * size] = high
        stacked[2 * size : 3 * size] = low
        return jnp.dot(table, stacked[0 : 3 * size], preferred_element_type=F32)

    @pl.loop(0, 3)
    def _(c):
        cuts = [out_ref[c, i * quarter : (i + 1) * quarter] for i in range(4)]
        first, second = cuts[0] + cuts[2], cuts[1] + cuts[3]
        odd = jnp.concatenate([cuts[0] - cuts[2], cuts[1] - cuts[3]], axis=0)
        odd = transform(forward_ref[...], odd)
        results = [
            transform(forward_half_ref[0], first + second),
            transform(forward_half_ref[1], first - second),
        ]
        out_ref[c, 0:quarter] = results[0]
        out_ref[c, quarter : 2 * quarter] = results[1]
        out_ref[c, 2 * quarter : NX] = odd

    wave_y = waves_ref[0:1]
    wave_z = waves_ref[1:2]
    mult = waves_ref[2:3]
    flat = wave_y * wave_y + wave_z * wave_z
    group = 8

    for base, count, stride, offset in families:

        @pl.loop(0, count // group)
        def _(index):
            row = pl.multiple_of(index * group, group)
            number = lax.broadcasted_iota(jnp.int32, (group, lanes), 0) + row
            number = (stride * number + offset).astype(F32)
            wave_x = number * (TWO_PI / NX)
            squared = wave_x * wave_x + flat
            anchor = squared == 0.0
            inverse = jnp.where(anchor, 0.0, 1.0 / jnp.where(anchor, 1.0, squared))
            factor = inverse * mult * jnp.where(number == 0.0, 1.0, 2.0)
            waves = (wave_x, wave_y, wave_z)

            def place(axis, state):
                first = pl.multiple_of(base + state[0] * count + row, group)
                tyz = 2 * state[1] + state[2]
                return axis, pl.ds(first, group), slice(tyz * lanes, (tyz + 1) * lanes)

            def flip(state, axis):
                return tuple(1 - t if i == axis else t for i, t in enumerate(state))

            states = [(a, b, d) for a in range(2) for b in range(2) for d in range(2)]
            values = {(c,) + state: out_ref[place(c, state)] for c in range(3) for state in states}
            divergence = {}
            for state in states:
                total = None
                for axis in range(3):
                    term = waves[axis] * values[(axis,) + flip(state, axis)]
                    if state[axis]:
                        term = -term
                    total = term if total is None else total + term
                divergence[state] = total * inverse
            for state in states:
                for axis in range(3):
                    term = waves[axis] * divergence[flip(state, axis)]
                    value = values[(axis,) + state]
                    value = value - term if state[axis] else value + term
                    out_ref[place(axis, state)] = value * factor

    @pl.loop(0, 3)
    def _(c):
        first = transform(back_half_ref[0], out_ref[c, 0:quarter])
        second = transform(back_half_ref[1], out_ref[c, quarter : 2 * quarter])
        odd = transform(back_ref[...], out_ref[c, 2 * quarter : NX])
        even = jnp.concatenate([first + second, first - second], axis=0)
        out_ref[c, 0 : 2 * quarter] = even + odd
        out_ref[c, 2 * quarter : NX] = even - odd
        out_ref[c, NX : NX + extra] = out_ref[c, 0:extra]


def solve(pieces, ids, waves, tables, planes, rows):
    full = pl.BlockSpec(memory_space=pltpu.VMEM)
    cols = pieces[0].shape[2]
    return pl.pallas_call(
        functools.partial(solve_kernel, planes, rows, len(pieces)),
        in_specs=[pl.BlockSpec(memory_space=pltpu.SMEM)] + [full] * (len(pieces) + 5),
        out_specs=full,
        out_shape=jax.ShapeDtypeStruct((3, NX + 8, cols), F32),
        scratch_shapes=[
            pltpu.VMEM((3 * NX // 2, cols), BF16),
        ],
        compiler_params=pltpu.CompilerParams(vmem_limit_bytes=SOLVE_LIMIT),
        cost_estimate=pl.CostEstimate(
            flops=27 * NX // 2 * NX // 2 * cols,
            bytes_accessed=6 * NX * cols * 4,
            transcendentals=0,
        ),
        name="solve",
    )(ids, *pieces, *tables, waves)


def gather_kernel(planes, rows, before, kept, ids_ref, points_ref, *refs):
    basis_refs, (lines_ref, out_ref, plane) = refs[:-3], refs[-3:]
    step = pl.program_id(0)
    first = pl.multiple_of(first_plane(ids_ref[before + step], planes), 8)
    stack = jnp.concatenate([lines_ref[c, pl.ds(first, rows)] for c in range(3)], axis=0)
    if 3 * rows < LANES:
        stack = jnp.concatenate([stack, jnp.zeros((LANES - 3 * rows, lines_ref.shape[2]), F32)], axis=0)
    high, low = split(stack)
    plane[0:LANES] = high
    plane[LANES:] = low
    main, last = unpack(points_ref[0])
    count = main.shape[1]
    chunk = count // 2
    if kept:
        own_y = basis_refs[0].shape[1] // 2 - KZ
    else:
        modes_y, modes_z = [[ref[i] for i in range(7)] for ref in basis_refs]
    for index in range(2):
        at = slice(index * chunk, (index + 1) * chunk)
        if kept:
            rows_y = [basis_refs[0][0, i * own_y : (i + 1) * own_y, at] for i in range(2)]
            rows_z = [
                basis_refs[0][0, 2 * own_y + i * KZ : 2 * own_y + (i + 1) * KZ, at] for i in range(2)
            ]
        else:
            rows_y, rows_z = basis_rows(main[:, at], last[:, at], modes_y, modes_z)
        pairs = [split(value) for value in column_values(rows_y, rows_z)]
        highs = jnp.concatenate([p[0] for p in pairs], axis=0)
        lows = jnp.concatenate([p[1] for p in pairs], axis=0)
        result = jnp.dot(plane[...], highs, preferred_element_type=F32)
        small = jnp.dot(plane[0:LANES], lows, preferred_element_type=F32)
        result = result[:LANES] + result[LANES:] + small
        weight = plane_rows(main[3:4, at], spline_weights(main[6:7, at]), rows)
        out_ref[0, :, at] = jnp.concatenate(
            [
                jnp.sum(weight * result[c * rows : (c + 1) * rows], axis=0, keepdims=True)
                for c in range(3)
            ],
            axis=0,
        )


def gather(points, skip, blocks, before, ids, basis, lines, planes, rows):
    width = points.shape[2]
    count = width // 9 * 8
    cols = lines.shape[2]
    kept = len(basis) == 1
    if kept:
        basis_specs = [pl.BlockSpec((1,) + basis[0].shape[1:], lambda i: (i + skip, 0, 0))]
    else:
        basis_specs = [pl.BlockSpec(table.shape, lambda i: (0, 0, 0)) for table in basis]
    return pl.pallas_call(
        functools.partial(gather_kernel, planes, rows, before, kept),
        grid=(blocks,),
        in_specs=[
            pl.BlockSpec(memory_space=pltpu.SMEM),
            pl.BlockSpec((1, 8, width), lambda i: (i + skip, 0, 0)),
            *basis_specs,
            pl.BlockSpec(memory_space=pltpu.VMEM),
        ],
        out_specs=pl.BlockSpec((1, 3, count), lambda i: (i, 0, 0)),
        out_shape=jax.ShapeDtypeStruct((blocks, 3, count), F32),
        scratch_shapes=[pltpu.VMEM((2 * LANES, cols), BF16)],
        compiler_params=pltpu.CompilerParams(vmem_limit_bytes=GATHER_LIMIT),
        cost_estimate=pl.CostEstimate(
            flops=blocks * count * cols * LANES * 5,
            bytes_accessed=blocks * 12 * count * 4,
            transcendentals=0,
        ),
        name="interpolate",
    )(ids, points, *basis, lines)


def line_tables():
    def table(numbers, length):
        angle = (numbers[:, None] * np.arange(length)[None, :] % NX) * (2.0 * np.pi / NX)
        return np.concatenate([np.cos(angle), np.sin(angle)], axis=0)

    def stacked(value):
        high = value.astype(ml_dtypes.bfloat16)
        low = (value - high.astype(np.float64)).astype(ml_dtypes.bfloat16)
        return np.concatenate([high, low, high], axis=1)

    quarter = NX // 4
    even = [table(4 * np.arange(quarter // 2) + first, quarter) for first in (0, 2)]
    odd = table(2 * np.arange(quarter) + 1, 2 * quarter)
    return (
        np.stack([stacked(value) for value in even]),
        stacked(odd),
        np.stack([stacked(value.T) for value in even]),
        stacked(odd.T),
    )


def mode_table(numbers, length):
    angle = numbers * (2.0 * np.pi / length)
    rows = [numbers]
    for stencil in range(1, 4):
        rows += [np.cos(stencil * angle), np.sin(stencil * angle)]
    table = np.stack(rows, axis=1)[..., None].astype(np.float32)
    return np.broadcast_to(table, table.shape[:3] + (LANES,))


def far_tables(device, devices):
    own_y = (NY // 2) * (NZ // 2) // devices // KZ
    parts_z = NZ // 2 // KZ
    number_y = np.arange(NY // 2).reshape(-1, own_y).astype(np.float64)
    number_z = np.arange(NZ // 2).reshape(-1, KZ).astype(np.float64)
    mult_y = np.where(number_y == 0, 1.0, 2.0)
    mult_z = np.where(number_z == 0, 1.0, 2.0) / float(NX * NY * NZ)
    shape = (number_y.shape[0], parts_z, own_y, KZ)
    waves = [
        np.broadcast_to(number_y[:, None, :, None] * (TWO_PI / NY), shape),
        np.broadcast_to(number_z[None, :, None, :] * (TWO_PI / NZ), shape),
        mult_y[:, None, :, None] * mult_z[None, :, None, :],
    ]
    waves = np.stack([w.reshape(devices, own_y * KZ) for w in waves], axis=1)
    waves = np.concatenate([waves, np.zeros((devices, 5, own_y * KZ))], axis=1)

    def own(table, index):
        return lax.dynamic_index_in_dim(jnp.asarray(table, F32), index, 0, keepdims=False)

    return (
        own(mode_table(number_y, NY), device // parts_z),
        own(mode_table(number_z, NZ), device % parts_z),
        own(waves, device),
    )


def per_device(forces, stencil_start, fraction, tile_pairs, pair_count):
    groups = lax.axis_size("group")
    members = lax.axis_size("dev")
    devices = groups * members
    planes = NX // devices
    device = lax.axis_index("group") * members + lax.axis_index("dev")
    rows = max(8, planes) + 8
    first = first_plane(device, planes).reshape(1)
    own = pack(first, forces, stencil_start, fraction)

    def from_flipped(values, mask):
        pairs = [(i, i ^ mask) for i in range(devices)]
        return lax.ppermute(values, ("group", "dev"), pairs)

    near_masks = (4, 8, 12)
    parts = [own, jnp.concatenate([from_flipped(own, mask) for mask in near_masks], axis=0)]
    masks = [0, *near_masks]
    own_half = jnp.concatenate(parts, axis=0)
    last_bit = devices.bit_length() - 2
    bits = [1] + list(range(4, last_bit))
    for bit in bits:
        parts.append(from_flipped(own_half, 1 << bit))
        own_half = jnp.concatenate([own_half, parts[-1]], axis=0)
        masks = masks + [m ^ 1 << bit for m in masks]
    top = 1 << last_bit
    parts.append(from_flipped(own_half, 1))
    other = from_flipped(own_half, top)
    parts += [other, from_flipped(other, 1)]
    masks = np.array([m ^ flip for flip in (0, 1, top, top ^ 1) for m in masks], np.int32)
    ids = device ^ jnp.asarray(masks)
    modes_y, modes_z, waves = far_tables(device, devices)
    tables = [jnp.asarray(table) for table in line_tables()]
    keep = keeps(own, modes_y)
    spreads = []
    modes = modes_y
    for part, points in enumerate(parts):
        wide_own = own if part == len(parts) - WIDE_PART else None
        result = spread(points, modes, modes_z, rows, keep, wide_own)
        if wide_own is not None:
            *result, wide = result
        piece, modes = lax.optimization_barrier((result[0], modes_y))
        spreads.append([piece, *result[1:]])
    pieces = [result[0] for result in spreads]
    lines = solve(pieces, ids, waves, tables, planes, rows)
    firsts = np.cumsum([0] + [points.shape[0] for points in parts])

    def sums(part, after, skip=0, blocks=None):
        basis = spreads[part][1:] if keep else [modes_y, modes_z]
        blocks = blocks or parts[part].shape[0]
        return gather(
            parts[part], skip, blocks, int(firsts[part]) + skip, after, basis, lines, planes, rows
        )

    def then(value):
        return lax.optimization_barrier((value, ids))

    count = len(parts)
    across, after = then(sums(count - 1, ids))
    across = sums(count - 2, after) + from_flipped(across, 1)
    across, after = then(across)
    across, beside = from_flipped(across, top), sums(count - 3, after)
    (across, beside), after = then((across, beside))
    beside = from_flipped(beside, 1)
    total = None
    for part in range(count - 4, 1, -1):
        given = sums(part, after)
        if total is None:
            (beside, given), after = then((beside, given))
            total = across + beside
        half = total.shape[0] // 2
        given = given + total[half:]
        if part == 2:
            given, after = then(given)
            far_pair = sums(1, after, 1, 2)
        given = from_flipped(given, 1 << bits[part - 2])
        if part == 2:
            (given, far_pair), after = then((given, far_pair))
        total = total[:half] + given
    far_pair, after = then(far_pair + total[2:])
    far_pair = from_flipped(far_pair, 8)
    last, far = sums(1, after, 0, 1), sums(0, after)
    (far_pair, last, far), after = then((far_pair, last, far))
    last = last + total[1:2] + far_pair[1:]
    far = far + total[:1] + far_pair[:1]
    count_late, last = lax.optimization_barrier((pair_count, last))
    near = near_field(own, wide, tile_pairs, count_late)
    return far[0] + from_flipped(last, 4)[0] + near


def solution(mesh):
    in_specs = (
        P(None, ("group", "dev")),
        P(None, ("group", "dev")),
        P(None, ("group", "dev")),
        P(("group", "dev"), None),
        P(("group", "dev")),
    )
    out_specs = P(None, ("group", "dev"))
    return jax.shard_map(
        per_device, mesh=mesh, in_specs=in_specs, out_specs=out_specs, check_vma=False
    )
```

```python
import functools

import jax
import jax.numpy as jnp
import ml_dtypes
import numpy as np
from jax import lax
from jax.experimental import pallas as pl
from jax.experimental.pallas import tpu as pltpu
from jax.sharding import PartitionSpec as P

NX = 1024
NY = 128
NZ = 128

TWO_PI = 6.283185307179586
EPS_SQ = 1.0
RANGE_SQ = 16.0
NEAR_SCALE = 0.25

LANES = 128
SPREAD_LIMIT = 16 * 2**20
SOLVE_LIMIT = 8 * 2**20
GATHER_LIMIT = 12 * 2**20
WIDE_PART = 3
KEEP_BYTES = 32 * 2**20
KZ = 16
BF16 = jnp.bfloat16
F32 = jnp.float32


def wrapped(gap, length):
    gap = jnp.where(gap > length / 2, gap - length, gap)
    return jnp.where(gap < -length / 2, gap + length, gap)


def tile_rows(own_ref, tile, points):
    per = points // 8 // LANES
    at = pl.ds(pl.multiple_of(tile * LANES, LANES), LANES)
    last_at = pl.ds(pl.multiple_of(points + lax.rem(tile, per) * LANES, LANES), LANES)
    pieces = own_ref[0, :, last_at]
    here = lax.broadcasted_iota(jnp.int32, pieces.shape, 0) == lax.div(tile, per)
    return own_ref[0, :, at], jnp.sum(jnp.where(here, pieces, 0.0), axis=0, keepdims=True)


def near_kernel(pairs_ref, count_ref, own_ref, wide_ref, out_ref):
    points = out_ref.shape[1]
    out_ref[...] = jnp.zeros_like(out_ref)

    @pl.loop(0, count_ref[0])
    def _(slot):
        tile = pairs_ref[2 * slot]
        target = pl.ds(pl.multiple_of(tile * LANES, LANES), LANES)
        base = pl.multiple_of(pairs_ref[2 * slot + 1] * LANES, LANES)
        main, last = tile_rows(own_ref, tile, points)
        start = [main[3 + axis : 4 + axis] for axis in range(3)]
        fraction = [main[6:7], main[7:8], last]
        sums = [jnp.zeros((8, LANES), F32) for _ in range(3)]
        for row in range(0, LANES, 8):
            source = [wide_ref[value, pl.ds(base + row, 8)] for value in range(9)]
            gaps = []
            for axis, length in enumerate((None, NY, NZ)):
                gap = start[axis] - source[3 + axis]
                if length is not None:
                    gap = wrapped(gap, float(length))
                gaps.append(gap + (fraction[axis] - source[6 + axis]))
            pulled = source[0:3]
            distance = gaps[0] * gaps[0] + gaps[1] * gaps[1] + gaps[2] * gaps[2]
            inverse = lax.rsqrt(distance + EPS_SQ)
            fall = NEAR_SCALE * jnp.exp(distance * (-1.0 / RANGE_SQ)) * (inverse * inverse * inverse)
            diagonal = (distance + 2.0 * EPS_SQ) * fall
            along = fall * (gaps[0] * pulled[0] + gaps[1] * pulled[1] + gaps[2] * pulled[2])
            sums = [sums[i] + (diagonal * pulled[i] + gaps[i] * along) for i in range(3)]
        out_ref[:, target] += jnp.concatenate(
            [jnp.sum(value, axis=0, keepdims=True) for value in sums], axis=0
        )


def near_field(own, wide, tile_pairs, pair_count):
    smem = pl.BlockSpec(memory_space=pltpu.SMEM)
    vmem = pl.BlockSpec(memory_space=pltpu.VMEM)
    points = wide.shape[1]
    slots = tile_pairs.shape[0]
    return pl.pallas_call(
        near_kernel,
        in_specs=[smem, smem, vmem, vmem],
        out_specs=vmem,
        out_shape=jax.ShapeDtypeStruct((3, points), F32),
        compiler_params=pltpu.CompilerParams(vmem_limit_bytes=16 * 2**20),
        cost_estimate=pl.CostEstimate(
            flops=slots * LANES * LANES * 6000, bytes_accessed=points * 48, transcendentals=0
        ),
        name="near",
    )(tile_pairs.reshape(-1), pair_count, own, wide)


def pack_kernel(first_ref, forces_ref, start_ref, fraction_ref, out_ref):
    points = forces_ref.shape[1]
    piece = points // 8
    start = start_ref[...]
    out_ref[0, 0:3, 0:points] = forces_ref[...]
    out_ref[0, 3:4, 0:points] = (start[0:1] - first_ref[0]).astype(F32)
    out_ref[0, 4:6, 0:points] = start[1:3].astype(F32)
    out_ref[0, 6:8, 0:points] = fraction_ref[0:2]
    for row in range(8):
        out_ref[0, row : row + 1, points:] = fraction_ref[2:3, row * piece : (row + 1) * piece]


def pack(first, forces, stencil_start, fraction):
    vmem = pl.BlockSpec(memory_space=pltpu.VMEM)
    points = forces.shape[1]
    return pl.pallas_call(
        pack_kernel,
        in_specs=[pl.BlockSpec(memory_space=pltpu.SMEM), vmem, vmem, vmem],
        out_specs=vmem,
        out_shape=jax.ShapeDtypeStruct((1, 8, points + points // 8), F32),
        name="pack",
    )(first, forces, stencil_start, fraction)


def unpacked(width):
    return width // 9 * 8


def unpack(values):
    points = unpacked(values.shape[1])
    pieces = [values[row : row + 1, points:] for row in range(8)]
    return values[:, :points], jnp.concatenate(pieces, axis=1)


def split(value):
    high = value.astype(BF16)
    low = (value - high.astype(F32)).astype(BF16)
    return high, low


def spline_weights(fraction):
    square = fraction * fraction
    cube = square * fraction
    rest = 1.0 - fraction
    return [
        rest * rest * rest * (1.0 / 6.0),
        (3.0 * cube - 6.0 * square + 4.0) * (1.0 / 6.0),
        (-3.0 * cube + 3.0 * square + 3.0 * fraction + 1.0) * (1.0 / 6.0),
        cube * (1.0 / 6.0),
    ]


def cos_sin_turns(turns):
    part = turns - jnp.floor(turns + 0.5)
    half = part * (0.5 * TWO_PI)
    square = half * half
    sine = half * (
        1.0
        + square
        * (
            -1.0 / 6.0
            + square
            * (1.0 / 120.0 + square * (-1.0 / 5040.0 + square * (1.0 / 362880.0 + square * (-1.0 / 39916800.0))))
        )
    )
    cosine = 1.0 + square * (
        -0.5
        + square
        * (
            1.0 / 24.0
            + square
            * (-1.0 / 720.0 + square * (1.0 / 40320.0 + square * (-1.0 / 3628800.0 + square * (1.0 / 479001600.0))))
        )
    )
    return 1.0 - 2.0 * sine * sine, 2.0 * sine * cosine


def widen(table, width):
    return jnp.concatenate([table] * (width // LANES), axis=1)


def mode_rows(start, weights, modes, length):
    width = start.shape[1]
    cosine, sine = cos_sin_turns(widen(modes[0], width) * start * (1.0 / length))
    sum_cos = weights[0] + weights[1] * widen(modes[1], width)
    sum_sin = weights[1] * widen(modes[2], width)
    sum_cos = sum_cos + weights[2] * widen(modes[3], width) + weights[3] * widen(modes[5], width)
    sum_sin = sum_sin + weights[2] * widen(modes[4], width) + weights[3] * widen(modes[6], width)
    return cosine * sum_cos - sine * sum_sin, sine * sum_cos + cosine * sum_sin


def basis_rows(main, last, modes_y, modes_z):
    weights_y = [w[1:2] for w in spline_weights(main[6:8])]
    rows_y = mode_rows(main[4:5], weights_y, modes_y, NY)
    rows_z = mode_rows(main[5:6], spline_weights(last), modes_z, NZ)
    return rows_y, rows_z


def column_values(rows_y, rows_z):
    values = []
    for ty in range(2):
        for tz in range(2):
            for iy in range(rows_y[0].shape[0]):
                values.append(rows_y[ty][iy : iy + 1] * rows_z[tz])
    return values


def plane_rows(start, weights, rows):
    iota = lax.broadcasted_iota(jnp.int32, (rows, start.shape[1]), 0).astype(F32)
    away = iota - start
    result = jnp.where(away == 0.0, weights[0], 0.0)
    for stencil in range(1, 4):
        result = jnp.where(away == float(stencil), weights[stencil], result)
    return result


def first_plane(block, planes):
    joined = max(1, 8 // planes)
    return lax.div(block, joined) * (joined * planes)


def spread_kernel(rows, tiles, points_ref, modes_y_ref, modes_z_ref, *refs):
    if tiles:
        own_ref, out_ref, *kept_refs, wide_ref = refs
        last_tile = unpacked(own_ref.shape[2]) // LANES - 1
        for index in range(tiles):
            tile = jnp.minimum(pl.program_id(0) * tiles + index, last_tile)
            eight, ninth = tile_rows(own_ref, tile, unpacked(own_ref.shape[2]))
            nine = jnp.concatenate([eight, ninth], axis=0)
            for value in range(9):
                wide = jnp.broadcast_to(nine[value : value + 1], (LANES, LANES))
                wide_ref[value, index * LANES : (index + 1) * LANES] = wide.T
    else:
        out_ref, *kept_refs = refs
    main, last = unpack(points_ref[0])
    count = main.shape[1]
    modes_y = [modes_y_ref[i] for i in range(7)]
    modes_z = [modes_z_ref[i] for i in range(7)]
    rows_y, rows_z = basis_rows(main, last, modes_y, modes_z)
    for kept_ref in kept_refs:
        kept_ref[0] = jnp.concatenate([*rows_y, *rows_z], axis=0)
    values = column_values(rows_y, rows_z)
    weights_x = spline_weights(main[6:7])
    weight = plane_rows(main[3:4], weights_x, rows)
    stack = jnp.concatenate([weight * main[c : c + 1] for c in range(3)], axis=0)
    if 3 * rows < LANES:
        stack = jnp.concatenate([stack, jnp.zeros((LANES - 3 * rows, count), F32)], axis=0)
    both = jnp.concatenate(split(stack), axis=0)
    parts = [split(value) for value in values]
    left = jnp.concatenate(
        [jnp.concatenate([p[i] for p in parts], axis=0) for i in range(2)], axis=1
    )
    right = jnp.concatenate([both, both], axis=1)
    acc = lax.dot_general(left, right, (((1,), (1,)), ((), ())), preferred_element_type=F32)
    total = (acc[:, :LANES] + acc[:, LANES:]).T
    out_ref[0] = total[: 3 * rows]


def keeps(points, modes_y):
    blocks_rows = 2 * (modes_y.shape[1] + KZ)
    return modes_y.shape[1] % 8 == 0 and lax.axis_size(("group", "dev")) * blocks_rows * (
        points.shape[2] // 9 * 8
    ) * 4 <= KEEP_BYTES


def spread(points, modes_y, modes_z, rows, keep, own=None):
    blocks, _, width = points.shape
    count = width // 9 * 8
    own_y = modes_y.shape[1]
    cols = 4 * own_y * KZ
    kept = 2 * (own_y + KZ)
    out_specs = [pl.BlockSpec((1, 3 * rows, cols), lambda i: (i, 0, 0))]
    out_shape = [jax.ShapeDtypeStruct((blocks, 3 * rows, cols), F32)]
    if keep:
        out_specs.append(pl.BlockSpec((1, kept, count), lambda i: (i, 0, 0)))
        out_shape.append(jax.ShapeDtypeStruct((blocks, kept, count), F32))
    in_specs = [
        pl.BlockSpec((1, 8, width), lambda i: (i, 0, 0)),
        pl.BlockSpec(modes_y.shape, lambda i: (0, 0, 0)),
        pl.BlockSpec(modes_z.shape, lambda i: (0, 0, 0)),
    ]
    operands = [points, modes_y, modes_z]
    tiles = 0
    if own is not None:
        tiles = max(1, count // LANES // blocks)
        last = count // LANES // tiles - 1
        in_specs.append(pl.BlockSpec((1, 8, width), lambda i: (0, 0, 0)))
        operands.append(own)
        out_specs.append(
            pl.BlockSpec((9, tiles * LANES, LANES), lambda i: (0, jnp.minimum(i, last), 0))
        )
        out_shape.append(jax.ShapeDtypeStruct((9, count, LANES), F32))
    return pl.pallas_call(
        functools.partial(spread_kernel, rows, tiles),
        grid=(blocks,),
        in_specs=in_specs,
        out_specs=out_specs,
        out_shape=out_shape,
        compiler_params=pltpu.CompilerParams(vmem_limit_bytes=SPREAD_LIMIT),
        cost_estimate=pl.CostEstimate(
            flops=blocks * count * cols * LANES * 14,
            bytes_accessed=blocks * (9 * count + 3 * rows * cols) * 4,
            transcendentals=0,
        ),
        name="spread",
    )(*operands)


def solve_kernel(planes, rows, parts, ids_ref, *refs):
    piece_refs = refs[:parts]
    forward_half_ref, forward_ref, back_half_ref, back_ref = refs[parts : parts + 4]
    waves_ref, out_ref, stacked = refs[parts + 4 :]
    extra = 8
    out_ref[...] = jnp.zeros_like(out_ref)
    before = 0
    for piece_ref in piece_refs:

        @pl.loop(0, piece_ref.shape[0])
        def _(index):
            first = pl.multiple_of(first_plane(ids_ref[before + index], planes), 8)
            for c in range(3):
                out_ref[c, pl.ds(first, rows)] += piece_ref[index, c * rows : (c + 1) * rows]

        before += piece_ref.shape[0]
    for c in range(3):
        out_ref[c, 0:extra] += out_ref[c, NX : NX + extra]
    quarter = NX // 4
    lanes = waves_ref.shape[1]
    families = ((0, quarter // 2, 4, 0), (quarter, quarter // 2, 4, 2), (2 * quarter, quarter, 2, 1))

    def transform(table, value):
        high, low = split(value)
        size = value.shape[0]
        stacked[0:size] = high
        stacked[size : 2 * size] = high
        stacked[2 * size : 3 * size] = low
        return jnp.dot(table, stacked[0 : 3 * size], preferred_element_type=F32)

    @pl.loop(0, 3)
    def _(c):
        cuts = [out_ref[c, i * quarter : (i + 1) * quarter] for i in range(4)]
        first, second = cuts[0] + cuts[2], cuts[1] + cuts[3]
        odd = jnp.concatenate([cuts[0] - cuts[2], cuts[1] - cuts[3]], axis=0)
        odd = transform(forward_ref[...], odd)
        results = [
            transform(forward_half_ref[0], first + second),
            transform(forward_half_ref[1], first - second),
        ]
        out_ref[c, 0:quarter] = results[0]
        out_ref[c, quarter : 2 * quarter] = results[1]
        out_ref[c, 2 * quarter : NX] = odd

    wave_y = waves_ref[0:1]
    wave_z = waves_ref[1:2]
    mult = waves_ref[2:3]
    flat = wave_y * wave_y + wave_z * wave_z
    group = 8

    for base, count, stride, offset in families:

        @pl.loop(0, count // group)
        def _(index):
            row = pl.multiple_of(index * group, group)
            number = lax.broadcasted_iota(jnp.int32, (group, lanes), 0) + row
            number = (stride * number + offset).astype(F32)
            wave_x = number * (TWO_PI / NX)
            squared = wave_x * wave_x + flat
            anchor = squared == 0.0
            inverse = jnp.where(anchor, 0.0, 1.0 / jnp.where(anchor, 1.0, squared))
            factor = inverse * mult * jnp.where(number == 0.0, 1.0, 2.0)
            waves = (wave_x, wave_y, wave_z)

            def place(axis, state):
                first = pl.multiple_of(base + state[0] * count + row, group)
                tyz = 2 * state[1] + state[2]
                return axis, pl.ds(first, group), slice(tyz * lanes, (tyz + 1) * lanes)

            def flip(state, axis):
                return tuple(1 - t if i == axis else t for i, t in enumerate(state))

            states = [(a, b, d) for a in range(2) for b in range(2) for d in range(2)]
            values = {(c,) + state: out_ref[place(c, state)] for c in range(3) for state in states}
            divergence = {}
            for state in states:
                total = None
                for axis in range(3):
                    term = waves[axis] * values[(axis,) + flip(state, axis)]
                    if state[axis]:
                        term = -term
                    total = term if total is None else total + term
                divergence[state] = total * inverse
            for state in states:
                for axis in range(3):
                    term = waves[axis] * divergence[flip(state, axis)]
                    value = values[(axis,) + state]
                    value = value - term if state[axis] else value + term
                    out_ref[place(axis, state)] = value * factor

    @pl.loop(0, 3)
    def _(c):
        first = transform(back_half_ref[0], out_ref[c, 0:quarter])
        second = transform(back_half_ref[1], out_ref[c, quarter : 2 * quarter])
        odd = transform(back_ref[...], out_ref[c, 2 * quarter : NX])
        even = jnp.concatenate([first + second, first - second], axis=0)
        out_ref[c, 0 : 2 * quarter] = even + odd
        out_ref[c, 2 * quarter : NX] = even - odd
        out_ref[c, NX : NX + extra] = out_ref[c, 0:extra]


def solve(pieces, ids, waves, tables, planes, rows):
    full = pl.BlockSpec(memory_space=pltpu.VMEM)
    cols = pieces[0].shape[2]
    return pl.pallas_call(
        functools.partial(solve_kernel, planes, rows, len(pieces)),
        in_specs=[pl.BlockSpec(memory_space=pltpu.SMEM)] + [full] * (len(pieces) + 5),
        out_specs=full,
        out_shape=jax.ShapeDtypeStruct((3, NX + 8, cols), F32),
        scratch_shapes=[
            pltpu.VMEM((3 * NX // 2, cols), BF16),
        ],
        compiler_params=pltpu.CompilerParams(vmem_limit_bytes=SOLVE_LIMIT),
        cost_estimate=pl.CostEstimate(
            flops=27 * NX // 2 * NX // 2 * cols,
            bytes_accessed=6 * NX * cols * 4,
            transcendentals=0,
        ),
        name="solve",
    )(ids, *pieces, *tables, waves)


def gather_kernel(planes, rows, before, kept, ids_ref, points_ref, *refs):
    basis_refs, (lines_ref, out_ref, plane) = refs[:-3], refs[-3:]
    step = pl.program_id(0)
    first = pl.multiple_of(first_plane(ids_ref[before + step], planes), 8)
    stack = jnp.concatenate([lines_ref[c, pl.ds(first, rows)] for c in range(3)], axis=0)
    if 3 * rows < LANES:
        stack = jnp.concatenate([stack, jnp.zeros((LANES - 3 * rows, lines_ref.shape[2]), F32)], axis=0)
    high, low = split(stack)
    plane[0:LANES] = high
    plane[LANES:] = low
    main, last = unpack(points_ref[0])
    count = main.shape[1]
    chunk = count // 2
    if kept:
        own_y = basis_refs[0].shape[1] // 2 - KZ
    else:
        modes_y, modes_z = [[ref[i] for i in range(7)] for ref in basis_refs]
    for index in range(2):
        at = slice(index * chunk, (index + 1) * chunk)
        if kept:
            rows_y = [basis_refs[0][0, i * own_y : (i + 1) * own_y, at] for i in range(2)]
            rows_z = [
                basis_refs[0][0, 2 * own_y + i * KZ : 2 * own_y + (i + 1) * KZ, at] for i in range(2)
            ]
        else:
            rows_y, rows_z = basis_rows(main[:, at], last[:, at], modes_y, modes_z)
        pairs = [split(value) for value in column_values(rows_y, rows_z)]
        highs = jnp.concatenate([p[0] for p in pairs], axis=0)
        lows = jnp.concatenate([p[1] for p in pairs], axis=0)
        result = jnp.dot(plane[...], highs, preferred_element_type=F32)
        small = jnp.dot(plane[0:LANES], lows, preferred_element_type=F32)
        result = result[:LANES] + result[LANES:] + small
        weight = plane_rows(main[3:4, at], spline_weights(main[6:7, at]), rows)
        out_ref[0, :, at] = jnp.concatenate(
            [
                jnp.sum(weight * result[c * rows : (c + 1) * rows], axis=0, keepdims=True)
                for c in range(3)
            ],
            axis=0,
        )


def gather(points, skip, blocks, before, ids, basis, lines, planes, rows):
    width = points.shape[2]
    count = width // 9 * 8
    cols = lines.shape[2]
    kept = len(basis) == 1
    if kept:
        basis_specs = [pl.BlockSpec((1,) + basis[0].shape[1:], lambda i: (i + skip, 0, 0))]
    else:
        basis_specs = [pl.BlockSpec(table.shape, lambda i: (0, 0, 0)) for table in basis]
    return pl.pallas_call(
        functools.partial(gather_kernel, planes, rows, before, kept),
        grid=(blocks,),
        in_specs=[
            pl.BlockSpec(memory_space=pltpu.SMEM),
            pl.BlockSpec((1, 8, width), lambda i: (i + skip, 0, 0)),
            *basis_specs,
            pl.BlockSpec(memory_space=pltpu.VMEM),
        ],
        out_specs=pl.BlockSpec((1, 3, count), lambda i: (i, 0, 0)),
        out_shape=jax.ShapeDtypeStruct((blocks, 3, count), F32),
        scratch_shapes=[pltpu.VMEM((2 * LANES, cols), BF16)],
        compiler_params=pltpu.CompilerParams(vmem_limit_bytes=GATHER_LIMIT),
        cost_estimate=pl.CostEstimate(
            flops=blocks * count * cols * LANES * (14 if blocks > 1 else 2),
            bytes_accessed=blocks * 12 * count * 4,
            transcendentals=0,
        ),
        name="interpolate",
    )(ids, points, *basis, lines)


def line_tables():
    def table(numbers, length):
        angle = (numbers[:, None] * np.arange(length)[None, :] % NX) * (2.0 * np.pi / NX)
        return np.concatenate([np.cos(angle), np.sin(angle)], axis=0)

    def stacked(value):
        high = value.astype(ml_dtypes.bfloat16)
        low = (value - high.astype(np.float64)).astype(ml_dtypes.bfloat16)
        return np.concatenate([high, low, high], axis=1)

    quarter = NX // 4
    even = [table(4 * np.arange(quarter // 2) + first, quarter) for first in (0, 2)]
    odd = table(2 * np.arange(quarter) + 1, 2 * quarter)
    return (
        np.stack([stacked(value) for value in even]),
        stacked(odd),
        np.stack([stacked(value.T) for value in even]),
        stacked(odd.T),
    )


def mode_table(numbers, length):
    angle = numbers * (2.0 * np.pi / length)
    rows = [numbers]
    for stencil in range(1, 4):
        rows += [np.cos(stencil * angle), np.sin(stencil * angle)]
    table = np.stack(rows, axis=1)[..., None].astype(np.float32)
    return np.broadcast_to(table, table.shape[:3] + (LANES,))


def far_tables(device, devices):
    own_y = (NY // 2) * (NZ // 2) // devices // KZ
    parts_z = NZ // 2 // KZ
    number_y = np.arange(NY // 2).reshape(-1, own_y).astype(np.float64)
    number_z = np.arange(NZ // 2).reshape(-1, KZ).astype(np.float64)
    mult_y = np.where(number_y == 0, 1.0, 2.0)
    mult_z = np.where(number_z == 0, 1.0, 2.0) / float(NX * NY * NZ)
    shape = (number_y.shape[0], parts_z, own_y, KZ)
    waves = [
        np.broadcast_to(number_y[:, None, :, None] * (TWO_PI / NY), shape),
        np.broadcast_to(number_z[None, :, None, :] * (TWO_PI / NZ), shape),
        mult_y[:, None, :, None] * mult_z[None, :, None, :],
    ]
    waves = np.stack([w.reshape(devices, own_y * KZ) for w in waves], axis=1)
    waves = np.concatenate([waves, np.zeros((devices, 5, own_y * KZ))], axis=1)

    def own(table, index):
        return lax.dynamic_index_in_dim(jnp.asarray(table, F32), index, 0, keepdims=False)

    return (
        own(mode_table(number_y, NY), device // parts_z),
        own(mode_table(number_z, NZ), device % parts_z),
        own(waves, device),
    )


def per_device(forces, stencil_start, fraction, tile_pairs, pair_count):
    groups = lax.axis_size("group")
    members = lax.axis_size("dev")
    devices = groups * members
    planes = NX // devices
    device = lax.axis_index("group") * members + lax.axis_index("dev")
    rows = max(8, planes) + 8
    first = first_plane(device, planes).reshape(1)
    own = pack(first, forces, stencil_start, fraction)

    def from_flipped(values, mask):
        pairs = [(i, i ^ mask) for i in range(devices)]
        return lax.ppermute(values, ("group", "dev"), pairs)

    near_masks = (4, 8, 12)
    parts = [own, jnp.concatenate([from_flipped(own, mask) for mask in near_masks], axis=0)]
    masks = [0, *near_masks]
    own_half = jnp.concatenate(parts, axis=0)
    last_bit = devices.bit_length() - 2
    bits = [1] + list(range(4, last_bit))
    for bit in bits:
        parts.append(from_flipped(own_half, 1 << bit))
        own_half = jnp.concatenate([own_half, parts[-1]], axis=0)
        masks = masks + [m ^ 1 << bit for m in masks]
    top = 1 << last_bit
    parts.append(from_flipped(own_half, 1))
    other = from_flipped(own_half, top)
    parts += [other, from_flipped(other, 1)]
    masks = np.array([m ^ flip for flip in (0, 1, top, top ^ 1) for m in masks], np.int32)
    ids = device ^ jnp.asarray(masks)
    modes_y, modes_z, waves = far_tables(device, devices)
    tables = [jnp.asarray(table) for table in line_tables()]
    keep = keeps(own, modes_y)
    spreads = []
    modes = modes_y
    for part, points in enumerate(parts):
        wide_own = own if part == len(parts) - WIDE_PART else None
        result = spread(points, modes, modes_z, rows, keep, wide_own)
        if wide_own is not None:
            *result, wide = result
        piece, modes = lax.optimization_barrier((result[0], modes_y))
        spreads.append([piece, *result[1:]])
    pieces = [result[0] for result in spreads]
    lines = solve(pieces, ids, waves, tables, planes, rows)
    firsts = np.cumsum([0] + [points.shape[0] for points in parts])

    def sums(part, after, skip=0, blocks=None):
        basis = spreads[part][1:] if keep else [modes_y, modes_z]
        blocks = blocks or parts[part].shape[0]
        return gather(
            parts[part], skip, blocks, int(firsts[part]) + skip, after, basis, lines, planes, rows
        )

    def then(value):
        return lax.optimization_barrier((value, ids))

    count = len(parts)
    across, after = then(sums(count - 1, ids))
    across = sums(count - 2, after) + from_flipped(across, 1)
    across, after = then(across)
    across, beside = from_flipped(across, top), sums(count - 3, after)
    (across, beside), after = then((across, beside))
    beside = from_flipped(beside, 1)
    total = None
    for part in range(count - 4, 1, -1):
        given = sums(part, after)
        if total is None:
            (beside, given), after = then((beside, given))
            total = across + beside
        half = total.shape[0] // 2
        given = given + total[half:]
        if part == 2:
            given, after = then(given)
            far_pair = sums(1, after, 1, 2)
        given = from_flipped(given, 1 << bits[part - 2])
        if part == 2:
            (given, far_pair), after = then((given, far_pair))
        total = total[:half] + given
    far_pair, after = then(far_pair + total[2:])
    far_pair = from_flipped(far_pair, 8)
    last, far = sums(1, after, 0, 1), sums(0, after)
    (far_pair, last, far), after = then((far_pair, last, far))
    last = last + total[1:2] + far_pair[1:]
    far = far + total[:1] + far_pair[:1]
    count_late, last = lax.optimization_barrier((pair_count, last))
    near = near_field(own, wide, tile_pairs, count_late)
    return far[0] + from_flipped(last, 4)[0] + near


def solution(mesh):
    in_specs = (
        P(None, ("group", "dev")),
        P(None, ("group", "dev")),
        P(None, ("group", "dev")),
        P(("group", "dev"), None),
        P(("group", "dev")),
    )
    out_specs = P(None, ("group", "dev"))
    return jax.shard_map(
        per_device, mesh=mesh, in_specs=in_specs, out_specs=out_specs, check_vma=False
    )
```
